32 devices in a mesh: dp: 2 (over core), context: 16 (over z, y, x).
Axes of the slice: x: 2, y: 2, z: 4, core: 2. Of those that a mesh axis runs over, the one named last changes fastest.
Arguments:
- query_input: float32 [2, 2048, 2048], P('dp', None, 'context'), may hold values from -6 to 6
- key_input: float32 [2, 2048, 2048], P('dp', None, 'context'), may hold values from -6 to 6
- value_input: float32 [2, 2048, 2048], P('dp', None, 'context'), may hold values from -6 to 6
- filters: float32 [2048, 2048], P('context'), may hold values from -2 to 2, as said below
- cotangent: float32 [2, 2048, 2048], P('dp', None, 'context'), may hold values from -6 to 6
Outputs:
- gated_output: float32 [2, 2048, 2048], P('dp', None, 'context')
- grad_query: float32 [2, 2048, 2048], P('dp', None, 'context')
- grad_key: float32 [2, 2048, 2048], P('dp', None, 'context')
- grad_value: float32 [2, 2048, 2048], P('dp', None, 'context')
- grad_filter: float32 [2048, 2048], P('context')
The draws below stay inside these ranges and needn't reach their ends.
Inputs may be any that keep to these rules, and one draw needn't show every extreme that they name: `filters`: real-valued filter taps, one for each channel and lag.
All inputs are finite; a program needn't handle non-finite values.
Results may differ from the reference program's by a relative error of at most 0.000098.
Values sent between devices are 32-bit elements; how exact they have to be, the bound alone decides.
No kernel may reach another device: no remote copies, remote signals or barrier semaphores. Data moves between devices by JAX's collectives and lax.ppermute only.
A program may use at most 128 MiB of HBM per device.

```python
import math
import jax
import jax.numpy as jnp
from jax import lax

C = 2048
SEQS = 2
LENGTH = 2048


def draw_filters(key, part):
    key = jax.random.fold_in(key, 7)
    key_fast, key_span, key_rate, key_noise = jax.random.split(key, 4)
    positions = jnp.arange(LENGTH, dtype=jnp.float32)[None, :]
    fast = jax.random.bernoulli(key_fast, 0.5, (C, 1))
    noise = jnp.clip(jax.random.normal(key_noise, (C, LENGTH)), -6.0, 6.0)
    span = jax.random.uniform(key_span, (C, 1), minval=30.0, maxval=50.0)
    rate = jax.random.uniform(key_rate, (C, 1), minval=0.2, maxval=2.0)
    fast_env = jnp.exp(-positions / span) * jnp.sqrt(2.0 / span)
    slow_env = jnp.exp(-rate * positions / LENGTH) * jnp.sqrt(2.0 * rate / LENGTH)
    envelope = jnp.where(fast, fast_env + 0.05 * slow_env, slow_env)
    return (noise * envelope).astype(jnp.float32)


def levels(rng, shape, pieces, low, largest):
    gain, own = 1.0, jax.random.fold_in(rng, 6)
    for position, shards_of in pieces:
        steps = jnp.exp(jax.random.uniform(jax.random.fold_in(own, position), (shards_of,), jnp.float32, low / len(pieces), largest / len(pieces)))
        gain = gain * jnp.repeat(steps, shape[position] // shards_of).reshape([-1 if axis == position else 1 for axis in range(len(shape))])
    return gain


def gaussian(own_key, extent, deviation, bound, pieces=(), kind=jnp.bfloat16):
    drawn = deviation * jax.random.normal(own_key, extent, jnp.float32)
    if pieces:
        drawn = drawn * levels(own_key, extent, pieces, -0.22, 0.18)
    return jnp.clip(drawn, -bound, bound).astype(kind)


def setup_inputs(seed: int = 0) -> dict:
    key_of = jax.random.split(jax.random.key(seed), 6)
    query_input = gaussian(key_of[0], (SEQS, C, LENGTH), 1.0, 6.0, ((0, 2), (2, 16)), jnp.float32)
    key_input = gaussian(key_of[1], (SEQS, C, LENGTH), 1.0, 6.0, ((0, 2), (2, 16)), jnp.float32)
    value_input = gaussian(key_of[2], (SEQS, C, LENGTH), 1.0, 6.0, ((0, 2), (2, 16)), jnp.float32)
    filters = draw_filters(jax.random.fold_in(key_of[5], 71), 0)
    cotangent = gaussian(key_of[4], (SEQS, C, LENGTH), 1.0, 6.0, ((0, 2), (2, 16)), jnp.float32)
    return {"query_input": query_input, "key_input": key_input, "value_input": value_input, "filters": filters, "cotangent": cotangent}


def block_pass(operands):
    query_block, key_block, value_block, filter_block, grad_block = operands
    total_size = 2 * LENGTH
    product = key_block * value_block
    conv_grad = grad_block * query_block
    spec_product = jnp.fft.rfft(product, n=total_size, axis=-1)
    spec_filter = jnp.fft.rfft(filter_block, n=total_size, axis=-1)[None]
    spec_grad = jnp.fft.rfft(conv_grad, n=total_size, axis=-1)
    conv = jnp.fft.irfft(spec_filter * spec_product, n=total_size, axis=-1)[..., :LENGTH]
    product_grad = jnp.fft.irfft(jnp.conj(spec_filter) * spec_grad, n=total_size, axis=-1)[..., :LENGTH]
    filter_grad = jnp.fft.irfft(jnp.conj(spec_product) * spec_grad, n=total_size, axis=-1)[..., :LENGTH]
    filter_grad = lax.optimization_barrier(jnp.sum(filter_grad, axis=0)) * (1.0 / math.sqrt(SEQS * LENGTH))
    return (query_block * conv, grad_block * conv, product_grad * value_block, product_grad * key_block, filter_grad)

def reference(query_input, key_input, value_input, filters, cotangent):
    block = min(C, 128)
    blocks = C // block

    def split(array):
        return array.reshape(SEQS, blocks, block, LENGTH).transpose(1, 0, 2, 3)

    def join(array):
        return array.transpose(1, 0, 2, 3).reshape(SEQS, C, LENGTH)
    results = lax.map(block_pass, (split(query_input), split(key_input), split(value_input), filters.reshape(blocks, block, LENGTH), split(cotangent)))
    gated, grad_q, grad_k, grad_v, grad_f = results
    return (join(gated), join(grad_q), join(grad_k), join(grad_v), grad_f.reshape(C, LENGTH))
```

```python
import math

import jax
import jax.numpy as jnp
import ml_dtypes
import numpy as np
from jax import lax
from jax.experimental import pallas as pl
from jax.experimental.pallas import tpu as pltpu
from jax.sharding import PartitionSpec as P

ROWS = 8
VMEM_BYTES = 48 * 1024 * 1024


def twist(value, turn):
    re, im = value
    turn = turn % 1.0
    if turn == 0.0:
        return re, im
    if turn == 0.25:
        return im, -re
    if turn == 0.5:
        return -re, -im
    if turn == 0.75:
        return -im, re
    if turn in (0.125, 0.375, 0.625, 0.875):
        half = math.sqrt(0.5)
        a, b = (re + im) * half, (im - re) * half
        return twist((a, b), turn - 0.125)
    c, s = math.cos(2 * math.pi * turn), math.sin(2 * math.pi * turn)
    return re * c + im * s, im * c - re * s


def dft(values, sign):
    n = len(values)
    if n == 1:
        return values
    even, odd = dft(values[0::2], sign), dft(values[1::2], sign)
    out = [None] * n
    for k in range(n // 2):
        a, b = even[k], twist(odd[k], sign * k / n)
        out[k] = (a[0] + b[0], a[1] + b[1])
        out[k + n // 2] = (a[0] - b[0], a[1] - b[1])
    return out


def split(x):
    hi = x.astype(jnp.bfloat16)
    lo = (x - hi.astype(jnp.float32)).astype(jnp.bfloat16)
    return hi, lo


def times_table(x, table_ref):
    hi, lo = split(x)
    out = jnp.dot(hi, table_ref[0], preferred_element_type=jnp.float32)
    out += jnp.dot(lo, table_ref[0], preferred_element_type=jnp.float32)
    out += jnp.dot(hi, table_ref[1], preferred_element_type=jnp.float32)
    return out


def outer_forward(read, n, channels, tokens, tw_ref, y_ref):
    @pl.loop(0, channels // ROWS)
    def _(r):
        rows = pl.ds(pl.multiple_of(r * ROWS, ROWS), ROWS)
        values = []
        for n1 in range(n):
            x = read(n1, rows)
            turn = 2 * math.pi * n1 / (4 * n)
            if n1 == 0:
                values.append((x, jnp.zeros_like(x)))
            else:
                values.append((x * math.cos(turn), x * -math.sin(turn)))
        for m, (re, im) in enumerate(dft(values, 1)):
            c, s = tw_ref[0, m], tw_ref[1, m]
            y_ref[m, rows, :tokens] = re * c + im * s
            y_ref[m, rows, tokens:] = im * c - re * s


def outer_inverse(write, n, channels, tokens, tw_ref, y_ref):
    @pl.loop(0, channels // ROWS)
    def _(r):
        rows = pl.ds(pl.multiple_of(r * ROWS, ROWS), ROWS)
        values = []
        for m in range(n):
            re, im = y_ref[m, rows, :tokens], y_ref[m, rows, tokens:]
            c, s = tw_ref[0, m], tw_ref[1, m]
            values.append((re * c - im * s, im * c + re * s))
        for n1, (re, im) in enumerate(dft(values, -1)):
            turn = 2 * math.pi * n1 / (4 * n)
            if n1 == 0:
                write(n1, rows, re)
            else:
                write(n1, rows, re * math.cos(turn) - im * math.sin(turn))


def groups(n, channels, body):
    size = max(1, min(n, 512 // channels))

    @pl.loop(0, n // size)
    def _(i):
        body(pl.ds(i * size, size), size)


def flat(x):
    return x.reshape(x.shape[0] * x.shape[1], x.shape[2])


def filter_kernel(n, channels, tokens, f_ref, tw_ref, fwd_ref, out_ref, y_ref):
    outer_forward(
        lambda n1, rows: f_ref[rows, n1 * tokens : (n1 + 1) * tokens],
        n, channels, tokens, tw_ref, y_ref,
    )

    def body(ms, size):
        out_ref[ms] = times_table(flat(y_ref[ms]), fwd_ref).reshape(size, channels, 2 * tokens)

    groups(n, channels, body)


def conv_kernel(
    sign, n, channels, tokens, x_ref, spec_ref, tw_ref, fwd_ref, inv_ref, out_ref, own_ref, y_ref
):
    outer_forward(lambda n1, rows: x_ref[n1, rows], n, channels, tokens, tw_ref, y_ref)

    def body(ms, size):
        own = times_table(flat(y_ref[ms]), fwd_ref)
        own_ref[ms] = own.reshape(size, channels, 2 * tokens)
        spec = flat(spec_ref[ms])
        re, im = own[:, :tokens], own[:, tokens:]
        s_re, s_im = spec[:, :tokens], spec[:, tokens:] * sign
        both = jnp.concatenate([re * s_re - im * s_im, re * s_im + im * s_re], axis=1)
        y_ref[ms] = times_table(both, inv_ref).reshape(size, channels, 2 * tokens)

    groups(n, channels, body)

    def write(n1, rows, value):
        out_ref[n1, rows] = value

    outer_inverse(write, n, channels, tokens, tw_ref, y_ref)


def filter_grad_kernel(scale, n, channels, tokens, p_ref, g_ref, tw_ref, inv_ref, out_ref, y_ref):
    def body(ms, size):
        p, g = flat(p_ref[ms]), flat(g_ref[ms])
        p_re, p_im = p[:, :tokens], p[:, tokens:]
        re, im = g[:, :tokens], g[:, tokens:]
        both = jnp.concatenate([re * p_re + im * p_im, im * p_re - re * p_im], axis=1)
        y_ref[ms] = times_table(both, inv_ref).reshape(size, channels, 2 * tokens)

    groups(n, channels, body)

    def write(n1, rows, value):
        out_ref[rows, n1 * tokens : (n1 + 1) * tokens] = value * scale

    outer_inverse(write, n, channels, tokens, tw_ref, y_ref)


def call(body, outs, n, channels, tokens, passes):
    size = n * channels * tokens
    return pl.pallas_call(
        body,
        out_shape=outs,
        scratch_shapes=[pltpu.VMEM((n, channels, 2 * tokens), jnp.float32)],
        compiler_params=pltpu.CompilerParams(vmem_limit_bytes=VMEM_BYTES),
        cost_estimate=pl.CostEstimate(
            flops=passes * size * 2 * 2 * tokens * 4, bytes_accessed=6 * size * 4, transcendentals=0
        ),
    )


def product_kernel(a_ref, b_ref, out_ref):
    out_ref[...] = a_ref[...] * b_ref[...]


def gate_kernel(x_ref, a_ref, b_ref, oa_ref, ob_ref):
    x = x_ref[...]
    oa_ref[...] = x * a_ref[...]
    ob_ref[...] = x * b_ref[...]


def tiled(body, n_in, n_out, shape):
    rows = math.gcd(shape[0], 512)
    spec = pl.BlockSpec((rows, shape[1]), lambda i: (i, 0))
    return pl.pallas_call(
        body,
        grid=(shape[0] // rows,),
        in_specs=[spec] * n_in,
        out_specs=[spec] * n_out,
        out_shape=[jax.ShapeDtypeStruct(shape, jnp.float32)] * n_out,
        compiler_params=pltpu.CompilerParams(vmem_limit_bytes=VMEM_BYTES),
        cost_estimate=pl.CostEstimate(
            flops=n_out * shape[0] * shape[1],
            bytes_accessed=(n_in + n_out) * 4 * shape[0] * shape[1],
            transcendentals=0,
        ),
    )


def tables(n, tokens):
    length = n * tokens
    m = np.arange(n)[:, None] + 0.25
    angle = 2 * np.pi * m * np.arange(tokens)[None, :] / length
    tw = np.stack([np.cos(angle), np.sin(angle)])[:, :, None, :]
    tw = np.broadcast_to(tw, (2, n, ROWS, tokens)).astype(np.float32)
    k = np.arange(tokens)
    inner = 2 * np.pi * ((k[:, None] * k[None, :]) % tokens) / tokens
    c, s = np.cos(inner), np.sin(inner)

    def pair(table):
        hi = table.astype(ml_dtypes.bfloat16)
        lo = (table - hi.astype(np.float64)).astype(ml_dtypes.bfloat16)
        return jnp.asarray(np.stack([hi, lo]))

    fwd = pair(np.block([[c, -s], [s, c]]))
    inv = pair(np.block([[c, s], [-s, c]]) / length)
    return jnp.asarray(tw), fwd, inv


def on_device(query_input, key_input, value_input, filters, cotangent):
    n = lax.axis_size("context")
    pair_size = lax.axis_size("dp")
    _, width, tokens = query_input.shape
    channels, length = filters.shape
    scale = 1.0 / math.sqrt(pair_size * length)
    sizes = (n, channels, tokens)
    tw, fwd, inv = tables(n, tokens)
    spectrum = jax.ShapeDtypeStruct((n, channels, 2 * tokens), jnp.float32)
    rows = jax.ShapeDtypeStruct((n, channels, tokens), jnp.float32)
    lags = jax.ShapeDtypeStruct((channels, length), jnp.float32)

    def exchange(x):
        return lax.all_to_all(x.reshape(rows.shape), "context", 0, 0, tiled=True)

    def part(body, *args):
        return lambda *refs: body(*args, *sizes, *refs)

    query, key, value, cot = (
        x.reshape(width, tokens) for x in (query_input, key_input, value_input, cotangent)
    )
    multiply = tiled(product_kernel, 2, 1, (width, tokens))
    (product,) = multiply(key, value)
    (conv_grad,) = multiply(cot, query)
    product_ch = exchange(product)
    grad_ch = exchange(conv_grad)
    filt = call(part(filter_kernel), spectrum, *sizes, 1)(filters, tw, fwd)
    conv_ch, prod_spec = call(part(conv_kernel, 1.0), [rows, spectrum], *sizes, 2)(
        product_ch, filt, tw, fwd, inv
    )
    conv_tok = exchange(conv_ch).reshape(width, tokens)
    back_ch, grad_spec = call(part(conv_kernel, -1.0), [rows, spectrum], *sizes, 2)(
        grad_ch, filt, tw, fwd, inv
    )
    back_tok = exchange(back_ch).reshape(width, tokens)
    own = call(part(filter_grad_kernel, scale), lags, *sizes, 1)(prod_spec, grad_spec, tw, inv)
    if pair_size == 2:
        grad_filter = own + lax.ppermute(own, "dp", [(0, 1), (1, 0)])
    else:
        grad_filter = lax.psum(own, "dp")
    gate = tiled(gate_kernel, 3, 2, (width, tokens))
    gated, grad_query = gate(conv_tok, query, cot)
    grad_key, grad_value = gate(back_tok, value, key)
    shape = query_input.shape
    return (
        gated.reshape(shape),
        grad_query.reshape(shape),
        grad_key.reshape(shape),
        grad_value.reshape(shape),
        grad_filter,
    )


def solution(mesh):
    in_specs = (
        P("dp", None, "context"),
        P("dp", None, "context"),
        P("dp", None, "context"),
        P("context", None),
        P("dp", None, "context"),
    )
    out_specs = (
        P("dp", None, "context"),
        P("dp", None, "context"),
        P("dp", None, "context"),
        P("dp", None, "context"),
        P("context", None),
    )
    return jax.shard_map(
        on_device, mesh=mesh, in_specs=in_specs, out_specs=out_specs, check_vma=False
    )
```

```python
import math

import jax
import jax.numpy as jnp
import ml_dtypes
import numpy as np
from jax import lax
from jax.experimental import pallas as pl
from jax.experimental.pallas import tpu as pltpu
from jax.sharding import PartitionSpec as P

ROWS = 8
MOST_SWAPS = 32
VMEM_BYTES = 24 * 1024 * 1024


def twist(value, turn):
    re, im = value
    turn = turn % 1.0
    if turn == 0.0:
        return re, im
    if turn == 0.25:
        return im, -re
    if turn == 0.5:
        return -re, -im
    if turn == 0.75:
        return -im, re
    if turn in (0.125, 0.375, 0.625, 0.875):
        half = math.sqrt(0.5)
        a, b = (re + im) * half, (im - re) * half
        return twist((a, b), turn - 0.125)
    c, s = math.cos(2 * math.pi * turn), math.sin(2 * math.pi * turn)
    return re * c + im * s, im * c - re * s


def dft(values, sign):
    n = len(values)
    if n == 1:
        return values
    even, odd = dft(values[0::2], sign), dft(values[1::2], sign)
    out = [None] * n
    for k in range(n // 2):
        a, b = even[k], twist(odd[k], sign * k / n)
        out[k] = (a[0] + b[0], a[1] + b[1])
        out[k + n // 2] = (a[0] - b[0], a[1] - b[1])
    return out


def split(x):
    hi = x.astype(jnp.bfloat16)
    lo = (x - hi.astype(jnp.float32)).astype(jnp.bfloat16)
    return hi, lo


def times_table(x, table_ref):
    hi, lo = split(x)
    out = jnp.dot(hi, table_ref[0], preferred_element_type=jnp.float32)
    out += jnp.dot(lo, table_ref[0], preferred_element_type=jnp.float32)
    out += jnp.dot(hi, table_ref[1], preferred_element_type=jnp.float32)
    return out


def outer_forward(read, n, channels, tokens, tw_ref, y_ref):
    @pl.loop(0, channels // ROWS)
    def _(r):
        rows = pl.ds(pl.multiple_of(r * ROWS, ROWS), ROWS)
        values = []
        for n1 in range(n):
            x = read(n1, rows)
            turn = 2 * math.pi * n1 / (4 * n)
            if n1 == 0:
                values.append((x, jnp.zeros_like(x)))
            else:
                values.append((x * math.cos(turn), x * -math.sin(turn)))
        for m, (re, im) in enumerate(dft(values, 1)):
            c, s = tw_ref[0, m], tw_ref[1, m]
            y_ref[m, rows, :tokens] = re * c + im * s
            y_ref[m, rows, tokens:] = im * c - re * s


def outer_inverse(write, n, channels, tokens, tw_ref, y_ref):
    @pl.loop(0, channels // ROWS)
    def _(r):
        rows = pl.ds(pl.multiple_of(r * ROWS, ROWS), ROWS)
        values = []
        for m in range(n):
            re, im = y_ref[m, rows, :tokens], y_ref[m, rows, tokens:]
            c, s = tw_ref[0, m], tw_ref[1, m]
            values.append((re * c - im * s, im * c + re * s))
        for n1, (re, im) in enumerate(dft(values, -1)):
            turn = 2 * math.pi * n1 / (4 * n)
            if n1 == 0:
                write(n1, rows, re)
            else:
                write(n1, rows, re * math.cos(turn) - im * math.sin(turn))


def groups(n, channels, body):
    size = max(1, min(n, 512 // channels))

    @pl.loop(0, n // size)
    def _(i):
        body(pl.ds(i * size, size), size)


def flat(x):
    return x.reshape(x.shape[0] * x.shape[1], x.shape[2])


def filter_kernel(n, channels, tokens, f_ref, tw_ref, fwd_ref, out_ref, y_ref):
    outer_forward(
        lambda n1, rows: f_ref[rows, n1 * tokens : (n1 + 1) * tokens],
        n, channels, tokens, tw_ref, y_ref,
    )

    def body(ms, size):
        out_ref[ms] = times_table(flat(y_ref[ms]), fwd_ref).reshape(size, channels, 2 * tokens)

    groups(n, channels, body)


def partners(n):
    far = list(range(n - 1, n // 2 - 1, -1))
    near = list(range(n // 2 - 1, -1, -1))
    return [d for pair in zip(far, near) for d in pair]


def conv_kernel(sign, n, channels, tokens, *refs):
    x_refs, refs = refs[:n], refs[n:]
    spec_ref, tw_ref, fwd_ref, inv_ref = refs[:4]
    out_refs, (own_ref, x_ref, y_ref) = refs[4 : n + 4], refs[n + 4 :]
    me = lax.axis_index("context")
    for d in partners(n):
        x_ref[me ^ d] = x_refs[d][...]
    outer_forward(lambda n1, rows: x_ref[n1, rows], n, channels, tokens, tw_ref, y_ref)

    def body(ms, size):
        own = times_table(flat(y_ref[ms]), fwd_ref)
        own_ref[ms] = own.reshape(size, channels, 2 * tokens)
        spec = flat(spec_ref[ms])
        re, im = own[:, :tokens], own[:, tokens:]
        s_re, s_im = spec[:, :tokens], spec[:, tokens:] * sign
        both = jnp.concatenate([re * s_re - im * s_im, re * s_im + im * s_re], axis=1)
        y_ref[ms] = times_table(both, inv_ref).reshape(size, channels, 2 * tokens)

    groups(n, channels, body)

    def write(n1, rows, value):
        x_ref[n1, rows] = value

    outer_inverse(write, n, channels, tokens, tw_ref, y_ref)
    for d in partners(n):
        out_refs[d][...] = x_ref[me ^ d]


def filter_grad_kernel(scale, n, channels, tokens, p_ref, g_ref, tw_ref, inv_ref, out_ref, y_ref):
    def body(ms, size):
        p, g = flat(p_ref[ms]), flat(g_ref[ms])
        p_re, p_im = p[:, :tokens], p[:, tokens:]
        re, im = g[:, :tokens], g[:, tokens:]
        both = jnp.concatenate([re * p_re + im * p_im, im * p_re - re * p_im], axis=1)
        y_ref[ms] = times_table(both, inv_ref).reshape(size, channels, 2 * tokens)

    groups(n, channels, body)

    def write(n1, rows, value):
        out_ref[rows, n1 * tokens : (n1 + 1) * tokens] = value * scale

    outer_inverse(write, n, channels, tokens, tw_ref, y_ref)


def call(body, outs, n, channels, tokens, passes, extra=()):
    size = n * channels * tokens
    return pl.pallas_call(
        body,
        out_shape=outs,
        scratch_shapes=[*extra, pltpu.VMEM((n, channels, 2 * tokens), jnp.float32)],
        compiler_params=pltpu.CompilerParams(vmem_limit_bytes=VMEM_BYTES),
        cost_estimate=pl.CostEstimate(
            flops=passes * size * 2 * 2 * tokens * 4, bytes_accessed=6 * size * 4, transcendentals=0
        ),
    )


def product_kernel(n, a_ref, b_ref, *refs):
    out_refs, (a_buf, b_buf, sems) = refs[:n], refs[n:]
    me = lax.axis_index("context")
    copies = {}
    for d in partners(n):
        copies[d] = [
            pltpu.make_async_copy(ref.at[me ^ d], buf.at[d], sems.at[i, d])
            for i, (ref, buf) in enumerate(((a_ref, a_buf), (b_ref, b_buf)))
        ]
        for copy in copies[d]:
            copy.start()
    for d in partners(n):
        for copy in copies[d]:
            copy.wait()
        out_refs[d][...] = a_buf[d] * b_buf[d]


def gate_kernel(n, *refs):
    x_refs, refs = refs[:n], refs[n:]
    a_ref, b_ref, oa_ref, ob_ref, a_buf, b_buf, sems = refs
    me = lax.axis_index("context")
    loads, stores = {}, {}
    for d in partners(n):
        pairs = ((a_ref, a_buf, oa_ref), (b_ref, b_buf, ob_ref))
        loads[d] = [
            pltpu.make_async_copy(ref.at[me ^ d], buf.at[d], sems.at[i, d])
            for i, (ref, buf, _) in enumerate(pairs)
        ]
        stores[d] = [
            pltpu.make_async_copy(buf.at[d], out.at[me ^ d], sems.at[i + 2, d])
            for i, (_, buf, out) in enumerate(pairs)
        ]
        for copy in loads[d]:
            copy.start()
    for d in partners(n):
        x = x_refs[d][...]
        for load, store, buf in zip(loads[d], stores[d], (a_buf, b_buf)):
            load.wait()
            buf[d] = buf[d] * x
            store.start()
    for d in partners(n):
        for store in stores[d]:
            store.wait()


def local_call(body, n, n_in, n_out, shape, blocks):
    whole, block = jax.ShapeDtypeStruct(shape, jnp.float32), jax.ShapeDtypeStruct(shape[1:], jnp.float32)
    hbm, vmem = pl.BlockSpec(memory_space=pltpu.HBM), pl.BlockSpec(memory_space=pltpu.VMEM)
    return pl.pallas_call(
        body,
        in_specs=[vmem] * blocks + [hbm] * n_in,
        out_specs=[hbm] * n_out if n_out else [vmem] * n,
        out_shape=[whole] * n_out if n_out else [block] * n,
        scratch_shapes=[pltpu.VMEM(shape, jnp.float32)] * 2 + [pltpu.SemaphoreType.DMA((4, n))],
        compiler_params=pltpu.CompilerParams(vmem_limit_bytes=VMEM_BYTES),
        cost_estimate=pl.CostEstimate(
            flops=2 * math.prod(shape), bytes_accessed=4 * 4 * math.prod(shape), transcendentals=0
        ),
    )


def tables(n, tokens):
    length = n * tokens
    m = np.arange(n)[:, None] + 0.25
    angle = 2 * np.pi * m * np.arange(tokens)[None, :] / length
    tw = np.stack([np.cos(angle), np.sin(angle)])[:, :, None, :]
    tw = np.broadcast_to(tw, (2, n, ROWS, tokens)).astype(np.float32)
    k = np.arange(tokens)
    inner = 2 * np.pi * ((k[:, None] * k[None, :]) % tokens) / tokens
    c, s = np.cos(inner), np.sin(inner)

    def pair(table):
        hi = table.astype(ml_dtypes.bfloat16)
        lo = (table - hi.astype(np.float64)).astype(ml_dtypes.bfloat16)
        return jnp.asarray(np.stack([hi, lo]))

    fwd = pair(np.block([[c, -s], [s, c]]))
    inv = pair(np.block([[c, s], [-s, c]]) / length)
    return jnp.asarray(tw), fwd, inv


def on_device(query_input, key_input, value_input, filters, cotangent):
    n = lax.axis_size("context")
    pair_size = lax.axis_size("dp")
    _, width, tokens = query_input.shape
    channels, length = filters.shape
    scale = 1.0 / math.sqrt(pair_size * length)
    sizes = (n, channels, tokens)
    tw, fwd, inv = tables(n, tokens)
    spectrum = jax.ShapeDtypeStruct((n, channels, 2 * tokens), jnp.float32)
    rows = jax.ShapeDtypeStruct((n, channels, tokens), jnp.float32)
    lags = jax.ShapeDtypeStruct((channels, length), jnp.float32)

    block = jax.ShapeDtypeStruct(rows.shape[1:], jnp.float32)
    swaps = [[(i, i ^ d) for i in range(n)] for d in range(n)]

    def exchange(blocks):
        if n > MOST_SWAPS:
            order = lax.axis_index("context") ^ jnp.arange(n)
            got = jnp.take(jnp.stack(blocks), order, axis=0)
            got = lax.all_to_all(got, "context", 0, 0, tiled=True)
            return list(jnp.take(got, order, axis=0))
        got = {0: blocks[0]}
        for d in partners(n):
            if d:
                got[d] = lax.ppermute(blocks[d], "context", swaps[d])
        return [got[d] for d in range(n)]

    def part(body, *args):
        return lambda *refs: body(*args, *sizes, *refs)

    query, key, value, cot = (
        x.reshape(rows.shape) for x in (query_input, key_input, value_input, cotangent)
    )
    multiply = local_call(lambda *refs: product_kernel(n, *refs), n, 2, 0, rows.shape, 0)
    product_ch = exchange(multiply(key, value))
    grad_ch = exchange(multiply(cot, query))
    filt = call(part(filter_kernel), spectrum, *sizes, 1)(filters, tw, fwd)
    buffer = [pltpu.VMEM(rows.shape, jnp.float32)]
    *conv_ch, prod_spec = call(part(conv_kernel, 1.0), [block] * n + [spectrum], *sizes, 2, buffer)(
        *product_ch, filt, tw, fwd, inv
    )
    conv_tok = exchange(conv_ch)
    *back_ch, grad_spec = call(part(conv_kernel, -1.0), [block] * n + [spectrum], *sizes, 2, buffer)(
        *grad_ch, filt, tw, fwd, inv
    )
    back_tok = exchange(back_ch)
    own = call(part(filter_grad_kernel, scale), lags, *sizes, 1)(prod_spec, grad_spec, tw, inv)
    if pair_size == 2:
        grad_filter = own + lax.ppermute(own, "dp", [(0, 1), (1, 0)])
    else:
        grad_filter = lax.psum(own, "dp")
    gate = local_call(lambda *refs: gate_kernel(n, *refs), n, 2, 2, rows.shape, n)
    gated, grad_query = gate(*conv_tok, query, cot)
    grad_key, grad_value = gate(*back_tok, value, key)
    shape = query_input.shape
    return (
        gated.reshape(shape),
        grad_query.reshape(shape),
        grad_key.reshape(shape),
        grad_value.reshape(shape),
        grad_filter,
    )


def solution(mesh):
    in_specs = (
        P("dp", None, "context"),
        P("dp", None, "context"),
        P("dp", None, "context"),
        P("context", None),
        P("dp", None, "context"),
    )
    out_specs = (
        P("dp", None, "context"),
        P("dp", None, "context"),
        P("dp", None, "context"),
        P("dp", None, "context"),
        P("context", None),
    )
    return jax.shard_map(
        on_device, mesh=mesh, in_specs=in_specs, out_specs=out_specs, check_vma=False
    )
```

```python
import math

import jax
import jax.numpy as jnp
import ml_dtypes
import numpy as np
from jax import lax
from jax.experimental import pallas as pl
from jax.experimental.pallas import tpu as pltpu
from jax.sharding import PartitionSpec as P

ROWS = 8
PARTS = 4
VMEM_BYTES = 24 * 1024 * 1024
MOST_VMEM = 56 * 1024 * 1024


def twist(value, turn):
    re, im = value
    turn = turn % 1.0
    if turn == 0.0:
        return re, im
    if turn == 0.25:
        return im, -re
    if turn == 0.5:
        return -re, -im
    if turn == 0.75:
        return -im, re
    if turn in (0.125, 0.375, 0.625, 0.875):
        half = math.sqrt(0.5)
        a, b = (re + im) * half, (im - re) * half
        return twist((a, b), turn - 0.125)
    c, s = math.cos(2 * math.pi * turn), math.sin(2 * math.pi * turn)
    return re * c + im * s, im * c - re * s


def dft(values, sign):
    n = len(values)
    if n == 1:
        return values
    even, odd = dft(values[0::2], sign), dft(values[1::2], sign)
    out = [None] * n
    for k in range(n // 2):
        a, b = even[k], twist(odd[k], sign * k / n)
        out[k] = (a[0] + b[0], a[1] + b[1])
        out[k + n // 2] = (a[0] - b[0], a[1] - b[1])
    return out


def split(x):
    hi = x.astype(jnp.bfloat16)
    lo = (x - hi.astype(jnp.float32)).astype(jnp.bfloat16)
    return hi, lo


def times_table(x, table_ref):
    hi, lo = split(x)
    out = jnp.dot(hi, table_ref[0], preferred_element_type=jnp.float32)
    out += jnp.dot(lo, table_ref[0], preferred_element_type=jnp.float32)
    out += jnp.dot(hi, table_ref[1], preferred_element_type=jnp.float32)
    return out


def outer_forward(read, n, channels, tokens, tw_ref, y_ref):
    @pl.loop(0, channels // ROWS)
    def _(r):
        rows = pl.ds(pl.multiple_of(r * ROWS, ROWS), ROWS)
        values = []
        for n1 in range(n):
            x = read(n1, rows)
            turn = 2 * math.pi * n1 / (4 * n)
            if n1 == 0:
                values.append((x, jnp.zeros_like(x)))
            else:
                values.append((x * math.cos(turn), x * -math.sin(turn)))
        for m, (re, im) in enumerate(dft(values, 1)):
            c, s = tw_ref[0, m], tw_ref[1, m]
            y_ref[m, rows, :tokens] = re * c + im * s
            y_ref[m, rows, tokens:] = im * c - re * s


def outer_inverse(write, n, channels, tokens, tw_ref, y_ref):
    @pl.loop(0, channels // ROWS)
    def _(r):
        rows = pl.ds(pl.multiple_of(r * ROWS, ROWS), ROWS)
        values = []
        for m in range(n):
            re, im = y_ref[m, rows, :tokens], y_ref[m, rows, tokens:]
            c, s = tw_ref[0, m], tw_ref[1, m]
            values.append((re * c - im * s, im * c + re * s))
        for n1, (re, im) in enumerate(dft(values, -1)):
            turn = 2 * math.pi * n1 / (4 * n)
            if n1 == 0:
                write(n1, rows, re)
            else:
                write(n1, rows, re * math.cos(turn) - im * math.sin(turn))


def flat(x):
    return x.reshape(x.shape[0] * x.shape[1], x.shape[2])


def spectrum_copies(n, pairs, sem):
    size = max(1, n // PARTS)
    return [
        [
            pltpu.make_async_copy(src.at[part], dst.at[part], sem.at[j, i])
            for j, (src, dst) in enumerate(pairs)
        ]
        for i, part in enumerate(pl.ds(k, size) for k in range(0, n, size))
    ]


def start_all(copies):
    for copy in copies:
        copy.start()


def wait_all(copies):
    for copy in copies:
        copy.wait()


def filter_kernel(n, channels, tokens, f_ref, tw_ref, fwd_ref, out_ref, own_ref, y_ref, sem):
    outer_forward(
        lambda n1, rows: f_ref[rows, n1 * tokens : (n1 + 1) * tokens],
        n, channels, tokens, tw_ref, y_ref,
    )
    stores = spectrum_copies(n, [(own_ref, out_ref)], sem)
    size = n // len(stores)
    for i, store in enumerate(stores):
        ms = pl.ds(i * size, size)
        own_ref[ms] = times_table(flat(y_ref[ms]), fwd_ref).reshape(size, channels, 2 * tokens)
        start_all(store)
    for store in stores:
        wait_all(store)


def conv_kernel(
    n, channels, tokens, x_ref, tw_ref, fwd_ref, inv_ref, spec_ref, out_ref, p_ref, g_ref,
    spec_buf, p_buf, g_buf, p_y, g_y, sem,
):
    loads = spectrum_copies(n, [(spec_ref, spec_buf)], sem)
    for load in loads:
        start_all(load)
    for j, y_ref in enumerate((p_y, g_y)):
        outer_forward(
            lambda n1, rows: x_ref[n1, j, rows], n, channels, tokens, tw_ref, y_ref
        )
    for load in loads:
        wait_all(load)
    stores = spectrum_copies(n, [(p_buf, p_ref), (g_buf, g_ref)], sem)
    size = n // len(stores)
    for i, store in enumerate(stores):
        ms = pl.ds(i * size, size)
        spec = flat(spec_buf[ms])
        for sign, own_buf, y_ref in ((1.0, p_buf, p_y), (-1.0, g_buf, g_y)):
            own = times_table(flat(y_ref[ms]), fwd_ref)
            own_buf[ms] = own.reshape(size, channels, 2 * tokens)
            re, im = own[:, :tokens], own[:, tokens:]
            s_re, s_im = spec[:, :tokens], spec[:, tokens:] * sign
            both = jnp.concatenate([re * s_re - im * s_im, re * s_im + im * s_re], axis=1)
            y_ref[ms] = times_table(both, inv_ref).reshape(size, channels, 2 * tokens)
        start_all(store)
    for j, y_ref in enumerate((p_y, g_y)):

        def write(n1, rows, value):
            out_ref[n1, j, rows] = value

        outer_inverse(write, n, channels, tokens, tw_ref, y_ref)
    for store in stores:
        wait_all(store)


def filter_grad_kernel(
    scale, n, channels, tokens, tw_ref, inv_ref, p_ref, g_ref, out_ref, p_buf, g_buf, y_ref, sem
):
    loads = spectrum_copies(n, [(p_ref, p_buf), (g_ref, g_buf)], sem)
    for load in loads:
        start_all(load)
    size = n // len(loads)
    for i, load in enumerate(loads):
        ms = pl.ds(i * size, size)
        wait_all(load)
        p, g = flat(p_buf[ms]), flat(g_buf[ms])
        p_re, p_im = p[:, :tokens], p[:, tokens:]
        re, im = g[:, :tokens], g[:, tokens:]
        both = jnp.concatenate([re * p_re + im * p_im, im * p_re - re * p_im], axis=1)
        y_ref[ms] = times_table(both, inv_ref).reshape(size, channels, 2 * tokens)

    def write(n1, rows, value):
        out_ref[rows, n1 * tokens : (n1 + 1) * tokens] = value * scale

    outer_inverse(write, n, channels, tokens, tw_ref, y_ref)


def call(body, n_vmem, n_hbm, outs, spectra, n, channels, tokens, passes):
    size = n * channels * tokens
    hbm, vmem = pl.BlockSpec(memory_space=pltpu.HBM), pl.BlockSpec(memory_space=pltpu.VMEM)
    spectrum = (n, channels, 2 * tokens)
    return pl.pallas_call(
        body,
        in_specs=[vmem] * n_vmem + [hbm] * n_hbm,
        out_specs=[hbm if out.shape == spectrum else vmem for out in outs],
        out_shape=outs,
        scratch_shapes=[pltpu.VMEM(spectrum, jnp.float32)] * spectra
        + [pltpu.SemaphoreType.DMA((2, PARTS))],
        compiler_params=pltpu.CompilerParams(vmem_limit_bytes=VMEM_BYTES),
        cost_estimate=pl.CostEstimate(
            flops=passes * size * 2 * 2 * tokens * 4, bytes_accessed=6 * size * 4, transcendentals=0
        ),
    )


def product_kernel(*refs):
    in_refs, (out_ref, *bufs, sem) = refs[:4], refs[4:]
    n = out_ref.shape[0]
    size = max(1, n // PARTS)
    parts = [pl.ds(k, size) for k in range(0, n, size)]
    loads = [
        [
            pltpu.make_async_copy(ref.at[part], buf.at[part], sem.at[j, i])
            for j, (ref, buf) in enumerate(zip(in_refs, bufs))
        ]
        for i, part in enumerate(parts)
    ]
    for load in loads:
        start_all(load)
    for load, part in zip(loads, parts):
        wait_all(load)
        out_ref[part, 0] = bufs[0][part] * bufs[1][part]
        out_ref[part, 1] = bufs[2][part] * bufs[3][part]


def gate_kernel(x_ref, *refs):
    in_refs, out_refs, bufs, sem = refs[:4], refs[4:8], refs[8:12], refs[12]
    n = x_ref.shape[0]
    size = max(1, n // PARTS)
    stores = []
    for i, k in enumerate(range(0, n, size)):
        part = pl.ds(k, size)
        for j, (ref, buf, out) in enumerate(zip(in_refs, bufs, out_refs)):
            buf[part] = x_ref[part, j // 2] * ref[part]
            stores.append(pltpu.make_async_copy(buf.at[part], out.at[part], sem.at[j, i]))
            stores[-1].start()
    wait_all(stores)


def rows_call(body, in_vmem, out, shape, grant):
    hbm, vmem = pl.BlockSpec(memory_space=pltpu.HBM), pl.BlockSpec(memory_space=pltpu.VMEM)
    return pl.pallas_call(
        body,
        in_specs=[vmem if near else hbm for near in in_vmem],
        out_specs=[hbm] * 4 if out == shape else vmem,
        out_shape=[jax.ShapeDtypeStruct(out, jnp.float32)] * 4
        if out == shape
        else jax.ShapeDtypeStruct(out, jnp.float32),
        scratch_shapes=[pltpu.VMEM(shape, jnp.float32)] * 4 + [pltpu.SemaphoreType.DMA((4, PARTS))],
        compiler_params=pltpu.CompilerParams(vmem_limit_bytes=grant),
        cost_estimate=pl.CostEstimate(
            flops=4 * math.prod(shape), bytes_accessed=10 * 4 * math.prod(shape), transcendentals=0
        ),
    )


def tables(n, tokens):
    length = n * tokens
    m = np.arange(n)[:, None] + 0.25
    angle = 2 * np.pi * m * np.arange(tokens)[None, :] / length
    tw = np.stack([np.cos(angle), np.sin(angle)])[:, :, None, :]
    tw = np.broadcast_to(tw, (2, n, ROWS, tokens)).astype(np.float32)
    k = np.arange(tokens)
    inner = 2 * np.pi * ((k[:, None] * k[None, :]) % tokens) / tokens
    c, s = np.cos(inner), np.sin(inner)

    def pair(table):
        hi = table.astype(ml_dtypes.bfloat16)
        lo = (table - hi.astype(np.float64)).astype(ml_dtypes.bfloat16)
        return jnp.asarray(np.stack([hi, lo]))

    fwd = pair(np.block([[c, -s], [s, c]]))
    inv = pair(np.block([[c, s], [-s, c]]) / length)
    return jnp.asarray(tw), fwd, inv


def on_device(query_input, key_input, value_input, filters, cotangent):
    n = lax.axis_size("context")
    pair_size = lax.axis_size("dp")
    _, width, tokens = query_input.shape
    channels, length = filters.shape
    scale = 1.0 / math.sqrt(pair_size * length)
    sizes = (n, channels, tokens)
    tw, fwd, inv = tables(n, tokens)
    spectrum = jax.ShapeDtypeStruct((n, channels, 2 * tokens), jnp.float32)
    rows = jax.ShapeDtypeStruct((n, channels, tokens), jnp.float32)
    lags = jax.ShapeDtypeStruct((channels, length), jnp.float32)

    pair = (n, 2, channels, tokens)

    def exchange(x):
        return lax.all_to_all(x, "context", 0, 0, tiled=True)

    def part(body, *args):
        return lambda *refs: body(*args, *sizes, *refs)

    query, key, value, cot = (
        x.reshape(rows.shape) for x in (query_input, key_input, value_input, cotangent)
    )
    products = rows_call(product_kernel, [False] * 4, pair, rows.shape, MOST_VMEM)(
        key, value, cot, query
    )
    products_ch = exchange(products)
    (filt,) = call(part(filter_kernel), 3, 0, [spectrum], 2, *sizes, 1)(filters, tw, fwd)
    outs = [jax.ShapeDtypeStruct(pair, jnp.float32), spectrum, spectrum]
    results_ch, prod_spec, grad_spec = call(part(conv_kernel), 4, 1, outs, 5, *sizes, 4)(
        products_ch, tw, fwd, inv, filt
    )
    results = exchange(results_ch)
    (own,) = call(part(filter_grad_kernel, scale), 2, 2, [lags], 3, *sizes, 1)(
        tw, inv, prod_spec, grad_spec
    )
    if pair_size == 2:
        grad_filter = own + lax.ppermute(own, "dp", [(0, 1), (1, 0)])
    else:
        grad_filter = lax.psum(own, "dp")
    gated, grad_query, grad_key, grad_value = rows_call(
        gate_kernel, [True] * 5, rows.shape, rows.shape, VMEM_BYTES
    )(results, query, cot, value, key)
    shape = query_input.shape
    return (
        gated.reshape(shape),
        grad_query.reshape(shape),
        grad_key.reshape(shape),
        grad_value.reshape(shape),
        grad_filter,
    )


def solution(mesh):
    in_specs = (
        P("dp", None, "context"),
        P("dp", None, "context"),
        P("dp", None, "context"),
        P("context", None),
        P("dp", None, "context"),
    )
    out_specs = (
        P("dp", None, "context"),
        P("dp", None, "context"),
        P("dp", None, "context"),
        P("dp", None, "context"),
        P("context", None),
    )
    return jax.shard_map(
        on_device, mesh=mesh, in_specs=in_specs, out_specs=out_specs, check_vma=False
    )
```

```python
import math

import jax
import jax.numpy as jnp
import ml_dtypes
import numpy as np
from jax import lax
from jax.experimental import pallas as pl
from jax.experimental.pallas import tpu as pltpu
from jax.sharding import PartitionSpec as P

ROWS = 8
PARTS = 4
VMEM_BYTES = 24 * 1024 * 1024


def twist(value, turn):
    re, im = value
    turn = turn % 1.0
    if turn == 0.0:
        return re, im
    if turn == 0.25:
        return im, -re
    if turn == 0.5:
        return -re, -im
    if turn == 0.75:
        return -im, re
    if turn in (0.125, 0.375, 0.625, 0.875):
        half = math.sqrt(0.5)
        a, b = (re + im) * half, (im - re) * half
        return twist((a, b), turn - 0.125)
    c, s = math.cos(2 * math.pi * turn), math.sin(2 * math.pi * turn)
    return re * c + im * s, im * c - re * s


def dft(values, sign):
    n = len(values)
    if n == 1:
        return values
    even, odd = dft(values[0::2], sign), dft(values[1::2], sign)
    out = [None] * n
    for k in range(n // 2):
        a, b = even[k], twist(odd[k], sign * k / n)
        out[k] = (a[0] + b[0], a[1] + b[1])
        out[k + n // 2] = (a[0] - b[0], a[1] - b[1])
    return out


def split(x):
    hi = x.astype(jnp.bfloat16)
    lo = (x - hi.astype(jnp.float32)).astype(jnp.bfloat16)
    return hi, lo


def times_table(x, table_ref):
    hi, lo = split(x)
    out = jnp.dot(hi, table_ref[0], preferred_element_type=jnp.float32)
    out += jnp.dot(lo, table_ref[0], preferred_element_type=jnp.float32)
    out += jnp.dot(hi, table_ref[1], preferred_element_type=jnp.float32)
    return out


def outer_forward(read, n, channels, tokens, tw_ref, y_ref):
    @pl.loop(0, channels // ROWS)
    def _(r):
        rows = pl.ds(pl.multiple_of(r * ROWS, ROWS), ROWS)
        values = []
        for n1 in range(n):
            x = read(n1, rows)
            turn = 2 * math.pi * n1 / (4 * n)
            if n1 == 0:
                values.append((x, jnp.zeros_like(x)))
            else:
                values.append((x * math.cos(turn), x * -math.sin(turn)))
        for m, (re, im) in enumerate(dft(values, 1)):
            c, s = tw_ref[0, m], tw_ref[1, m]
            y_ref[m, rows, :tokens] = re * c + im * s
            y_ref[m, rows, tokens:] = im * c - re * s


def outer_inverse(write, n, channels, tokens, tw_ref, y_ref):
    @pl.loop(0, channels // ROWS)
    def _(r):
        rows = pl.ds(pl.multiple_of(r * ROWS, ROWS), ROWS)
        values = []
        for m in range(n):
            re, im = y_ref[m, rows, :tokens], y_ref[m, rows, tokens:]
            c, s = tw_ref[0, m], tw_ref[1, m]
            values.append((re * c - im * s, im * c + re * s))
        for n1, (re, im) in enumerate(dft(values, -1)):
            turn = 2 * math.pi * n1 / (4 * n)
            if n1 == 0:
                write(n1, rows, re)
            else:
                write(n1, rows, re * math.cos(turn) - im * math.sin(turn))


def flat(x):
    return x.reshape(x.shape[0] * x.shape[1], x.shape[2])


def start_all(copies):
    for copy in copies:
        copy.start()


def wait_all(copies):
    for copy in copies:
        copy.wait()


def parts_of(size):
    step = max(1, size // PARTS)
    return [pl.ds(k, step) for k in range(0, size, step)]


def side(half):
    return lax.axis_index("context") // half


def filter_kernel(n, channels, tokens, f_ref, tw_ref, fwd_ref, out_ref, y_ref):
    outer_forward(
        lambda n1, rows: f_ref[rows, n1 * tokens : (n1 + 1) * tokens],
        n, channels, tokens, tw_ref, y_ref,
    )
    for ms in parts_of(n):
        out_ref[ms] = times_table(flat(y_ref[ms]), fwd_ref).reshape(ms.size, channels, 2 * tokens)


def conv_middle(sign, n, channels, tokens, fwd_ref, inv_ref, spec_ref, own_ref, y_ref):
    for ms in parts_of(n):
        own = times_table(flat(y_ref[ms]), fwd_ref)
        own_ref[ms] = own.reshape(ms.size, channels, 2 * tokens)
        spec = flat(spec_ref[ms])
        re, im = own[:, :tokens], own[:, tokens:]
        s_re, s_im = spec[:, :tokens], spec[:, tokens:] * sign
        both = jnp.concatenate([re * s_re - im * s_im, re * s_im + im * s_re], axis=1)
        y_ref[ms] = times_table(both, inv_ref).reshape(ms.size, channels, 2 * tokens)


def conv_kernel(
    n, channels, tokens, x_ref, tw_ref, fwd_ref, inv_ref, spec_ref, after_ref,
    keep_ref, send_ref, own_ref, buf_ref, y_ref, sem,
):
    half = n // 2
    mine = side(half)
    outer_forward(
        lambda n1, rows: x_ref[n1 % half, mine ^ (n1 // half), rows],
        n, channels, tokens, tw_ref, y_ref,
    )
    conv_middle(1.0, n, channels, tokens, fwd_ref, inv_ref, spec_ref, own_ref, y_ref)

    def write(n1, rows, value):
        buf_ref[n1, rows] = value

    outer_inverse(write, n, channels, tokens, tw_ref, y_ref)
    keep_ref[...] = buf_ref[pl.ds(mine * half, half)]
    send_ref[...] = buf_ref[pl.ds((1 - mine) * half, half)]


def back_kernel(
    n, channels, tokens, near_ref, far_ref, tw_ref, fwd_ref, inv_ref, spec_ref, after_ref,
    out_ref, own_ref, buf_ref, y_ref, sem,
):
    half = n // 2
    mine = side(half)
    for r in range(half):
        buf_ref[r, mine] = near_ref[r, mine]
        buf_ref[r, 1 - mine] = far_ref[r]
    outer_forward(
        lambda n1, rows: buf_ref[n1 % half, n1 // half, rows],
        n, channels, tokens, tw_ref, y_ref,
    )
    conv_middle(-1.0, n, channels, tokens, fwd_ref, inv_ref, spec_ref, own_ref, y_ref)

    def write(n1, rows, value):
        buf_ref[n1 % half, n1 // half, rows] = value

    outer_inverse(write, n, channels, tokens, tw_ref, y_ref)
    stores = [
        pltpu.make_async_copy(buf_ref.at[part], out_ref.at[part], sem.at[i])
        for i, part in enumerate(parts_of(half))
    ]
    start_all(stores)
    wait_all(stores)


def filter_grad_kernel(scale, n, channels, tokens, tw_ref, inv_ref, p_ref, g_ref, out_ref, y_ref):
    for ms in parts_of(n):
        p, g = flat(p_ref[ms]), flat(g_ref[ms])
        p_re, p_im = p[:, :tokens], p[:, tokens:]
        re, im = g[:, :tokens], g[:, tokens:]
        both = jnp.concatenate([re * p_re + im * p_im, im * p_re - re * p_im], axis=1)
        y_ref[ms] = times_table(both, inv_ref).reshape(ms.size, channels, 2 * tokens)

    def write(n1, rows, value):
        out_ref[rows, n1 * tokens : (n1 + 1) * tokens] = value * scale

    outer_inverse(write, n, channels, tokens, tw_ref, y_ref)


def load_pairs(n, a_ref, b_ref, a_buf, b_buf, sem):
    loads = []
    for i, part in enumerate(parts_of(n)):
        loads.append(
            [
                pltpu.make_async_copy(a_ref.at[part], a_buf.at[part], sem.at[0, i]),
                pltpu.make_async_copy(b_ref.at[part], b_buf.at[part], sem.at[1, i]),
            ]
        )
        start_all(loads[-1])
    return loads


def product_split_kernel(n, a_ref, b_ref, keep_ref, send_ref, a_buf, b_buf, sem):
    half = n // 2
    mine = side(half)
    loads = load_pairs(n, a_ref, b_ref, a_buf, b_buf, sem)
    for load in loads:
        wait_all(load)
    for ref, first in ((send_ref, (1 - mine) * half), (keep_ref, mine * half)):
        for k in range(half):
            ref[k] = a_buf[first + k] * b_buf[first + k]


def product_kernel(n, a_ref, b_ref, after_ref, out_ref, a_buf, b_buf, buf_ref, sem):
    half = n // 2
    loads = load_pairs(n, a_ref, b_ref, a_buf, b_buf, sem)
    for load in loads:
        wait_all(load)
    stores = [
        pltpu.make_async_copy(buf_ref.at[part], out_ref.at[part], sem.at[2, i])
        for i, part in enumerate(parts_of(half))
    ]
    for part, store in zip(parts_of(half), stores):
        for s in range(2):
            rows = pl.ds(part.start + s * half, part.size)
            buf_ref[part, s] = a_buf[rows] * b_buf[rows]
        store.start()
    wait_all(stores)


def send_kernel(half, x_ref, send_ref):
    send_ref[...] = x_ref[:, 1 - side(half)]


def merge_kernel(half, keep_ref, got_ref, after_ref, out_ref, sem):
    stores = [
        pltpu.make_async_copy(ref.at[part], out_ref.at[part, s], sem.at[s, i])
        for i, part in enumerate(parts_of(half))
        for s, ref in enumerate((keep_ref, got_ref))
    ]
    start_all(stores)
    wait_all(stores)


def gate_parts(n, blocks, a_ref, b_ref, outs, bufs, sem):
    stores = []
    size = max(1, n // 2 // PARTS)
    for h, (read, first) in enumerate(blocks):
        for i, k in enumerate(range(0, n // 2, size)):
            part = pl.ds(first + k, size)
            x = read(pl.ds(k, size))
            for j, (ref, buf, out) in enumerate(zip((a_ref, b_ref), bufs, outs)):
                buf[part] = x * ref[part]
                stores.append(pltpu.make_async_copy(buf.at[part], out.at[part], sem.at[j, h, i]))
                stores[-1].start()
    wait_all(stores)


def gate_kernel(n, x_ref, a_ref, b_ref, oa_ref, ob_ref, a_buf, b_buf, sem):
    half = n // 2
    blocks = [
        (lambda part, s=s: x_ref[part, s], (side(half) ^ s) * half) for s in range(2)
    ]
    gate_parts(n, blocks, a_ref, b_ref, (oa_ref, ob_ref), (a_buf, b_buf), sem)


def gate_split_kernel(n, near_ref, far_ref, a_ref, b_ref, oa_ref, ob_ref, a_buf, b_buf, sem):
    half = n // 2
    mine = side(half)
    blocks = [
        (lambda part: near_ref[part, mine], mine * half),
        (lambda part: far_ref[part], (1 - mine) * half),
    ]
    gate_parts(n, blocks, a_ref, b_ref, (oa_ref, ob_ref), (a_buf, b_buf), sem)


SPACES = {"v": pltpu.VMEM, "h": pltpu.HBM, "a": pl.ANY}


def kernel_call(body, ins, outs, scratch, flops=0):
    shapes = [SPACES[space](shape, jnp.float32) for space, shape in outs]

    def run(*args):
        args = [
            pltpu.with_memory_space_constraint(x, pltpu.HBM) if space == "h" else x
            for space, x in zip(ins, args, strict=True)
        ]
        size = sum(math.prod(x.shape) for x in (*args, *shapes))
        return pl.pallas_call(
            body,
            in_specs=[pl.BlockSpec(memory_space=SPACES[space]) for space in ins],
            out_specs=[pl.BlockSpec(memory_space=SPACES[space]) for space, _ in outs],
            out_shape=shapes,
            scratch_shapes=scratch,
            compiler_params=pltpu.CompilerParams(vmem_limit_bytes=VMEM_BYTES),
            cost_estimate=pl.CostEstimate(flops=flops, bytes_accessed=4 * size, transcendentals=0),
        )(*args)

    return run


def tables(n, tokens):
    length = n * tokens
    m = np.arange(n)[:, None] + 0.25
    angle = 2 * np.pi * m * np.arange(tokens)[None, :] / length
    tw = np.stack([np.cos(angle), np.sin(angle)])[:, :, None, :]
    tw = np.broadcast_to(tw, (2, n, ROWS, tokens)).astype(np.float32)
    k = np.arange(tokens)
    inner = 2 * np.pi * ((k[:, None] * k[None, :]) % tokens) / tokens
    c, s = np.cos(inner), np.sin(inner)

    def pair(table):
        hi = table.astype(ml_dtypes.bfloat16)
        lo = (table - hi.astype(np.float64)).astype(ml_dtypes.bfloat16)
        return jnp.asarray(np.stack([hi, lo]))

    fwd = pair(np.block([[c, -s], [s, c]]))
    inv = pair(np.block([[c, s], [-s, c]]) / length)
    return jnp.asarray(tw), fwd, inv


def on_device(query_input, key_input, value_input, filters, cotangent):
    n = lax.axis_size("context")
    pair_size = lax.axis_size("dp")
    _, width, tokens = query_input.shape
    channels, length = filters.shape
    scale = 1.0 / math.sqrt(pair_size * length)
    sizes = (n, channels, tokens)
    tw, fwd, inv = tables(n, tokens)
    half = n // 2
    blocks, spectrum = (n, channels, tokens), (n, channels, 2 * tokens)
    halves, paired, lags = (half, channels, tokens), (half, 2, channels, tokens), (channels, length)
    flops = 4 * 2 * 2 * tokens * n * channels * tokens
    f32 = jnp.float32
    y = pltpu.VMEM(spectrum, f32)

    def semaphores(*shape):
        return pltpu.SemaphoreType.DMA(shape)

    def part(body, *args):
        return lambda *refs: body(*args, *refs)

    def mirror(x):
        return lax.ppermute(x, "context", [(i, i ^ half) for i in range(n)])

    def within_half(x):
        members = [[h * half + r for r in range(half)] for h in range(2)]
        return lax.all_to_all(x, "context", 0, 0, axis_index_groups=members, tiled=True)

    query, key, value, cot = (
        x.reshape(blocks) for x in (query_input, key_input, value_input, cotangent)
    )
    bufs = [pltpu.VMEM(blocks, f32)] * 2
    send = kernel_call(part(send_kernel, half), "v", [("v", halves)], [])
    merge = kernel_call(
        part(merge_kernel, half), "aaa", [("h", paired)], [semaphores(2, PARTS)]
    )

    keep_p, send_p = kernel_call(
        part(product_split_kernel, n), "hh", [("v", halves)] * 2, [*bufs, semaphores(2, PARTS)]
    )(key, value)
    got_p = mirror(send_p)
    (conv_grad,) = kernel_call(
        part(product_kernel, n), "hha", [("h", paired)],
        [*bufs, pltpu.VMEM(paired, f32), semaphores(3, PARTS)],
    )(cot, query, keep_p)
    near_g = within_half(conv_grad)
    (send_g,) = send(near_g)
    far_g = mirror(send_g)
    (filt,) = kernel_call(
        part(filter_kernel, *sizes), "vvv", [("v", spectrum)], [y], flops
    )(filters, tw, fwd)
    product_ch = within_half(*merge(keep_p, got_p, send_g))
    keep_c, send_c, prod_spec = kernel_call(
        part(conv_kernel, *sizes), "vvvvva", [("v", halves)] * 2 + [("v", spectrum)],
        [pltpu.VMEM(blocks, f32), y, semaphores(PARTS)], 2 * flops,
    )(product_ch, tw, fwd, inv, filt, send_g)
    got_c = mirror(send_c)
    back_ch, grad_spec = kernel_call(
        part(back_kernel, *sizes), "vvvvvva", [("h", paired), ("v", spectrum)],
        [pltpu.VMEM(paired, f32), y, semaphores(PARTS)], 2 * flops,
    )(near_g, far_g, tw, fwd, inv, filt, keep_c)
    near_b = within_half(back_ch)
    (send_b,) = send(near_b)
    far_b = mirror(send_b)
    conv_tok = within_half(*merge(keep_c, got_c, send_b))
    (own,) = kernel_call(
        part(filter_grad_kernel, scale, *sizes), "vvvv", [("v", lags)], [y], flops
    )(tw, inv, prod_spec, grad_spec)
    if pair_size == 2:
        grad_filter = own + lax.ppermute(own, "dp", [(0, 1), (1, 0)])
    else:
        grad_filter = lax.psum(own, "dp")
    gate_scratch = [*bufs, semaphores(2, 2, PARTS)]
    gated, grad_query = kernel_call(
        part(gate_kernel, n), "vvv", [("h", blocks)] * 2, gate_scratch
    )(conv_tok, query, cot)
    grad_key, grad_value = kernel_call(
        part(gate_split_kernel, n), "vvvv", [("h", blocks)] * 2, gate_scratch
    )(near_b, far_b, value, key)
    shape = query_input.shape
    return (
        gated.reshape(shape),
        grad_query.reshape(shape),
        grad_key.reshape(shape),
        grad_value.reshape(shape),
        grad_filter,
    )


def solution(mesh):
    in_specs = (
        P("dp", None, "context"),
        P("dp", None, "context"),
        P("dp", None, "context"),
        P("context", None),
        P("dp", None, "context"),
    )
    out_specs = (
        P("dp", None, "context"),
        P("dp", None, "context"),
        P("dp", None, "context"),
        P("dp", None, "context"),
        P("context", None),
    )
    return jax.shard_map(
        on_device, mesh=mesh, in_specs=in_specs, out_specs=out_specs, check_vma=False
    )
```

```python
import math

import jax
import jax.numpy as jnp
import ml_dtypes
import numpy as np
from jax import lax
from jax.experimental import pallas as pl
from jax.experimental.pallas import tpu as pltpu
from jax.sharding import PartitionSpec as P

ROWS = 8
PLANES = 4
PARTS = 4
VMEM_BYTES = 24 * 1024 * 1024


def twist(value, turn):
    re, im = value
    turn = turn % 1.0
    if turn == 0.0:
        return re, im
    if turn == 0.25:
        return im, -re
    if turn == 0.5:
        return -re, -im
    if turn == 0.75:
        return -im, re
    if turn in (0.125, 0.375, 0.625, 0.875):
        half = math.sqrt(0.5)
        a, b = (re + im) * half, (im - re) * half
        return twist((a, b), turn - 0.125)
    c, s = math.cos(2 * math.pi * turn), math.sin(2 * math.pi * turn)
    return re * c + im * s, im * c - re * s


def dft(values, sign):
    n = len(values)
    if n == 1:
        return values
    even, odd = dft(values[0::2], sign), dft(values[1::2], sign)
    out = [None] * n
    for k in range(n // 2):
        a, b = even[k], twist(odd[k], sign * k / n)
        out[k] = (a[0] + b[0], a[1] + b[1])
        out[k + n // 2] = (a[0] - b[0], a[1] - b[1])
    return out


def split(x):
    hi = x.astype(jnp.bfloat16)
    lo = (x - hi.astype(jnp.float32)).astype(jnp.bfloat16)
    return hi, lo


def times_table(x, table_ref):
    hi, lo = split(x)
    out = jnp.dot(hi, table_ref[0], preferred_element_type=jnp.float32)
    out += jnp.dot(lo, table_ref[0], preferred_element_type=jnp.float32)
    out += jnp.dot(hi, table_ref[1], preferred_element_type=jnp.float32)
    return out


def outer_forward(read, n, channels, tokens, tw_ref, y_ref):
    @pl.loop(0, channels // ROWS)
    def _(r):
        rows = pl.ds(pl.multiple_of(r * ROWS, ROWS), ROWS)
        values = []
        for n1 in range(n):
            x = read(n1, rows)
            turn = 2 * math.pi * n1 / (4 * n)
            if n1 == 0:
                values.append((x, jnp.zeros_like(x)))
            else:
                values.append((x * math.cos(turn), x * -math.sin(turn)))
        for m, (re, im) in enumerate(dft(values, 1)):
            c, s = tw_ref[0, m], tw_ref[1, m]
            y_ref[m, rows, :tokens] = re * c + im * s
            y_ref[m, rows, tokens:] = im * c - re * s


def outer_inverse(write, n, channels, tokens, tw_ref, y_ref):
    @pl.loop(0, channels // ROWS)
    def _(r):
        rows = pl.ds(pl.multiple_of(r * ROWS, ROWS), ROWS)
        values = []
        for m in range(n):
            re, im = y_ref[m, rows, :tokens], y_ref[m, rows, tokens:]
            c, s = tw_ref[0, m], tw_ref[1, m]
            values.append((re * c - im * s, im * c + re * s))
        for n1, (re, im) in enumerate(dft(values, -1)):
            turn = 2 * math.pi * n1 / (4 * n)
            if n1 == 0:
                write(n1, rows, re)
            else:
                write(n1, rows, re * math.cos(turn) - im * math.sin(turn))


def flat(x):
    return x.reshape(x.shape[0] * x.shape[1], x.shape[2])


def start_all(copies):
    for copy in copies:
        copy.start()


def wait_all(copies):
    for copy in copies:
        copy.wait()


def parts_of(size):
    step = max(1, size // PARTS)
    return [pl.ds(k, step) for k in range(0, size, step)]


def plane(width):
    return lax.axis_index("context") // width


def filter_kernel(n, channels, tokens, f_ref, tw_ref, fwd_ref, out_ref, y_ref):
    outer_forward(
        lambda n1, rows: f_ref[rows, n1 * tokens : (n1 + 1) * tokens],
        n, channels, tokens, tw_ref, y_ref,
    )
    for ms in parts_of(n):
        out_ref[ms] = times_table(flat(y_ref[ms]), fwd_ref).reshape(ms.size, channels, 2 * tokens)


def conv_middle(sign, n, channels, tokens, fwd_ref, inv_ref, spec_ref, own_ref, y_ref):
    for ms in parts_of(n):
        own = times_table(flat(y_ref[ms]), fwd_ref)
        own_ref[ms] = own.reshape(ms.size, channels, 2 * tokens)
        spec = flat(spec_ref[ms])
        re, im = own[:, :tokens], own[:, tokens:]
        s_re, s_im = spec[:, :tokens], spec[:, tokens:] * sign
        both = jnp.concatenate([re * s_re - im * s_im, re * s_im + im * s_re], axis=1)
        y_ref[ms] = times_table(both, inv_ref).reshape(ms.size, channels, 2 * tokens)


def conv_kernel(planes, n, channels, tokens, x_ref, *refs):
    tw_ref, fwd_ref, inv_ref, spec_ref, after_ref = refs[:5]
    out_refs, (own_ref, buf_ref, y_ref) = refs[5 : planes + 5], refs[planes + 5 :]
    width = n // planes
    z = plane(width)
    outer_forward(
        lambda n1, rows: x_ref[n1 % width, z ^ (n1 // width), rows],
        n, channels, tokens, tw_ref, y_ref,
    )
    conv_middle(1.0, n, channels, tokens, fwd_ref, inv_ref, spec_ref, own_ref, y_ref)

    def write(n1, rows, value):
        buf_ref[n1, rows] = value

    outer_inverse(write, n, channels, tokens, tw_ref, y_ref)
    for d in range(planes):
        out_refs[d][...] = buf_ref[pl.ds((z ^ d) * width, width)]


def back_kernel(planes, n, channels, tokens, near_ref, *refs):
    far_refs, refs = refs[: planes - 1], refs[planes - 1 :]
    (
        tw_ref, fwd_ref, inv_ref, spec_ref, after_ref, out_ref, own_ref, buf_ref, y_ref, sem
    ) = refs
    width = n // planes
    z = plane(width)
    for q in range(width):
        buf_ref[q, z] = near_ref[q, z]
        for d in range(1, planes):
            buf_ref[q, z ^ d] = far_refs[d - 1][q]
    outer_forward(
        lambda n1, rows: buf_ref[n1 % width, n1 // width, rows],
        n, channels, tokens, tw_ref, y_ref,
    )
    conv_middle(-1.0, n, channels, tokens, fwd_ref, inv_ref, spec_ref, own_ref, y_ref)

    def write(n1, rows, value):
        buf_ref[n1 % width, n1 // width, rows] = value

    outer_inverse(write, n, channels, tokens, tw_ref, y_ref)
    stores = [
        pltpu.make_async_copy(buf_ref.at[part], out_ref.at[part], sem.at[i])
        for i, part in enumerate(parts_of(width))
    ]
    start_all(stores)
    wait_all(stores)


def filter_grad_kernel(scale, n, channels, tokens, tw_ref, inv_ref, p_ref, g_ref, out_ref, y_ref):
    for ms in parts_of(n):
        p, g = flat(p_ref[ms]), flat(g_ref[ms])
        p_re, p_im = p[:, :tokens], p[:, tokens:]
        re, im = g[:, :tokens], g[:, tokens:]
        both = jnp.concatenate([re * p_re + im * p_im, im * p_re - re * p_im], axis=1)
        y_ref[ms] = times_table(both, inv_ref).reshape(ms.size, channels, 2 * tokens)

    def write(n1, rows, value):
        out_ref[rows, n1 * tokens : (n1 + 1) * tokens] = value * scale

    outer_inverse(write, n, channels, tokens, tw_ref, y_ref)


def load_pairs(n, a_ref, b_ref, a_buf, b_buf, sem):
    loads = []
    for i, part in enumerate(parts_of(n)):
        loads.append(
            [
                pltpu.make_async_copy(a_ref.at[part], a_buf.at[part], sem.at[0, i]),
                pltpu.make_async_copy(b_ref.at[part], b_buf.at[part], sem.at[1, i]),
            ]
        )
        start_all(loads[-1])
    return loads


def product_split_kernel(planes, n, a_ref, b_ref, *refs):
    out_refs, (a_buf, b_buf, sem) = refs[:planes], refs[planes:]
    width = n // planes
    z = plane(width)
    for load in load_pairs(n, a_ref, b_ref, a_buf, b_buf, sem):
        wait_all(load)
    for d in range(planes):
        for q in range(width):
            out_refs[d][q] = a_buf[(z ^ d) * width + q] * b_buf[(z ^ d) * width + q]


def product_kernel(planes, n, a_ref, b_ref, after_ref, out_ref, a_buf, b_buf, buf_ref, sem):
    width = n // planes
    for load in load_pairs(n, a_ref, b_ref, a_buf, b_buf, sem):
        wait_all(load)
    stores = [
        pltpu.make_async_copy(buf_ref.at[part], out_ref.at[part], sem.at[2, i])
        for i, part in enumerate(parts_of(width))
    ]
    for part, store in zip(parts_of(width), stores):
        for z in range(planes):
            rows = pl.ds(part.start + z * width, part.size)
            buf_ref[part, z] = a_buf[rows] * b_buf[rows]
        store.start()
    wait_all(stores)


def send_kernel(planes, width, x_ref, *out_refs):
    for d in range(1, planes):
        out_refs[d - 1][...] = x_ref[:, plane(width) ^ d]


def merge_kernel(planes, width, *refs):
    in_refs, (after_ref, out_ref, sem) = refs[:planes], refs[planes:]
    stores = [
        pltpu.make_async_copy(ref.at[part], out_ref.at[part, d], sem.at[d, i])
        for d, ref in enumerate(in_refs)
        for i, part in enumerate(parts_of(width))
    ]
    start_all(stores)
    wait_all(stores)


def gate_parts(width, blocks, a_ref, b_ref, outs, bufs, sem):
    stores = []
    for d, (read, first) in enumerate(blocks):
        part = pl.ds(first, width)
        x = read()
        for j, (ref, buf, out) in enumerate(zip((a_ref, b_ref), bufs, outs)):
            buf[part] = x * ref[part]
            stores.append(pltpu.make_async_copy(buf.at[part], out.at[part], sem.at[j, d]))
            stores[-1].start()
    wait_all(stores)


def gate_kernel(planes, width, x_ref, a_ref, b_ref, oa_ref, ob_ref, a_buf, b_buf, sem):
    z = plane(width)
    blocks = [(lambda d=d: x_ref[:, d], (z ^ d) * width) for d in range(planes)]
    gate_parts(width, blocks, a_ref, b_ref, (oa_ref, ob_ref), (a_buf, b_buf), sem)


def gate_split_kernel(planes, width, near_ref, *refs):
    far_refs, refs = refs[: planes - 1], refs[planes - 1 :]
    a_ref, b_ref, oa_ref, ob_ref, a_buf, b_buf, sem = refs
    z = plane(width)
    blocks = [(lambda: near_ref[:, z], z * width)]
    for d in range(1, planes):
        blocks.append((lambda d=d: far_refs[d - 1][...], (z ^ d) * width))
    gate_parts(width, blocks, a_ref, b_ref, (oa_ref, ob_ref), (a_buf, b_buf), sem)


SPACES = {"v": pltpu.VMEM, "h": pltpu.HBM, "a": pl.ANY}


def kernel_call(body, ins, outs, scratch, flops=0):
    shapes = [SPACES[space](shape, jnp.float32) for space, shape in outs]

    def run(*args):
        args = [
            pltpu.with_memory_space_constraint(x, pltpu.HBM) if space == "h" else x
            for space, x in zip(ins, args, strict=True)
        ]
        size = sum(math.prod(x.shape) for x in (*args, *shapes))
        return pl.pallas_call(
            body,
            in_specs=[pl.BlockSpec(memory_space=SPACES[space]) for space in ins],
            out_specs=[pl.BlockSpec(memory_space=SPACES[space]) for space, _ in outs],
            out_shape=shapes,
            scratch_shapes=scratch,
            compiler_params=pltpu.CompilerParams(vmem_limit_bytes=VMEM_BYTES),
            cost_estimate=pl.CostEstimate(flops=flops, bytes_accessed=4 * size, transcendentals=0),
        )(*args)

    return run


def tables(n, tokens):
    length = n * tokens
    m = np.arange(n)[:, None] + 0.25
    angle = 2 * np.pi * m * np.arange(tokens)[None, :] / length
    tw = np.stack([np.cos(angle), np.sin(angle)])[:, :, None, :]
    tw = np.broadcast_to(tw, (2, n, ROWS, tokens)).astype(np.float32)
    k = np.arange(tokens)
    inner = 2 * np.pi * ((k[:, None] * k[None, :]) % tokens) / tokens
    c, s = np.cos(inner), np.sin(inner)

    def pair(table):
        hi = table.astype(ml_dtypes.bfloat16)
        lo = (table - hi.astype(np.float64)).astype(ml_dtypes.bfloat16)
        return jnp.asarray(np.stack([hi, lo]))

    fwd = pair(np.block([[c, -s], [s, c]]))
    inv = pair(np.block([[c, s], [-s, c]]) / length)
    return jnp.asarray(tw), fwd, inv


def on_device(query_input, key_input, value_input, filters, cotangent):
    n = lax.axis_size("context")
    pair_size = lax.axis_size("dp")
    _, width, tokens = query_input.shape
    channels, length = filters.shape
    scale = 1.0 / math.sqrt(pair_size * length)
    sizes = (n, channels, tokens)
    tw, fwd, inv = tables(n, tokens)
    planes = math.gcd(n, PLANES)
    width = n // planes
    blocks, spectrum = (n, channels, tokens), (n, channels, 2 * tokens)
    one, paired, lags = (width, channels, tokens), (width, planes, channels, tokens), (channels, length)
    flops = 4 * 2 * 2 * tokens * n * channels * tokens
    f32 = jnp.float32
    y = pltpu.VMEM(spectrum, f32)

    def semaphores(*shape):
        return pltpu.SemaphoreType.DMA(shape)

    def part(body, *args):
        return lambda *refs: body(*args, *refs)

    def along_z(xs):
        return [
            lax.ppermute(x, "context", [(i, i ^ (d * width)) for i in range(n)])
            for d, x in enumerate(xs, 1)
        ]

    def within_plane(x):
        members = [[z * width + q for q in range(width)] for z in range(planes)]
        return lax.all_to_all(x, "context", 0, 0, axis_index_groups=members, tiled=True)

    query, key, value, cot = (
        x.reshape(blocks) for x in (query_input, key_input, value_input, cotangent)
    )
    bufs = [pltpu.VMEM(blocks, f32)] * 2
    send = kernel_call(part(send_kernel, planes, width), "v", [("v", one)] * (planes - 1), [])
    merge = kernel_call(
        part(merge_kernel, planes, width), "a" * (planes + 1), [("h", paired)],
        [semaphores(planes, PARTS)],
    )

    keep_p, *send_p = kernel_call(
        part(product_split_kernel, planes, n), "hh", [("v", one)] * planes,
        [*bufs, semaphores(2, PARTS)],
    )(key, value)
    got_p = along_z(send_p)
    (conv_grad,) = kernel_call(
        part(product_kernel, planes, n), "hha", [("h", paired)],
        [*bufs, pltpu.VMEM(paired, f32), semaphores(3, PARTS)],
    )(cot, query, keep_p)
    near_g = within_plane(conv_grad)
    send_g = send(near_g)
    far_g = along_z(send_g)
    (filt,) = kernel_call(
        part(filter_kernel, *sizes), "vvv", [("v", spectrum)], [y], flops
    )(filters, tw, fwd)
    product_ch = within_plane(*merge(keep_p, *got_p, send_g[0]))
    keep_c, *send_c, prod_spec = kernel_call(
        part(conv_kernel, planes, *sizes), "vvvvva", [("v", one)] * planes + [("v", spectrum)],
        [pltpu.VMEM(blocks, f32), y], 2 * flops,
    )(product_ch, tw, fwd, inv, filt, send_g[0])
    got_c = along_z(send_c)
    back_ch, grad_spec = kernel_call(
        part(back_kernel, planes, *sizes), "v" * (planes + 4) + "a",
        [("h", paired), ("v", spectrum)],
        [pltpu.VMEM(paired, f32), y, semaphores(PARTS)], 2 * flops,
    )(near_g, *far_g, tw, fwd, inv, filt, keep_c)
    near_b = within_plane(back_ch)
    send_b = send(near_b)
    far_b = along_z(send_b)
    conv_tok = within_plane(*merge(keep_c, *got_c, send_b[0]))
    (own,) = kernel_call(
        part(filter_grad_kernel, scale, *sizes), "vvvv", [("v", lags)], [y], flops
    )(tw, inv, prod_spec, grad_spec)
    if pair_size == 2:
        grad_filter = own + lax.ppermute(own, "dp", [(0, 1), (1, 0)])
    else:
        grad_filter = lax.psum(own, "dp")
    gate_scratch = [*bufs, semaphores(2, planes)]
    gated, grad_query = kernel_call(
        part(gate_kernel, planes, width), "vvv", [("h", blocks)] * 2, gate_scratch
    )(conv_tok, query, cot)
    grad_key, grad_value = kernel_call(
        part(gate_split_kernel, planes, width), "v" * (planes + 2), [("h", blocks)] * 2, gate_scratch
    )(near_b, *far_b, value, key)
    shape = query_input.shape
    return (
        gated.reshape(shape),
        grad_query.reshape(shape),
        grad_key.reshape(shape),
        grad_value.reshape(shape),
        grad_filter,
    )


def solution(mesh):
    in_specs = (
        P("dp", None, "context"),
        P("dp", None, "context"),
        P("dp", None, "context"),
        P("context", None),
        P("dp", None, "context"),
    )
    out_specs = (
        P("dp", None, "context"),
        P("dp", None, "context"),
        P("dp", None, "context"),
        P("dp", None, "context"),
        P("context", None),
    )
    return jax.shard_map(
        on_device, mesh=mesh, in_specs=in_specs, out_specs=out_specs, check_vma=False
    )
```

```python
import math

import jax
import jax.numpy as jnp
import ml_dtypes
import numpy as np
from jax import lax
from jax.experimental import pallas as pl
from jax.experimental.pallas import tpu as pltpu
from jax.sharding import PartitionSpec as P

ROWS = 8
PLANES = 4
PARTS = 4
VMEM_BYTES = 24 * 1024 * 1024


def twist(value, turn):
    re, im = value
    turn = turn % 1.0
    if turn == 0.0:
        return re, im
    if turn == 0.25:
        return im, -re
    if turn == 0.5:
        return -re, -im
    if turn == 0.75:
        return -im, re
    if turn in (0.125, 0.375, 0.625, 0.875):
        half = math.sqrt(0.5)
        a, b = (re + im) * half, (im - re) * half
        return twist((a, b), turn - 0.125)
    c, s = math.cos(2 * math.pi * turn), math.sin(2 * math.pi * turn)
    return re * c + im * s, im * c - re * s


def dft(values, sign):
    n = len(values)
    if n == 1:
        return values
    even, odd = dft(values[0::2], sign), dft(values[1::2], sign)
    out = [None] * n
    for k in range(n // 2):
        a, b = even[k], twist(odd[k], sign * k / n)
        out[k] = (a[0] + b[0], a[1] + b[1])
        out[k + n // 2] = (a[0] - b[0], a[1] - b[1])
    return out


def split(x):
    hi = x.astype(jnp.bfloat16)
    lo = (x - hi.astype(jnp.float32)).astype(jnp.bfloat16)
    return hi, lo


def times_table(x, table_ref):
    hi, lo = split(x)
    out = jnp.dot(hi, table_ref[0], preferred_element_type=jnp.float32)
    out += jnp.dot(lo, table_ref[0], preferred_element_type=jnp.float32)
    out += jnp.dot(hi, table_ref[1], preferred_element_type=jnp.float32)
    return out


def outer_forward(read, n, part, tokens, tw_ref, y_ref):
    @pl.loop(part.start // ROWS, (part.start + part.size) // ROWS)
    def _(r):
        rows = pl.ds(pl.multiple_of(r * ROWS, ROWS), ROWS)
        values = []
        for n1 in range(n):
            x = read(n1, rows)
            turn = 2 * math.pi * n1 / (4 * n)
            if n1 == 0:
                values.append((x, jnp.zeros_like(x)))
            else:
                values.append((x * math.cos(turn), x * -math.sin(turn)))
        for m, (re, im) in enumerate(dft(values, 1)):
            c, s = tw_ref[0, m], tw_ref[1, m]
            y_ref[m, rows, :tokens] = re * c + im * s
            y_ref[m, rows, tokens:] = im * c - re * s


def outer_inverse(write, n, part, tokens, tw_ref, y_ref):
    @pl.loop(part.start // ROWS, (part.start + part.size) // ROWS)
    def _(r):
        rows = pl.ds(pl.multiple_of(r * ROWS, ROWS), ROWS)
        values = []
        for m in range(n):
            re, im = y_ref[m, rows, :tokens], y_ref[m, rows, tokens:]
            c, s = tw_ref[0, m], tw_ref[1, m]
            values.append((re * c - im * s, im * c + re * s))
        for n1, (re, im) in enumerate(dft(values, -1)):
            turn = 2 * math.pi * n1 / (4 * n)
            if n1 == 0:
                write(n1, rows, re)
            else:
                write(n1, rows, re * math.cos(turn) - im * math.sin(turn))


def flat(x):
    return x.reshape(x.shape[0] * x.shape[1], x.shape[2])


def start_all(copies):
    for copy in copies:
        copy.start()


def wait_all(copies):
    for copy in copies:
        copy.wait()


def parts_of(size, least=1):
    step = max(least, size // PARTS)
    return [pl.ds(k, step) for k in range(0, size, step)]


def plane(width):
    return lax.axis_index("context") // width


def copies_of(pairs, sem):
    return [pltpu.make_async_copy(src, dst, sem.at[i]) for i, (src, dst) in enumerate(pairs)]


def filter_kernel(
    first, n, channels, tokens, f_ref, tw_ref, fwd_ref, out_ref, f_buf, y_ref, own_ref, sem
):
    rows = parts_of(channels, ROWS)
    loads = copies_of(
        [(f_ref.at[pl.ds(first + part.start, part.size)], f_buf.at[part]) for part in rows],
        sem.at[0],
    )
    start_all(loads)
    for part, load in zip(rows, loads):
        load.wait()
        outer_forward(
            lambda n1, r: f_buf[r, n1 * tokens : (n1 + 1) * tokens], n, part, tokens, tw_ref, y_ref
        )
    stores = copies_of([(own_ref.at[ms], out_ref.at[ms]) for ms in parts_of(n)], sem.at[1])
    for ms, store in zip(parts_of(n), stores):
        own_ref[ms] = times_table(flat(y_ref[ms]), fwd_ref).reshape(ms.size, channels, 2 * tokens)
        store.start()
    wait_all(stores)


def transform(
    sign, n, channels, tokens, sources, targets, tw_ref, fwd_ref, inv_ref, spec_refs, own_ref,
    buf_ref, spec_buf, own_buf, y_ref, sem,
):
    rows = parts_of(channels, ROWS)
    loads = [copies_of(sources(part), sem.at[0, i]) for i, part in enumerate(rows)]
    for load in loads:
        start_all(load)
    half = channels // 2
    spec_loads = [
        copies_of(
            [
                (ref.at[ms], spec_buf.at[ms, pl.ds(j * half, half)])
                for j, ref in enumerate(spec_refs)
            ],
            sem.at[1, i],
        )
        for i, ms in enumerate(parts_of(n))
    ]
    for load in spec_loads:
        start_all(load)
    for part, load in zip(rows, loads):
        wait_all(load)
        outer_forward(lambda n1, r: buf_ref[n1, r], n, part, tokens, tw_ref, y_ref)
    own_stores = copies_of([(own_buf.at[ms], own_ref.at[ms]) for ms in parts_of(n)], sem.at[2, 0])
    for ms, load, store in zip(parts_of(n), spec_loads, own_stores):
        own = times_table(flat(y_ref[ms]), fwd_ref)
        own_buf[ms] = own.reshape(ms.size, channels, 2 * tokens)
        store.start()
        wait_all(load)
        spec = flat(spec_buf[ms])
        re, im = own[:, :tokens], own[:, tokens:]
        s_re, s_im = spec[:, :tokens], spec[:, tokens:] * sign
        both = jnp.concatenate([re * s_re - im * s_im, re * s_im + im * s_re], axis=1)
        y_ref[ms] = times_table(both, inv_ref).reshape(ms.size, channels, 2 * tokens)

    def write(n1, r, value):
        buf_ref[n1, r] = value

    stores = [copies_of(targets(part), sem.at[3, i]) for i, part in enumerate(rows)]
    for part, store in zip(rows, stores):
        outer_inverse(write, n, part, tokens, tw_ref, y_ref)
        start_all(store)
    for store in (*stores, own_stores):
        wait_all(store)


def conv_kernel(planes, n, channels, tokens, x_ref, *refs):
    tables, spec_refs, refs = refs[:3], refs[3:5], refs[5:]
    out_refs, (own_ref, buf_ref, *scratch) = refs[:planes], refs[planes:]
    width = n // planes
    z = plane(width)

    def block(d, part):
        return buf_ref.at[pl.ds((z ^ d) * width, width), part]

    def sources(part):
        return [(x_ref.at[:, d, part], block(d, part)) for d in range(planes)]

    def targets(part):
        return [(block(d, part), out_refs[d].at[:, part]) for d in range(planes)]

    transform(
        1.0, n, channels, tokens, sources, targets, *tables, spec_refs, own_ref, buf_ref, *scratch
    )


def back_kernel(planes, n, channels, tokens, near_ref, *refs):
    far_refs, refs = refs[: planes - 1], refs[planes - 1 :]
    tables, spec_refs, refs = refs[:3], refs[3:5], refs[5:]
    after_ref, out_ref, own_ref, buf_ref, *scratch = refs
    width = n // planes
    z = plane(width)

    def block(z, part):
        return buf_ref.at[pl.ds(z * width, width), part]

    def sources(part):
        near = [(near_ref.at[:, z, part], block(z, part))]
        return near + [
            (ref.at[:, part], block(z ^ d, part)) for d, ref in enumerate(far_refs, 1)
        ]

    def targets(part):
        return [(block(z, part), out_ref.at[:, z, part]) for z in range(planes)]

    transform(
        -1.0, n, channels, tokens, sources, targets, *tables, spec_refs, own_ref, buf_ref, *scratch
    )


def filter_grad_kernel(
    scale, n, channels, tokens, tw_ref, inv_ref, p_ref, g_ref, out_ref, p_buf, g_buf, y_ref, sem
):
    loads = [
        copies_of([(p_ref.at[ms], p_buf.at[ms]), (g_ref.at[ms], g_buf.at[ms])], sem.at[i])
        for i, ms in enumerate(parts_of(n))
    ]
    for load in loads:
        start_all(load)
    for ms, load in zip(parts_of(n), loads):
        wait_all(load)
        p, g = flat(p_buf[ms]), flat(g_buf[ms])
        p_re, p_im = p[:, :tokens], p[:, tokens:]
        re, im = g[:, :tokens], g[:, tokens:]
        both = jnp.concatenate([re * p_re + im * p_im, im * p_re - re * p_im], axis=1)
        y_ref[ms] = times_table(both, inv_ref).reshape(ms.size, channels, 2 * tokens)

    def write(n1, r, value):
        out_ref[r, n1 * tokens : (n1 + 1) * tokens] = value * scale

    outer_inverse(write, n, pl.ds(0, channels), tokens, tw_ref, y_ref)


def load_pairs(n, a_ref, b_ref, a_buf, b_buf, sem):
    loads = [
        copies_of([(a_ref.at[part], a_buf.at[part]), (b_ref.at[part], b_buf.at[part])], sem.at[i])
        for i, part in enumerate(parts_of(n))
    ]
    for load in loads:
        start_all(load)
    return loads


def product_split_kernel(planes, n, a_ref, b_ref, *refs):
    out_refs, (a_buf, b_buf, sem) = refs[:planes], refs[planes:]
    width = n // planes
    z = plane(width)
    for load in load_pairs(n, a_ref, b_ref, a_buf, b_buf, sem):
        wait_all(load)
    for d in range(planes):
        for q in range(width):
            out_refs[d][q] = a_buf[(z ^ d) * width + q] * b_buf[(z ^ d) * width + q]


def product_kernel(planes, n, a_ref, b_ref, after_ref, out_ref, a_buf, b_buf, buf_ref, sem):
    width = n // planes
    parts = [pl.ds(z * width, width) for z in range(planes)]
    loads = [
        copies_of([(a_ref.at[part], a_buf.at[part]), (b_ref.at[part], b_buf.at[part])], sem.at[z])
        for z, part in enumerate(parts)
    ]
    for load in loads:
        start_all(load)
    stores = copies_of([(buf_ref.at[z], out_ref.at[:, z]) for z in range(planes)], sem.at[planes])
    for z, part in enumerate(parts):
        wait_all(loads[z])
        buf_ref[z] = a_buf[part] * b_buf[part]
        stores[z].start()
    wait_all(stores)


def send_kernel(planes, width, x_ref, *refs):
    out_refs, (buf_ref, sem) = refs[: planes - 1], refs[planes - 1 :]
    z = plane(width)
    parts = parts_of(width)
    loads = [
        copies_of([(x_ref.at[part, z ^ d], buf_ref.at[d, part]) for part in parts], sem.at[d])
        for d in range(1, planes)
    ]
    for load in loads:
        start_all(load)
    stores = copies_of([(buf_ref.at[d + 1], ref) for d, ref in enumerate(out_refs)], sem.at[0])
    for load, store in zip(loads, stores):
        wait_all(load)
        store.start()
    wait_all(stores)


def merge_kernel(planes, width, *refs):
    in_refs, (after_ref, out_ref, buf_ref, sem) = refs[:planes], refs[planes:]
    parts = parts_of(width)
    loads = [
        copies_of([(ref.at[part], buf_ref.at[part, d]) for d, ref in enumerate(in_refs)], sem.at[i])
        for i, part in enumerate(parts)
    ]
    for load in loads:
        start_all(load)
    stores = copies_of([(buf_ref.at[part], out_ref.at[part]) for part in parts], sem.at[len(parts)])
    for load, store in zip(loads, stores):
        wait_all(load)
        store.start()
    wait_all(stores)


def gate_parts(width, blocks, a_ref, b_ref, outs, a_buf, b_buf, sem):
    stores = []
    for d, (read, first) in enumerate(blocks):
        part = pl.ds(first, width)
        x = read()
        a_buf[part] = x * a_ref[part]
        b_buf[part] = x * b_ref[part]
        pairs = [(buf.at[part], out.at[part]) for buf, out in zip((a_buf, b_buf), outs)]
        stores.extend(copies_of(pairs, sem.at[d]))
        start_all(stores[-2:])
    wait_all(stores)


def gate_kernel(
    planes, width, x_ref, a_ref, b_ref, oa_ref, ob_ref, x_buf, a_in, b_in, a_buf, b_buf, sem
):
    z = plane(width)
    loads = []
    for d in range(planes):
        part = pl.ds((z ^ d) * width, width)
        pairs = [
            (x_ref.at[:, d], x_buf.at[d]),
            (a_ref.at[part], a_in.at[part]),
            (b_ref.at[part], b_in.at[part]),
        ]
        loads.append(copies_of(pairs, sem.at[planes + d]))
        start_all(loads[-1])

    def read(d):
        wait_all(loads[d])
        return x_buf[d]

    blocks = [(lambda d=d: read(d), (z ^ d) * width) for d in range(planes)]
    gate_parts(width, blocks, a_in, b_in, (oa_ref, ob_ref), a_buf, b_buf, sem)


def gate_split_kernel(planes, width, *refs):
    far_refs, refs = refs[: planes - 1], refs[planes - 1 :]
    a_ref, b_ref, near_ref, oa_ref, ob_ref, x_buf, a_buf, b_buf, sem = refs
    z = plane(width)
    load = pltpu.make_async_copy(near_ref.at[:, z], x_buf, sem.at[planes, 0])
    load.start()

    def read():
        load.wait()
        return x_buf[...]

    blocks = [(lambda d=d: far_refs[d - 1][...], (z ^ d) * width) for d in range(1, planes)]
    blocks.append((read, z * width))
    gate_parts(width, blocks, a_ref, b_ref, (oa_ref, ob_ref), a_buf, b_buf, sem)


SPACES = {"v": pltpu.VMEM, "u": pltpu.VMEM, "h": pltpu.HBM, "a": pl.ANY}


def kernel_call(body, ins, outs, scratch, flops=0):
    shapes = [
        jax.ShapeDtypeStruct(shape, jnp.float32) if space == "u" else SPACES[space](shape, jnp.float32)
        for space, shape in outs
    ]

    def run(*args):
        args = [
            pltpu.with_memory_space_constraint(x, pltpu.HBM) if space == "h" else x
            for space, x in zip(ins, args, strict=True)
        ]
        size = sum(math.prod(x.shape) for x in (*args, *shapes))
        return pl.pallas_call(
            body,
            in_specs=[pl.BlockSpec(memory_space=SPACES[space]) for space in ins],
            out_specs=[pl.BlockSpec(memory_space=SPACES[space]) for space, _ in outs],
            out_shape=shapes,
            scratch_shapes=scratch,
            compiler_params=pltpu.CompilerParams(vmem_limit_bytes=VMEM_BYTES),
            cost_estimate=pl.CostEstimate(flops=flops, bytes_accessed=4 * size, transcendentals=0),
        )(*args)

    return run


def tables(n, tokens):
    length = n * tokens
    m = np.arange(n)[:, None] + 0.25
    angle = 2 * np.pi * m * np.arange(tokens)[None, :] / length
    tw = np.stack([np.cos(angle), np.sin(angle)])[:, :, None, :]
    tw = np.broadcast_to(tw, (2, n, ROWS, tokens)).astype(np.float32)
    k = np.arange(tokens)
    inner = 2 * np.pi * ((k[:, None] * k[None, :]) % tokens) / tokens
    c, s = np.cos(inner), np.sin(inner)

    def pair(table):
        hi = table.astype(ml_dtypes.bfloat16)
        lo = (table - hi.astype(np.float64)).astype(ml_dtypes.bfloat16)
        return jnp.asarray(np.stack([hi, lo]))

    fwd = pair(np.block([[c, -s], [s, c]]))
    inv = pair(np.block([[c, s], [-s, c]]) / length)
    return jnp.asarray(tw), fwd, inv


def on_device(query_input, key_input, value_input, filters, cotangent):
    n = lax.axis_size("context")
    pair_size = lax.axis_size("dp")
    _, width, tokens = query_input.shape
    channels, length = filters.shape
    scale = 1.0 / math.sqrt(pair_size * length)
    sizes = (n, channels, tokens)
    tw, fwd, inv = tables(n, tokens)
    planes = math.gcd(n, PLANES)
    width = n // planes
    blocks, spectrum = (n, channels, tokens), (n, channels, 2 * tokens)
    one, paired, lags = (width, channels, tokens), (width, planes, channels, tokens), (channels, length)
    flops = 4 * 2 * 2 * tokens * n * channels * tokens
    f32 = jnp.float32
    y = pltpu.VMEM(spectrum, f32)

    def semaphores(*shape):
        return pltpu.SemaphoreType.DMA(shape)

    def part(body, *args):
        return lambda *refs: body(*args, *refs)

    def along_z(xs):
        return [
            lax.ppermute(x, "context", [(i, i ^ (d * width)) for i in range(n)])
            for d, x in enumerate(xs, 1)
        ]

    def within_plane(x):
        members = [[z * width + q for q in range(width)] for z in range(planes)]
        return lax.all_to_all(x, "context", 0, 0, axis_index_groups=members, tiled=True)

    query, key, value, cot = (
        x.reshape(blocks) for x in (query_input, key_input, value_input, cotangent)
    )
    rows, paired_buf = pltpu.VMEM(blocks, f32), pltpu.VMEM(paired, f32)
    by_plane = pltpu.VMEM((planes, *one), f32)
    outs = [("h", one)] * (planes - 1)
    send = kernel_call(
        part(send_kernel, planes, width), "h", outs, [by_plane, semaphores(planes, planes + PARTS)]
    )
    merge = kernel_call(
        part(merge_kernel, planes, width), "h" * planes + "a", [("h", paired)],
        [paired_buf, semaphores(PARTS + 1, planes + PARTS)],
    )
    half_sizes = (n, channels // 2, tokens)
    half_spectrum = (n, channels // 2, 2 * tokens)

    def transform_filters(first):
        return kernel_call(
            part(filter_kernel, first, *half_sizes), "hvv", [("h", half_spectrum)],
            [
                pltpu.VMEM((channels // 2, length), f32),
                *[pltpu.VMEM(half_spectrum, f32)] * 2,
                semaphores(2, PARTS),
            ],
            flops // 2,
        )(filters, tw, fwd)[0]

    transform_scratch = [rows, y, y, y, semaphores(4, PARTS, max(PARTS, planes))]
    always = lax.axis_index("context") < n

    def grouped(body, *args):
        shapes = jax.eval_shape(body, *args)

        def never(*args):
            return jax.tree.map(lambda x: jnp.zeros(x.shape, x.dtype), shapes)

        return lax.cond(always, body, never, *args)

    keep_p, *send_p = kernel_call(
        part(product_split_kernel, planes, n), "hh", [("u", one)] * planes,
        [rows, rows, semaphores(PARTS, 2)],
    )(key, value)
    got_p = along_z(send_p)

    def first(cot, query, keep_p):
        (conv_grad,) = kernel_call(
            part(product_kernel, planes, n), "hha", [("h", paired)],
            [rows, rows, by_plane, semaphores(planes + 1, planes)],
        )(cot, query, keep_p)
        near_g = within_plane(conv_grad)
        return near_g, send(near_g), transform_filters(0)

    near_g, send_g, filt_a = grouped(first, cot, query, keep_p)
    far_g = along_z(send_g)

    def second(keep_p, got_p, send_g, filt_a):
        product_ch = within_plane(*merge(keep_p, *got_p, send_g))
        filt = (filt_a, transform_filters(channels // 2))
        *outs, prod_spec = kernel_call(
            part(conv_kernel, planes, *sizes), "hvvvhh",
            [("h", one)] * planes + [("h", spectrum)], transform_scratch, 2 * flops,
        )(product_ch, tw, fwd, inv, *filt)
        return outs, prod_spec, filt

    (keep_c, *send_c), prod_spec, filt = grouped(second, keep_p, got_p, send_g[0], filt_a)
    got_c = along_z(send_c)

    def third(near_g, far_g, filt, keep_c, prod_spec):
        back_ch, grad_spec = kernel_call(
            part(back_kernel, planes, *sizes), "h" * planes + "vvvhha",
            [("h", paired), ("h", spectrum)], transform_scratch, 2 * flops,
        )(near_g, *far_g, tw, fwd, inv, *filt, keep_c)
        near_b = within_plane(back_ch)
        (own,) = kernel_call(
            part(filter_grad_kernel, scale, *sizes), "vvhh", [("u", lags)],
            [y, y, y, semaphores(PARTS, 2)], flops,
        )(tw, inv, prod_spec, grad_spec)
        return near_b, send(near_b), own

    near_b, send_b, own = grouped(third, near_g, far_g, filt, keep_c, prod_spec)
    far_b = along_z(send_b)

    def fourth(keep_c, got_c, send_b, query, cot, own):
        conv_tok = within_plane(*merge(keep_c, *got_c, send_b))
        if pair_size == 2:
            grad_filter = own + lax.ppermute(own, "dp", [(0, 1), (1, 0)])
        else:
            grad_filter = lax.psum(own, "dp")
        gated, grad_query = kernel_call(
            part(gate_kernel, planes, width), "hhh", [("h", blocks)] * 2,
            [by_plane, *[rows] * 4, semaphores(2 * planes, 3)],
        )(conv_tok, query, cot)
        return gated, grad_query, grad_filter

    gated, grad_query, grad_filter = grouped(
        fourth, keep_c, got_c, send_b[0], query, cot, own
    )
    grad_key, grad_value = kernel_call(
        part(gate_split_kernel, planes, width), "v" * (planes + 1) + "h", [("h", blocks)] * 2,
        [pltpu.VMEM(one, f32), rows, rows, semaphores(planes + 1, 2)],
    )(*far_b, value, key, near_b)
    shape = query_input.shape
    return (
        gated.reshape(shape),
        grad_query.reshape(shape),
        grad_key.reshape(shape),
        grad_value.reshape(shape),
        grad_filter,
    )


def solution(mesh):
    in_specs = (
        P("dp", None, "context"),
        P("dp", None, "context"),
        P("dp", None, "context"),
        P("context", None),
        P("dp", None, "context"),
    )
    out_specs = (
        P("dp", None, "context"),
        P("dp", None, "context"),
        P("dp", None, "context"),
        P("dp", None, "context"),
        P("context", None),
    )
    return jax.shard_map(
        on_device, mesh=mesh, in_specs=in_specs, out_specs=out_specs, check_vma=False
    )
```

```python
import math

import jax
import jax.numpy as jnp
import ml_dtypes
import numpy as np
from jax import lax
from jax.experimental import pallas as pl
from jax.experimental.pallas import tpu as pltpu
from jax.sharding import PartitionSpec as P

ROWS = 8
PLANES = 4
PARTS = 4
VMEM_BYTES = 24 * 1024 * 1024


def twist(value, turn):
    re, im = value
    turn = turn % 1.0
    if turn == 0.0:
        return re, im
    if turn == 0.25:
        return im, -re
    if turn == 0.5:
        return -re, -im
    if turn == 0.75:
        return -im, re
    if turn in (0.125, 0.375, 0.625, 0.875):
        half = math.sqrt(0.5)
        a, b = (re + im) * half, (im - re) * half
        return twist((a, b), turn - 0.125)
    c, s = math.cos(2 * math.pi * turn), math.sin(2 * math.pi * turn)
    return re * c + im * s, im * c - re * s


def dft(values, sign):
    n = len(values)
    if n == 1:
        return values
    even, odd = dft(values[0::2], sign), dft(values[1::2], sign)
    out = [None] * n
    for k in range(n // 2):
        a, b = even[k], twist(odd[k], sign * k / n)
        out[k] = (a[0] + b[0], a[1] + b[1])
        out[k + n // 2] = (a[0] - b[0], a[1] - b[1])
    return out


def split(x):
    hi = x.astype(jnp.bfloat16)
    lo = (x - hi.astype(jnp.float32)).astype(jnp.bfloat16)
    return hi, lo


def times_table(x, table_ref):
    hi, lo = split(x)
    out = jnp.dot(hi, table_ref[0], preferred_element_type=jnp.float32)
    out += jnp.dot(lo, table_ref[0], preferred_element_type=jnp.float32)
    out += jnp.dot(hi, table_ref[1], preferred_element_type=jnp.float32)
    return out


def outer_forward(read, n, part, tokens, tw_ref, y_ref):
    @pl.loop(part.start // ROWS, (part.start + part.size) // ROWS)
    def _(r):
        rows = pl.ds(pl.multiple_of(r * ROWS, ROWS), ROWS)
        values = []
        for n1 in range(n):
            x = read(n1, rows)
            turn = 2 * math.pi * n1 / (4 * n)
            if n1 == 0:
                values.append((x, jnp.zeros_like(x)))
            else:
                values.append((x * math.cos(turn), x * -math.sin(turn)))
        for m, (re, im) in enumerate(dft(values, 1)):
            c, s = tw_ref[0, m], tw_ref[1, m]
            y_ref[m, rows, :tokens] = re * c + im * s
            y_ref[m, rows, tokens:] = im * c - re * s


def outer_inverse(write, n, part, tokens, tw_ref, y_ref):
    @pl.loop(part.start // ROWS, (part.start + part.size) // ROWS)
    def _(r):
        rows = pl.ds(pl.multiple_of(r * ROWS, ROWS), ROWS)
        values = []
        for m in range(n):
            re, im = y_ref[m, rows, :tokens], y_ref[m, rows, tokens:]
            c, s = tw_ref[0, m], tw_ref[1, m]
            values.append((re * c - im * s, im * c + re * s))
        for n1, (re, im) in enumerate(dft(values, -1)):
            turn = 2 * math.pi * n1 / (4 * n)
            if n1 == 0:
                write(n1, rows, re)
            else:
                write(n1, rows, re * math.cos(turn) - im * math.sin(turn))


def flat(x):
    return x.reshape(x.shape[0] * x.shape[1], x.shape[2])


def start_all(copies):
    for copy in copies:
        copy.start()


def wait_all(copies):
    for copy in copies:
        copy.wait()


def parts_of(size, least=1):
    step = max(least, size // PARTS)
    return [pl.ds(k, step) for k in range(0, size, step)]


def plane(width):
    return lax.axis_index("context") // width


def copies_of(pairs, sem):
    return [pltpu.make_async_copy(src, dst, sem.at[i]) for i, (src, dst) in enumerate(pairs)]


def load_tables(refs, bufs, sem):
    loads = copies_of(list(zip(refs, bufs)), sem)
    start_all(loads)
    return loads


def filter_kernel(
    first, n, channels, tokens, f_ref, tw_ref, fwd_ref, out_ref,
    tw_buf, fwd_buf, f_buf, y_ref, own_ref, sem,
):
    rows = parts_of(channels, ROWS)
    load_tw, load_fwd = load_tables((tw_ref, fwd_ref), (tw_buf, fwd_buf), sem.at[0])
    loads = copies_of(
        [(f_ref.at[pl.ds(first + part.start, part.size)], f_buf.at[part]) for part in rows],
        sem.at[1],
    )
    start_all(loads)
    load_tw.wait()
    for part, load in zip(rows, loads):
        load.wait()
        outer_forward(
            lambda n1, r: f_buf[r, n1 * tokens : (n1 + 1) * tokens], n, part, tokens, tw_buf, y_ref
        )
    load_fwd.wait()
    stores = copies_of([(own_ref.at[ms], out_ref.at[ms]) for ms in parts_of(n)], sem.at[2])
    for ms, store in zip(parts_of(n), stores):
        own_ref[ms] = times_table(flat(y_ref[ms]), fwd_buf).reshape(ms.size, channels, 2 * tokens)
        store.start()
    wait_all(stores)


def transform(
    sign, n, channels, tokens, sources, targets, tables, spec_refs, own_ref,
    tw_buf, fwd_buf, inv_buf, buf_ref, spec_buf, own_buf, y_ref, sem,
):
    rows = parts_of(channels // 2, ROWS)
    rows = [(j, part, pl.ds(part.start + j * (channels // 2), part.size)) for j in range(2) for part in rows]
    load_tw, *load_rest = load_tables(tables, (tw_buf, fwd_buf, inv_buf), sem.at[0, 0])
    loads = [copies_of(sources(part), sem.at[1, i]) for i, (_, _, part) in enumerate(rows)]
    for load in loads:
        start_all(load)
    spec_loads = copies_of(
        [(spec_refs[j].at[:, own], spec_buf.at[:, part]) for j, own, part in rows], sem.at[0, 1]
    )
    start_all(spec_loads)
    own_stores = copies_of(
        [(own_buf.at[:, part], own_ref.at[:, part]) for _, _, part in rows], sem.at[0, 2]
    )
    stores = [copies_of(targets(part), sem.at[2, i]) for i, (_, _, part) in enumerate(rows)]

    def write(n1, r, value):
        buf_ref[n1, r] = value

    load_tw.wait()
    for i, (_, _, part) in enumerate(rows):
        wait_all(loads[i])
        outer_forward(lambda n1, r: buf_ref[n1, r], n, part, tokens, tw_buf, y_ref)
        if i == 0:
            wait_all(load_rest)
        spec_loads[i].wait()
        shape = (n, part.size, 2 * tokens)
        own = times_table(flat(y_ref[:, part]), fwd_buf)
        own_buf[:, part] = own.reshape(shape)
        own_stores[i].start()
        spec = flat(spec_buf[:, part])
        re, im = own[:, :tokens], own[:, tokens:]
        s_re, s_im = spec[:, :tokens], spec[:, tokens:] * sign
        both = jnp.concatenate([re * s_re - im * s_im, re * s_im + im * s_re], axis=1)
        y_ref[:, part] = times_table(both, inv_buf).reshape(shape)
        outer_inverse(write, n, part, tokens, tw_buf, y_ref)
        start_all(stores[i])
    for store in (*stores, own_stores):
        wait_all(store)


def conv_kernel(planes, n, channels, tokens, x_ref, *refs):
    tables, spec_refs, refs = refs[:3], refs[3:5], refs[5:]
    out_refs, (own_ref, *scratch) = refs[:planes], refs[planes:]
    buf_ref = scratch[3]
    width = n // planes
    z = plane(width)

    def block(d, part):
        return buf_ref.at[pl.ds((z ^ d) * width, width), part]

    def sources(part):
        return [(x_ref.at[:, d, part], block(d, part)) for d in range(planes)]

    def targets(part):
        return [(block(d, part), out_refs[d].at[:, part]) for d in range(planes)]

    transform(
        1.0, n, channels, tokens, sources, targets, tables, spec_refs, own_ref, *scratch
    )


def back_kernel(planes, n, channels, tokens, near_ref, *refs):
    far_refs, refs = refs[: planes - 1], refs[planes - 1 :]
    tables, spec_refs, refs = refs[:3], refs[3:5], refs[5:]
    after_ref, out_ref, own_ref, *scratch = refs
    buf_ref = scratch[3]
    width = n // planes
    z = plane(width)

    def block(z, part):
        return buf_ref.at[pl.ds(z * width, width), part]

    def sources(part):
        near = [(near_ref.at[:, z, part], block(z, part))]
        return near + [
            (ref.at[:, part], block(z ^ d, part)) for d, ref in enumerate(far_refs, 1)
        ]

    def targets(part):
        return [(block(z, part), out_ref.at[:, z, part]) for z in range(planes)]

    transform(
        -1.0, n, channels, tokens, sources, targets, tables, spec_refs, own_ref, *scratch
    )


def filter_grad_kernel(
    scale, n, channels, tokens, tw_ref, inv_ref, p_ref, g_ref, out_ref,
    tw_buf, inv_buf, p_buf, g_buf, y_ref, sem,
):
    tables = load_tables((tw_ref, inv_ref), (tw_buf, inv_buf), sem.at[PARTS])
    loads = [
        copies_of([(p_ref.at[ms], p_buf.at[ms]), (g_ref.at[ms], g_buf.at[ms])], sem.at[i])
        for i, ms in enumerate(parts_of(n))
    ]
    for load in loads:
        start_all(load)
    wait_all(tables)
    for ms, load in zip(parts_of(n), loads):
        wait_all(load)
        p, g = flat(p_buf[ms]), flat(g_buf[ms])
        p_re, p_im = p[:, :tokens], p[:, tokens:]
        re, im = g[:, :tokens], g[:, tokens:]
        both = jnp.concatenate([re * p_re + im * p_im, im * p_re - re * p_im], axis=1)
        y_ref[ms] = times_table(both, inv_buf).reshape(ms.size, channels, 2 * tokens)

    def write(n1, r, value):
        out_ref[r, n1 * tokens : (n1 + 1) * tokens] = value * scale

    outer_inverse(write, n, pl.ds(0, channels), tokens, tw_buf, y_ref)


def add_kernel(a_ref, b_ref, out_ref):
    out_ref[...] = a_ref[...] + b_ref[...]


def load_pairs(n, a_ref, b_ref, a_buf, b_buf, sem):
    loads = [
        copies_of([(a_ref.at[part], a_buf.at[part]), (b_ref.at[part], b_buf.at[part])], sem.at[i])
        for i, part in enumerate(parts_of(n))
    ]
    for load in loads:
        start_all(load)
    return loads


def product_split_kernel(planes, n, a_ref, b_ref, *refs):
    out_refs, (a_buf, b_buf, sem) = refs[:planes], refs[planes:]
    width = n // planes
    z = plane(width)
    for load in load_pairs(n, a_ref, b_ref, a_buf, b_buf, sem):
        wait_all(load)
    for d in range(planes):
        for q in range(width):
            out_refs[d][q] = a_buf[(z ^ d) * width + q] * b_buf[(z ^ d) * width + q]


def product_kernel(planes, n, a_ref, b_ref, after_ref, out_ref, a_buf, b_buf, buf_ref, sem):
    width = n // planes
    parts = [pl.ds(z * width, width) for z in range(planes)]
    loads = [
        copies_of([(a_ref.at[part], a_buf.at[part]), (b_ref.at[part], b_buf.at[part])], sem.at[z])
        for z, part in enumerate(parts)
    ]
    for load in loads:
        start_all(load)
    stores = copies_of([(buf_ref.at[z], out_ref.at[:, z]) for z in range(planes)], sem.at[planes])
    for z, part in enumerate(parts):
        wait_all(loads[z])
        buf_ref[z] = a_buf[part] * b_buf[part]
        stores[z].start()
    wait_all(stores)


def send_kernel(planes, width, x_ref, *refs):
    out_refs, (buf_ref, sem) = refs[: planes - 1], refs[planes - 1 :]
    z = plane(width)
    parts = parts_of(width)
    loads = [
        copies_of([(x_ref.at[part, z ^ d], buf_ref.at[d, part]) for part in parts], sem.at[d])
        for d in range(1, planes)
    ]
    for load in loads:
        start_all(load)
    stores = copies_of([(buf_ref.at[d + 1], ref) for d, ref in enumerate(out_refs)], sem.at[0])
    for load, store in zip(loads, stores):
        wait_all(load)
        store.start()
    wait_all(stores)


def merge_kernel(planes, width, *refs):
    in_refs, (after_ref, out_ref, buf_ref, sem) = refs[:planes], refs[planes:]
    parts = parts_of(width)
    loads = [
        copies_of([(ref.at[part], buf_ref.at[part, d]) for d, ref in enumerate(in_refs)], sem.at[i])
        for i, part in enumerate(parts)
    ]
    for load in loads:
        start_all(load)
    stores = copies_of([(buf_ref.at[part], out_ref.at[part]) for part in parts], sem.at[len(parts)])
    for load, store in zip(loads, stores):
        wait_all(load)
        store.start()
    wait_all(stores)


def gate_parts(width, blocks, a_ref, b_ref, outs, a_buf, b_buf, sem):
    stores = []
    for d, (read, first) in enumerate(blocks):
        part = pl.ds(first, width)
        x = read()
        a_buf[part] = x * a_ref[part]
        b_buf[part] = x * b_ref[part]
        pairs = [(buf.at[part], out.at[part]) for buf, out in zip((a_buf, b_buf), outs)]
        stores.extend(copies_of(pairs, sem.at[d]))
        start_all(stores[-2:])
    wait_all(stores)


def gate_kernel(
    planes, width, x_ref, a_ref, b_ref, oa_ref, ob_ref, x_buf, a_in, b_in, a_buf, b_buf, sem
):
    z = plane(width)
    loads = []
    for d in range(planes):
        part = pl.ds((z ^ d) * width, width)
        pairs = [
            (x_ref.at[:, d], x_buf.at[d]),
            (a_ref.at[part], a_in.at[part]),
            (b_ref.at[part], b_in.at[part]),
        ]
        loads.append(copies_of(pairs, sem.at[planes + d]))
        start_all(loads[-1])

    def read(d):
        wait_all(loads[d])
        return x_buf[d]

    blocks = [(lambda d=d: read(d), (z ^ d) * width) for d in range(planes)]
    gate_parts(width, blocks, a_in, b_in, (oa_ref, ob_ref), a_buf, b_buf, sem)


def gate_split_kernel(planes, width, *refs):
    far_refs, refs = refs[: planes - 1], refs[planes - 1 :]
    a_ref, b_ref, near_ref, after_ref, oa_ref, ob_ref, x_buf, a_buf, b_buf, sem = refs
    z = plane(width)
    load = pltpu.make_async_copy(near_ref.at[:, z], x_buf, sem.at[planes, 0])
    load.start()

    def read():
        load.wait()
        return x_buf[...]

    blocks = [(lambda d=d: far_refs[d - 1][...], (z ^ d) * width) for d in range(1, planes)]
    blocks.append((read, z * width))
    gate_parts(width, blocks, a_ref, b_ref, (oa_ref, ob_ref), a_buf, b_buf, sem)


SPACES = {"v": pltpu.VMEM, "u": pltpu.VMEM, "h": pltpu.HBM, "a": pl.ANY}


def kernel_call(body, ins, outs, scratch, flops=0):
    shapes = [
        jax.ShapeDtypeStruct(shape, jnp.float32) if space == "u" else SPACES[space](shape, jnp.float32)
        for space, shape in outs
    ]

    def run(*args):
        args = [
            pltpu.with_memory_space_constraint(x, pltpu.HBM) if space == "h" else x
            for space, x in zip(ins, args, strict=True)
        ]
        size = sum(math.prod(x.shape) for x in (*args, *shapes))
        return pl.pallas_call(
            body,
            in_specs=[pl.BlockSpec(memory_space=SPACES[space]) for space in ins],
            out_specs=[pl.BlockSpec(memory_space=SPACES[space]) for space, _ in outs],
            out_shape=shapes,
            scratch_shapes=scratch,
            compiler_params=pltpu.CompilerParams(vmem_limit_bytes=VMEM_BYTES),
            cost_estimate=pl.CostEstimate(flops=flops, bytes_accessed=4 * size, transcendentals=0),
        )(*args)

    return run


def tables(n, tokens):
    length = n * tokens
    m = np.arange(n)[:, None] + 0.25
    angle = 2 * np.pi * m * np.arange(tokens)[None, :] / length
    tw = np.stack([np.cos(angle), np.sin(angle)])[:, :, None, :]
    tw = np.broadcast_to(tw, (2, n, ROWS, tokens)).astype(np.float32)
    k = np.arange(tokens)
    inner = 2 * np.pi * ((k[:, None] * k[None, :]) % tokens) / tokens
    c, s = np.cos(inner), np.sin(inner)

    def pair(table):
        hi = table.astype(ml_dtypes.bfloat16)
        lo = (table - hi.astype(np.float64)).astype(ml_dtypes.bfloat16)
        return jnp.asarray(np.stack([hi, lo]))

    fwd = pair(np.block([[c, -s], [s, c]]))
    inv = pair(np.block([[c, s], [-s, c]]) / length)
    return jnp.asarray(tw), fwd, inv


def on_device(query_input, key_input, value_input, filters, cotangent):
    n = lax.axis_size("context")
    pair_size = lax.axis_size("dp")
    _, width, tokens = query_input.shape
    channels, length = filters.shape
    scale = 1.0 / math.sqrt(pair_size * length)
    sizes = (n, channels, tokens)
    tw, fwd, inv = tables(n, tokens)
    planes = math.gcd(n, PLANES)
    width = n // planes
    blocks, spectrum = (n, channels, tokens), (n, channels, 2 * tokens)
    one, paired, lags = (width, channels, tokens), (width, planes, channels, tokens), (channels, length)
    flops = 4 * 2 * 2 * tokens * n * channels * tokens
    f32 = jnp.float32
    y = pltpu.VMEM(spectrum, f32)

    def semaphores(*shape):
        return pltpu.SemaphoreType.DMA(shape)

    def part(body, *args):
        return lambda *refs: body(*args, *refs)

    def along_z(xs):
        return [
            lax.ppermute(x, "context", [(i, i ^ (d * width)) for i in range(n)])
            for d, x in enumerate(xs, 1)
        ]

    def within_plane(x):
        members = [[z * width + q for q in range(width)] for z in range(planes)]
        return lax.all_to_all(x, "context", 0, 0, axis_index_groups=members, tiled=True)

    query, key, value, cot = (
        x.reshape(blocks) for x in (query_input, key_input, value_input, cotangent)
    )
    rows, paired_buf = pltpu.VMEM(blocks, f32), pltpu.VMEM(paired, f32)
    by_plane = pltpu.VMEM((planes, *one), f32)
    outs = [("h", one)] * (planes - 1)
    send = kernel_call(
        part(send_kernel, planes, width), "a", outs, [by_plane, semaphores(planes, planes + PARTS)]
    )
    merge = kernel_call(
        part(merge_kernel, planes, width), "a" * planes + "a", [("h", paired)],
        [paired_buf, semaphores(PARTS + 1, planes + PARTS)],
    )
    half_sizes = (n, channels // 2, tokens)
    half_spectrum = (n, channels // 2, 2 * tokens)
    table_bufs = [pltpu.VMEM(table.shape, table.dtype) for table in (tw, fwd, inv)]

    def transform_filters(first):
        return kernel_call(
            part(filter_kernel, first, *half_sizes), "hhh", [("h", half_spectrum)],
            [
                *table_bufs[:2],
                pltpu.VMEM((channels // 2, length), f32),
                *[pltpu.VMEM(half_spectrum, f32)] * 2,
                semaphores(3, PARTS),
            ],
            flops // 2,
        )(filters, tw, fwd)[0]

    transform_scratch = [
        *table_bufs, rows, y, y, y, semaphores(3, 2 * PARTS, max(2 * PARTS, planes))
    ]
    always = lax.axis_index("context") < n

    def grouped(body, *args):
        shapes = jax.eval_shape(body, *args)

        def never(*args):
            return jax.tree.map(lambda x: jnp.zeros(x.shape, x.dtype), shapes)

        return lax.cond(always, body, never, *args)

    keep_p, *send_p = kernel_call(
        part(product_split_kernel, planes, n), "hh", [("u", one)] * planes,
        [rows, rows, semaphores(PARTS, 2)],
    )(key, value)
    got_p = along_z(send_p)

    def first(cot, query, keep_p):
        (conv_grad,) = kernel_call(
            part(product_kernel, planes, n), "hha", [("h", paired)],
            [rows, rows, by_plane, semaphores(planes + 1, planes)],
        )(cot, query, keep_p)
        near_g = within_plane(conv_grad)
        return near_g, send(near_g), transform_filters(0)

    near_g, send_g, filt_a = grouped(first, cot, query, keep_p)
    far_g = along_z(send_g)

    def second(keep_p, got_p, send_g, filt_a):
        product_ch = within_plane(*merge(keep_p, *got_p, send_g))
        filt = (filt_a, transform_filters(channels // 2))
        *outs, prod_spec = kernel_call(
            part(conv_kernel, planes, *sizes), "ahhhhh",
            [("h", one)] * planes + [("h", spectrum)], transform_scratch, 2 * flops,
        )(product_ch, tw, fwd, inv, *filt)
        return outs, prod_spec, filt

    (keep_c, *send_c), prod_spec, filt = grouped(second, keep_p, got_p, send_g[0], filt_a)
    got_c = along_z(send_c)

    def third(near_g, far_g, filt, keep_c, prod_spec):
        back_ch, grad_spec = kernel_call(
            part(back_kernel, planes, *sizes), "a" * planes + "hhhhha",
            [("h", paired), ("h", spectrum)], transform_scratch, 2 * flops,
        )(near_g, *far_g, tw, fwd, inv, *filt, keep_c)
        near_b = within_plane(back_ch)
        (own,) = kernel_call(
            part(filter_grad_kernel, scale, *sizes), "hhhh", [("u", lags)],
            [table_bufs[0], table_bufs[2], y, y, y, semaphores(PARTS + 1, 2)], flops,
        )(tw, inv, prod_spec, grad_spec)
        if pair_size == 2:
            other = lax.ppermute(own, "dp", [(0, 1), (1, 0)])
        else:
            other = lax.psum(own, "dp") - own
        return near_b, send(near_b), own, other

    near_b, send_b, own, other = grouped(third, near_g, far_g, filt, keep_c, prod_spec)
    far_b = along_z(send_b)

    def fourth(keep_c, got_c, send_b, query, cot, own, other):
        conv_tok = within_plane(*merge(keep_c, *got_c, send_b))
        (grad_filter,) = kernel_call(add_kernel, "vv", [("u", lags)], [])(own, other)
        gated, grad_query = kernel_call(
            part(gate_kernel, planes, width), "ahh", [("h", blocks)] * 2,
            [by_plane, *[rows] * 4, semaphores(2 * planes, 3)],
        )(conv_tok, query, cot)
        return gated, grad_query, grad_filter

    gated, grad_query, grad_filter = grouped(
        fourth, keep_c, got_c, send_b[0], query, cot, own, other
    )
    grad_key, grad_value = kernel_call(
        part(gate_split_kernel, planes, width), "v" * (planes + 1) + "aa", [("h", blocks)] * 2,
        [pltpu.VMEM(one, f32), rows, rows, semaphores(planes + 1, 2)],
    )(*far_b, value, key, near_b, gated)
    shape = query_input.shape
    return (
        gated.reshape(shape),
        grad_query.reshape(shape),
        grad_key.reshape(shape),
        grad_value.reshape(shape),
        grad_filter,
    )


def solution(mesh):
    in_specs = (
        P("dp", None, "context"),
        P("dp", None, "context"),
        P("dp", None, "context"),
        P("context", None),
        P("dp", None, "context"),
    )
    out_specs = (
        P("dp", None, "context"),
        P("dp", None, "context"),
        P("dp", None, "context"),
        P("dp", None, "context"),
        P("context", None),
    )
    return jax.shard_map(
        on_device, mesh=mesh, in_specs=in_specs, out_specs=out_specs, check_vma=False
    )
```

```python
import math

import jax
import jax.numpy as jnp
import ml_dtypes
import numpy as np
from jax import lax
from jax.experimental import pallas as pl
from jax.experimental.pallas import tpu as pltpu
from jax.sharding import PartitionSpec as P

ROWS = 8
PLANES = 4
PARTS = 4
VMEM_BYTES = 24 * 1024 * 1024


def twist(value, turn):
    re, im = value
    turn = turn % 1.0
    if turn == 0.0:
        return re, im
    if turn == 0.25:
        return im, -re
    if turn == 0.5:
        return -re, -im
    if turn == 0.75:
        return -im, re
    if turn in (0.125, 0.375, 0.625, 0.875):
        half = math.sqrt(0.5)
        a, b = (re + im) * half, (im - re) * half
        return twist((a, b), turn - 0.125)
    c, s = math.cos(2 * math.pi * turn), math.sin(2 * math.pi * turn)
    return re * c + im * s, im * c - re * s


def dft(values, sign):
    n = len(values)
    if n == 1:
        return values
    even, odd = dft(values[0::2], sign), dft(values[1::2], sign)
    out = [None] * n
    for k in range(n // 2):
        a, b = even[k], twist(odd[k], sign * k / n)
        out[k] = (a[0] + b[0], a[1] + b[1])
        out[k + n // 2] = (a[0] - b[0], a[1] - b[1])
    return out


def times_table(x, table_ref):
    hi = x.astype(jnp.bfloat16)
    lo = (x - hi.astype(jnp.float32)).astype(jnp.bfloat16)
    return jnp.dot(
        jnp.concatenate([hi, lo, hi], axis=1), table_ref[...], preferred_element_type=jnp.float32
    )


def outer_forward(read, n, part, tokens, tw_ref, y_ref):
    @pl.loop(part.start // ROWS, (part.start + part.size) // ROWS)
    def _(r):
        rows = pl.ds(pl.multiple_of(r * ROWS, ROWS), ROWS)
        values = []
        for n1 in range(n):
            x = read(n1, rows)
            turn = 2 * math.pi * n1 / (4 * n)
            if n1 == 0:
                values.append((x, jnp.zeros_like(x)))
            else:
                values.append((x * math.cos(turn), x * -math.sin(turn)))
        for m, (re, im) in enumerate(dft(values, 1)):
            c, s = tw_ref[0, m], tw_ref[1, m]
            y_ref[m, rows, :tokens] = re * c + im * s
            y_ref[m, rows, tokens:] = im * c - re * s


def outer_inverse(write, n, part, tokens, tw_ref, y_ref):
    @pl.loop(part.start // ROWS, (part.start + part.size) // ROWS)
    def _(r):
        rows = pl.ds(pl.multiple_of(r * ROWS, ROWS), ROWS)
        values = []
        for m in range(n):
            re, im = y_ref[m, rows, :tokens], y_ref[m, rows, tokens:]
            c, s = tw_ref[0, m], tw_ref[1, m]
            values.append((re * c - im * s, im * c + re * s))
        for n1, (re, im) in enumerate(dft(values, -1)):
            turn = 2 * math.pi * n1 / (4 * n)
            if n1 == 0:
                write(n1, rows, re)
            else:
                write(n1, rows, re * math.cos(turn) - im * math.sin(turn))


def flat(x):
    return x.reshape(x.shape[0] * x.shape[1], x.shape[2])


def start_all(copies):
    for copy in copies:
        copy.start()


def wait_all(copies):
    for copy in copies:
        copy.wait()


def parts_of(size, least=1):
    step = max(least, size // PARTS)
    return [pl.ds(k, step) for k in range(0, size, step)]


def plane(width):
    return lax.axis_index("context") // width


def copies_of(pairs, sem):
    return [pltpu.make_async_copy(src, dst, sem.at[i]) for i, (src, dst) in enumerate(pairs)]


def filter_kernel(
    first, n, channels, tokens, f_ref, tw_ref, fwd_ref, out_ref, f_buf, y_ref, own_ref, sem
):
    rows = parts_of(channels, ROWS)
    loads = copies_of(
        [(f_ref.at[pl.ds(first + part.start, part.size)], f_buf.at[part]) for part in rows],
        sem.at[0],
    )
    start_all(loads)
    for part, load in zip(rows, loads):
        load.wait()
        outer_forward(
            lambda n1, r: f_buf[r, n1 * tokens : (n1 + 1) * tokens], n, part, tokens, tw_ref, y_ref
        )
    stores = copies_of([(own_ref.at[ms], out_ref.at[ms]) for ms in parts_of(n)], sem.at[1])
    for ms, store in zip(parts_of(n), stores):
        own_ref[ms] = times_table(flat(y_ref[ms]), fwd_ref).reshape(ms.size, channels, 2 * tokens)
        store.start()
    wait_all(stores)


def transform(
    sign, n, channels, tokens, sources, targets, tw_ref, fwd_ref, inv_ref, spec_refs, own_ref,
    buf_ref, spec_buf, own_buf, y_ref, sem,
):
    half = channels // 2
    rows = [pl.ds(0, half), pl.ds(half, half)]
    loads = [copies_of(sources(part), sem.at[0, i]) for i, part in enumerate(rows)]
    for load in loads:
        start_all(load)
    spec_loads = [
        copies_of(
            [
                (ref.at[ms], spec_buf.at[ms, pl.ds(j * half, half)])
                for j, ref in enumerate(spec_refs)
            ],
            sem.at[1, i],
        )
        for i, ms in enumerate(parts_of(n))
    ]
    for load in spec_loads:
        start_all(load)
    for part, load in zip(rows, loads):
        wait_all(load)
        outer_forward(lambda n1, r: buf_ref[n1, r], n, part, tokens, tw_ref, y_ref)
    own_stores = copies_of([(own_buf.at[ms], own_ref.at[ms]) for ms in parts_of(n)], sem.at[2, 0])
    for ms, load, store in zip(parts_of(n), spec_loads, own_stores):
        own = times_table(flat(y_ref[ms]), fwd_ref)
        own_buf[ms] = own.reshape(ms.size, channels, 2 * tokens)
        store.start()
        wait_all(load)
        spec = flat(spec_buf[ms])
        re, im = own[:, :tokens], own[:, tokens:]
        s_re, s_im = spec[:, :tokens], spec[:, tokens:] * sign
        both = jnp.concatenate([re * s_re - im * s_im, re * s_im + im * s_re], axis=1)
        y_ref[ms] = times_table(both, inv_ref).reshape(ms.size, channels, 2 * tokens)

    def write(n1, r, value):
        buf_ref[n1, r] = value

    stores = [copies_of(targets(part), sem.at[3, i]) for i, part in enumerate(rows)]
    for part, store in zip(rows, stores):
        outer_inverse(write, n, part, tokens, tw_ref, y_ref)
        start_all(store)
    for store in (*stores, own_stores):
        wait_all(store)


def conv_kernel(planes, n, channels, tokens, x_ref, *refs):
    tables, spec_refs, refs = refs[:3], refs[3:5], refs[5:]
    out_refs, (own_ref, *scratch) = refs[:planes], refs[planes:]
    buf_ref = scratch[0]
    width = n // planes
    z = plane(width)

    def block(d, part):
        return buf_ref.at[pl.ds((z ^ d) * width, width), part]

    def sources(part):
        return [(x_ref.at[:, d, part], block(d, part)) for d in range(planes)]

    def targets(part):
        return [(block(d, part), out_refs[d].at[:, part]) for d in range(planes)]

    transform(
        1.0, n, channels, tokens, sources, targets, *tables, spec_refs, own_ref, *scratch
    )


def back_kernel(planes, n, channels, tokens, near_ref, *refs):
    far_refs, refs = refs[: planes - 1], refs[planes - 1 :]
    tables, spec_refs, refs = refs[:3], refs[3:5], refs[5:]
    after_ref, out_ref, own_ref, *scratch = refs
    buf_ref = scratch[0]
    width = n // planes
    z = plane(width)

    def block(z, part):
        return buf_ref.at[pl.ds(z * width, width), part]

    def sources(part):
        near = [(near_ref.at[:, z, part], block(z, part))]
        return near + [
            (ref.at[:, part], block(z ^ d, part)) for d, ref in enumerate(far_refs, 1)
        ]

    def targets(part):
        return [(block(z, part), out_ref.at[:, z, part]) for z in range(planes)]

    transform(
        -1.0, n, channels, tokens, sources, targets, *tables, spec_refs, own_ref, *scratch
    )


def filter_grad_kernel(
    scale, n, channels, tokens, tw_ref, inv_ref, p_ref, g_ref, out_ref, p_buf, g_buf, y_ref, sem
):
    loads = [
        copies_of([(p_ref.at[ms], p_buf.at[ms]), (g_ref.at[ms], g_buf.at[ms])], sem.at[i])
        for i, ms in enumerate(parts_of(n))
    ]
    for load in loads:
        start_all(load)
    for ms, load in zip(parts_of(n), loads):
        wait_all(load)
        p, g = flat(p_buf[ms]), flat(g_buf[ms])
        p_re, p_im = p[:, :tokens], p[:, tokens:]
        re, im = g[:, :tokens], g[:, tokens:]
        both = jnp.concatenate([re * p_re + im * p_im, im * p_re - re * p_im], axis=1)
        y_ref[ms] = times_table(both, inv_ref).reshape(ms.size, channels, 2 * tokens)

    def write(n1, r, value):
        out_ref[r, n1 * tokens : (n1 + 1) * tokens] = value * scale

    outer_inverse(write, n, pl.ds(0, channels), tokens, tw_ref, y_ref)


def add_kernel(a_ref, b_ref, out_ref):
    out_ref[...] = a_ref[...] + b_ref[...]


def load_pairs(n, a_ref, b_ref, a_buf, b_buf, sem):
    loads = [
        copies_of([(a_ref.at[part], a_buf.at[part]), (b_ref.at[part], b_buf.at[part])], sem.at[i])
        for i, part in enumerate(parts_of(n))
    ]
    for load in loads:
        start_all(load)
    return loads


def product_split_kernel(planes, n, a_ref, b_ref, *refs):
    out_refs, (a_buf, b_buf, sem) = refs[:planes], refs[planes:]
    width = n // planes
    z = plane(width)
    for load in load_pairs(n, a_ref, b_ref, a_buf, b_buf, sem):
        wait_all(load)
    for d in range(planes):
        for q in range(width):
            out_refs[d][q] = a_buf[(z ^ d) * width + q] * b_buf[(z ^ d) * width + q]


def product_kernel(planes, n, a_ref, b_ref, after_ref, out_ref, a_buf, b_buf, buf_ref, sem):
    width = n // planes
    parts = [pl.ds(z * width, width) for z in range(planes)]
    loads = [
        copies_of([(a_ref.at[part], a_buf.at[part]), (b_ref.at[part], b_buf.at[part])], sem.at[z])
        for z, part in enumerate(parts)
    ]
    for load in loads:
        start_all(load)
    stores = copies_of([(buf_ref.at[z], out_ref.at[:, z]) for z in range(planes)], sem.at[planes])
    for z, part in enumerate(parts):
        wait_all(loads[z])
        buf_ref[z] = a_buf[part] * b_buf[part]
        stores[z].start()
    wait_all(stores)


def send_kernel(planes, width, x_ref, *refs):
    out_refs, (buf_ref, sem) = refs[: planes - 1], refs[planes - 1 :]
    z = plane(width)
    parts = parts_of(width)
    loads = [
        copies_of([(x_ref.at[part, z ^ d], buf_ref.at[d, part]) for part in parts], sem.at[d])
        for d in range(1, planes)
    ]
    for load in loads:
        start_all(load)
    stores = copies_of([(buf_ref.at[d + 1], ref) for d, ref in enumerate(out_refs)], sem.at[0])
    for load, store in zip(loads, stores):
        wait_all(load)
        store.start()
    wait_all(stores)


def merge_kernel(planes, width, *refs):
    in_refs, (after_ref, out_ref, buf_ref, sem) = refs[:planes], refs[planes:]
    parts = parts_of(width)
    loads = [
        copies_of([(ref.at[part], buf_ref.at[part, d]) for d, ref in enumerate(in_refs)], sem.at[i])
        for i, part in enumerate(parts)
    ]
    for load in loads:
        start_all(load)
    stores = copies_of([(buf_ref.at[part], out_ref.at[part]) for part in parts], sem.at[len(parts)])
    for load, store in zip(loads, stores):
        wait_all(load)
        store.start()
    wait_all(stores)


def gate_parts(width, blocks, a_ref, b_ref, outs, a_buf, b_buf, sem):
    stores = []
    for d, (read, first) in enumerate(blocks):
        part = pl.ds(first, width)
        x = read()
        a_buf[part] = x * a_ref[part]
        b_buf[part] = x * b_ref[part]
        pairs = [(buf.at[part], out.at[part]) for buf, out in zip((a_buf, b_buf), outs)]
        stores.extend(copies_of(pairs, sem.at[d]))
        start_all(stores[-2:])
    wait_all(stores)


def gate_kernel(
    planes, width, x_ref, a_ref, b_ref, oa_ref, ob_ref, x_buf, a_in, b_in, a_buf, b_buf, sem
):
    z = plane(width)
    loads = []
    for d in range(planes):
        part = pl.ds((z ^ d) * width, width)
        pairs = [
            (x_ref.at[:, d], x_buf.at[d]),
            (a_ref.at[part], a_in.at[part]),
            (b_ref.at[part], b_in.at[part]),
        ]
        loads.append(copies_of(pairs, sem.at[planes + d]))
        start_all(loads[-1])

    def read(d):
        wait_all(loads[d])
        return x_buf[d]

    blocks = [(lambda d=d: read(d), (z ^ d) * width) for d in range(planes)]
    gate_parts(width, blocks, a_in, b_in, (oa_ref, ob_ref), a_buf, b_buf, sem)


def gate_near_kernel(
    planes, width, near_ref, a_ref, b_ref, oa_ref, ob_ref, x_buf, a_buf, b_buf, sem
):
    z = plane(width)
    part = pl.ds(z * width, width)
    pairs = [(near_ref.at[:, z], x_buf), (a_ref.at[part], a_buf), (b_ref.at[part], b_buf)]
    loads = copies_of(pairs, sem.at[0])
    start_all(loads)
    wait_all(loads)
    a_buf[...] = x_buf[...] * a_buf[...]
    b_buf[...] = x_buf[...] * b_buf[...]
    stores = copies_of([(a_buf, oa_ref.at[part]), (b_buf, ob_ref.at[part])], sem.at[1])
    start_all(stores)
    wait_all(stores)


def gate_far_kernel(planes, width, *refs):
    far_refs, refs = refs[: planes - 1], refs[planes - 1 :]
    a_ref, b_ref, _, _, _, oa_ref, ob_ref, a_buf, b_buf, sem = refs
    z = plane(width)
    blocks = [(lambda d=d: far_refs[d - 1][...], (z ^ d) * width) for d in range(1, planes)]
    gate_parts(width, blocks, a_ref, b_ref, (oa_ref, ob_ref), a_buf, b_buf, sem)


SPACES = {"v": pltpu.VMEM, "u": pltpu.VMEM, "h": pltpu.HBM, "a": pl.ANY}


def kernel_call(body, ins, outs, scratch, flops=0, aliases=None):
    shapes = [
        jax.ShapeDtypeStruct(shape, jnp.float32) if space == "u" else SPACES[space](shape, jnp.float32)
        for space, shape in outs
    ]

    def run(*args):
        args = [
            pltpu.with_memory_space_constraint(x, pltpu.HBM) if space == "h" else x
            for space, x in zip(ins, args, strict=True)
        ]
        size = sum(math.prod(x.shape) for x in (*args, *shapes))
        return pl.pallas_call(
            body,
            in_specs=[pl.BlockSpec(memory_space=SPACES[space]) for space in ins],
            out_specs=[pl.BlockSpec(memory_space=SPACES[space]) for space, _ in outs],
            out_shape=shapes,
            scratch_shapes=scratch,
            input_output_aliases=aliases or {},
            compiler_params=pltpu.CompilerParams(vmem_limit_bytes=VMEM_BYTES),
            cost_estimate=pl.CostEstimate(flops=flops, bytes_accessed=4 * size, transcendentals=0),
        )(*args)

    return run


def tables(n, tokens):
    length = n * tokens
    m = np.arange(n)[:, None] + 0.25
    angle = 2 * np.pi * m * np.arange(tokens)[None, :] / length
    tw = np.stack([np.cos(angle), np.sin(angle)])[:, :, None, :]
    tw = np.broadcast_to(tw, (2, n, ROWS, tokens)).astype(np.float32)
    k = np.arange(tokens)
    inner = 2 * np.pi * ((k[:, None] * k[None, :]) % tokens) / tokens
    c, s = np.cos(inner), np.sin(inner)

    def pair(table):
        hi = table.astype(ml_dtypes.bfloat16)
        lo = (table - hi.astype(np.float64)).astype(ml_dtypes.bfloat16)
        return jnp.asarray(np.concatenate([hi, hi, lo]))

    fwd = pair(np.block([[c, -s], [s, c]]))
    inv = pair(np.block([[c, s], [-s, c]]) / length)
    return jnp.asarray(tw), fwd, inv


def on_device(query_input, key_input, value_input, filters, cotangent):
    n = lax.axis_size("context")
    pair_size = lax.axis_size("dp")
    _, width, tokens = query_input.shape
    channels, length = filters.shape
    scale = 1.0 / math.sqrt(pair_size * length)
    sizes = (n, channels, tokens)
    tw, fwd, inv = tables(n, tokens)
    planes = math.gcd(n, PLANES)
    width = n // planes
    blocks, spectrum = (n, channels, tokens), (n, channels, 2 * tokens)
    one, paired, lags = (width, channels, tokens), (width, planes, channels, tokens), (channels, length)
    flops = 4 * 2 * 2 * tokens * n * channels * tokens
    f32 = jnp.float32
    y = pltpu.VMEM(spectrum, f32)

    def semaphores(*shape):
        return pltpu.SemaphoreType.DMA(shape)

    def part(body, *args):
        return lambda *refs: body(*args, *refs)

    def along_z(xs):
        return [
            lax.ppermute(x, "context", [(i, i ^ (d * width)) for i in range(n)])
            for d, x in enumerate(xs, 1)
        ]

    def within_plane(x):
        members = [[z * width + q for q in range(width)] for z in range(planes)]
        return lax.all_to_all(x, "context", 0, 0, axis_index_groups=members, tiled=True)

    query, key, value, cot = (
        x.reshape(blocks) for x in (query_input, key_input, value_input, cotangent)
    )
    rows, paired_buf = pltpu.VMEM(blocks, f32), pltpu.VMEM(paired, f32)
    by_plane = pltpu.VMEM((planes, *one), f32)
    outs = [("h", one)] * (planes - 1)
    send = kernel_call(
        part(send_kernel, planes, width), "a", outs, [by_plane, semaphores(planes, planes + PARTS)]
    )
    merge = kernel_call(
        part(merge_kernel, planes, width), "a" * planes + "a", [("h", paired)],
        [paired_buf, semaphores(PARTS + 1, planes + PARTS)],
    )
    half_sizes = (n, channels // 2, tokens)
    half_spectrum = (n, channels // 2, 2 * tokens)
    def transform_filters(first):
        return kernel_call(
            part(filter_kernel, first, *half_sizes), "hvv", [("h", half_spectrum)],
            [
                pltpu.VMEM((channels // 2, length), f32),
                *[pltpu.VMEM(half_spectrum, f32)] * 2,
                semaphores(2, PARTS),
            ],
            flops // 2,
        )(filters, tw, fwd)[0]

    transform_scratch = [rows, y, y, y, semaphores(4, PARTS, max(PARTS, planes))]
    always = lax.axis_index("context") < n

    def grouped(body, *args):
        shapes = jax.eval_shape(body, *args)

        def never(*args):
            return jax.tree.map(lambda x: jnp.zeros(x.shape, x.dtype), shapes)

        return lax.cond(always, body, never, *args)

    keep_p, *send_p = kernel_call(
        part(product_split_kernel, planes, n), "hh", [("u", one)] * planes,
        [rows, rows, semaphores(PARTS, 2)],
    )(key, value)
    got_p = along_z(send_p)

    def first(cot, query, keep_p):
        (conv_grad,) = kernel_call(
            part(product_kernel, planes, n), "hha", [("h", paired)],
            [rows, rows, by_plane, semaphores(planes + 1, planes)],
        )(cot, query, keep_p)
        near_g = within_plane(conv_grad)
        return near_g, send(near_g), transform_filters(0)

    near_g, send_g, filt_a = grouped(first, cot, query, keep_p)
    far_g = along_z(send_g)

    def second(keep_p, got_p, send_g, filt_a):
        product_ch = within_plane(*merge(keep_p, *got_p, send_g))
        filt = (filt_a, transform_filters(channels // 2))
        *outs, prod_spec = kernel_call(
            part(conv_kernel, planes, *sizes), "avvvhh",
            [("h", one)] * planes + [("h", spectrum)], transform_scratch, 2 * flops,
        )(product_ch, tw, fwd, inv, *filt)
        return outs, prod_spec, filt

    (keep_c, *send_c), prod_spec, filt = grouped(second, keep_p, got_p, send_g[0], filt_a)
    got_c = along_z(send_c)

    def third(near_g, far_g, filt, keep_c, prod_spec):
        back_ch, grad_spec = kernel_call(
            part(back_kernel, planes, *sizes), "a" * planes + "vvvhha",
            [("h", paired), ("h", spectrum)], transform_scratch, 2 * flops,
        )(near_g, *far_g, tw, fwd, inv, *filt, keep_c)
        near_b = within_plane(back_ch)
        (own,) = kernel_call(
            part(filter_grad_kernel, scale, *sizes), "vvhh", [("u", lags)],
            [y, y, y, semaphores(PARTS, 2)], flops,
        )(tw, inv, prod_spec, grad_spec)
        return near_b, send(near_b), own

    near_b, send_b, own = grouped(third, near_g, far_g, filt, keep_c, prod_spec)
    far_b = along_z(send_b)

    def fourth(keep_c, got_c, query, cot, near_b, value, key, own):
        if pair_size == 2:
            other = lax.ppermute(own, "dp", [(0, 1), (1, 0)])
        else:
            other = lax.psum(own, "dp") - own
        conv_tok = within_plane(*merge(keep_c, *got_c, other))
        (grad_filter,) = kernel_call(add_kernel, "vv", [("u", lags)], [])(own, other)
        begun = kernel_call(
            part(gate_near_kernel, planes, width), "ahh", [("h", blocks)] * 2,
            [pltpu.VMEM(one, f32)] * 3 + [semaphores(2, 3)],
        )(near_b, value, key)
        gated, grad_query = kernel_call(
            part(gate_kernel, planes, width), "ahh", [("h", blocks)] * 2,
            [by_plane, *[rows] * 4, semaphores(2 * planes, 3)],
        )(conv_tok, query, cot)
        return gated, grad_query, begun, grad_filter

    gated, grad_query, begun, grad_filter = grouped(
        fourth, keep_c, got_c, query, cot, near_b, value, key, own
    )
    grad_key, grad_value = kernel_call(
        part(gate_far_kernel, planes, width), "v" * (planes + 1) + "hha", [("h", blocks)] * 2,
        [rows, rows, semaphores(planes, 2)], aliases={planes + 1: 0, planes + 2: 1},
    )(*far_b, value, key, *begun, gated)
    shape = query_input.shape
    return (
        gated.reshape(shape),
        grad_query.reshape(shape),
        grad_key.reshape(shape),
        grad_value.reshape(shape),
        grad_filter,
    )


def solution(mesh):
    in_specs = (
        P("dp", None, "context"),
        P("dp", None, "context"),
        P("dp", None, "context"),
        P("context", None),
        P("dp", None, "context"),
    )
    out_specs = (
        P("dp", None, "context"),
        P("dp", None, "context"),
        P("dp", None, "context"),
        P("dp", None, "context"),
        P("context", None),
    )
    return jax.shard_map(
        on_device, mesh=mesh, in_specs=in_specs, out_specs=out_specs, check_vma=False
    )
```

```python
import math

import jax
import jax.numpy as jnp
import ml_dtypes
import numpy as np
from jax import lax
from jax.experimental import pallas as pl
from jax.experimental.pallas import tpu as pltpu
from jax.sharding import PartitionSpec as P

ROWS = 8
PLANES = 4
PARTS = 4
VMEM_BYTES = 24 * 1024 * 1024


def twist(value, turn):
    re, im = value
    turn = turn % 1.0
    if turn == 0.0:
        return re, im
    if turn == 0.25:
        return im, -re
    if turn == 0.5:
        return -re, -im
    if turn == 0.75:
        return -im, re
    if turn in (0.125, 0.375, 0.625, 0.875):
        half = math.sqrt(0.5)
        a, b = (re + im) * half, (im - re) * half
        return twist((a, b), turn - 0.125)
    c, s = math.cos(2 * math.pi * turn), math.sin(2 * math.pi * turn)
    return re * c + im * s, im * c - re * s


def dft(values, sign):
    n = len(values)
    if n == 1:
        return values
    even, odd = dft(values[0::2], sign), dft(values[1::2], sign)
    out = [None] * n
    for k in range(n // 2):
        a, b = even[k], twist(odd[k], sign * k / n)
        out[k] = (a[0] + b[0], a[1] + b[1])
        out[k + n // 2] = (a[0] - b[0], a[1] - b[1])
    return out


def times_table(x, table_ref):
    hi = x.astype(jnp.bfloat16)
    lo = (x - hi.astype(jnp.float32)).astype(jnp.bfloat16)
    return jnp.dot(
        jnp.concatenate([hi, lo, hi], axis=1), table_ref[...], preferred_element_type=jnp.float32
    )


def outer_forward(read, n, part, tokens, tw_ref, y_ref):
    @pl.loop(part.start // ROWS, (part.start + part.size) // ROWS)
    def _(r):
        rows = pl.ds(pl.multiple_of(r * ROWS, ROWS), ROWS)
        values = []
        for n1 in range(n):
            x = read(n1, rows)
            turn = 2 * math.pi * n1 / (4 * n)
            if n1 == 0:
                values.append((x, jnp.zeros_like(x)))
            else:
                values.append((x * math.cos(turn), x * -math.sin(turn)))
        for m, (re, im) in enumerate(dft(values, 1)):
            c, s = tw_ref[0, m], tw_ref[1, m]
            y_ref[m, rows, :tokens] = re * c + im * s
            y_ref[m, rows, tokens:] = im * c - re * s


def outer_inverse(write, n, part, tokens, tw_ref, y_ref):
    @pl.loop(part.start // ROWS, (part.start + part.size) // ROWS)
    def _(r):
        rows = pl.ds(pl.multiple_of(r * ROWS, ROWS), ROWS)
        values = []
        for m in range(n):
            re, im = y_ref[m, rows, :tokens], y_ref[m, rows, tokens:]
            c, s = tw_ref[0, m], tw_ref[1, m]
            values.append((re * c - im * s, im * c + re * s))
        for n1, (re, im) in enumerate(dft(values, -1)):
            turn = 2 * math.pi * n1 / (4 * n)
            if n1 == 0:
                write(n1, rows, re)
            else:
                write(n1, rows, re * math.cos(turn) - im * math.sin(turn))


def flat(x):
    return x.reshape(x.shape[0] * x.shape[1], x.shape[2])


def start_all(copies):
    for copy in copies:
        copy.start()


def wait_all(copies):
    for copy in copies:
        copy.wait()


def parts_of(size, least=1):
    step = max(least, size // PARTS)
    return [pl.ds(k, step) for k in range(0, size, step)]


def plane(width):
    return lax.axis_index("context") // width


def copies_of(pairs, sem):
    return [pltpu.make_async_copy(src, dst, sem.at[i]) for i, (src, dst) in enumerate(pairs)]


def filter_kernel(
    first, n, channels, tokens, f_ref, tw_ref, fwd_ref, out_ref, f_buf, y_ref, own_ref, sem
):
    rows = parts_of(channels, ROWS)
    loads = copies_of(
        [(f_ref.at[pl.ds(first + part.start, part.size)], f_buf.at[part]) for part in rows],
        sem.at[0],
    )
    start_all(loads)
    for part, load in zip(rows, loads):
        load.wait()
        outer_forward(
            lambda n1, r: f_buf[r, n1 * tokens : (n1 + 1) * tokens], n, part, tokens, tw_ref, y_ref
        )
    stores = copies_of([(own_ref.at[ms], out_ref.at[ms]) for ms in parts_of(n)], sem.at[1])
    for ms, store in zip(parts_of(n), stores):
        own_ref[ms] = times_table(flat(y_ref[ms]), fwd_ref).reshape(ms.size, channels, 2 * tokens)
        store.start()
    wait_all(stores)


def transform(
    sign, n, channels, tokens, read, sources, targets, tw_ref, fwd_ref, inv_ref, spec_refs, own_ref,
    buf_ref, spec_buf, own_buf, y_ref, sem,
):
    half = channels // 2
    rows = [pl.ds(0, half), pl.ds(half, half)]
    loads = [copies_of(sources(part), sem.at[0, i]) for i, part in enumerate(rows)]
    for load in loads:
        start_all(load)
    spec_loads = [
        copies_of(
            [
                (ref.at[ms], spec_buf.at[ms, pl.ds(j * half, half)])
                for j, ref in enumerate(spec_refs)
            ],
            sem.at[1, i],
        )
        for i, ms in enumerate(parts_of(n))
    ]
    for load in spec_loads:
        start_all(load)
    for part, load in zip(rows, loads):
        wait_all(load)
        outer_forward(read, n, part, tokens, tw_ref, y_ref)
    own_stores = copies_of([(own_buf.at[ms], own_ref.at[ms]) for ms in parts_of(n)], sem.at[2, 0])
    for ms, load, store in zip(parts_of(n), spec_loads, own_stores):
        own = times_table(flat(y_ref[ms]), fwd_ref)
        own_buf[ms] = own.reshape(ms.size, channels, 2 * tokens)
        store.start()
        wait_all(load)
        spec = flat(spec_buf[ms])
        re, im = own[:, :tokens], own[:, tokens:]
        s_re, s_im = spec[:, :tokens], spec[:, tokens:] * sign
        both = jnp.concatenate([re * s_re - im * s_im, re * s_im + im * s_re], axis=1)
        y_ref[ms] = times_table(both, inv_ref).reshape(ms.size, channels, 2 * tokens)

    def write(n1, r, value):
        buf_ref[n1, r] = value

    stores = [copies_of(targets(part), sem.at[3, i]) for i, part in enumerate(rows)]
    for part, store in zip(rows, stores):
        outer_inverse(write, n, part, tokens, tw_ref, y_ref)
        start_all(store)
    for store in (*stores, own_stores):
        wait_all(store)


def conv_kernel(planes, n, channels, tokens, x_ref, *refs):
    tables, spec_refs, refs = refs[:3], refs[3:5], refs[5:]
    out_refs, (own_ref, *scratch) = refs[:planes], refs[planes:]
    buf_ref = scratch[0]
    width = n // planes
    z = plane(width)

    def block(d, part):
        return buf_ref.at[pl.ds((z ^ d) * width, width), part]

    def read(n1, r):
        return x_ref[n1 % width, z ^ (n1 // width), r]

    def sources(part):
        return []

    def targets(part):
        return [(block(d, part), out_refs[d].at[:, part]) for d in range(planes)]

    transform(
        1.0, n, channels, tokens, read, sources, targets, *tables, spec_refs, own_ref, *scratch
    )


def back_kernel(planes, n, channels, tokens, near_ref, *refs):
    far_refs, refs = refs[: planes - 1], refs[planes - 1 :]
    tables, spec_refs, refs = refs[:3], refs[3:5], refs[5:]
    after_ref, out_ref, own_ref, *scratch = refs
    buf_ref = scratch[0]
    width = n // planes
    z = plane(width)

    def block(z, part):
        return buf_ref.at[pl.ds(z * width, width), part]

    def sources(part):
        blocks = enumerate((near_ref, *far_refs))
        return [(ref.at[:, part], block(z ^ d, part)) for d, ref in blocks]

    def read(n1, r):
        return buf_ref[n1, r]

    def targets(part):
        return [(block(z, part), out_ref.at[:, z, part]) for z in range(planes)]

    transform(
        -1.0, n, channels, tokens, read, sources, targets, *tables, spec_refs, own_ref, *scratch
    )


def filter_grad_kernel(
    scale, n, channels, tokens, tw_ref, inv_ref, p_ref, g_ref, out_ref, p_buf, g_buf, y_ref, sem
):
    loads = [
        copies_of([(p_ref.at[ms], p_buf.at[ms]), (g_ref.at[ms], g_buf.at[ms])], sem.at[i])
        for i, ms in enumerate(parts_of(n))
    ]
    for load in loads:
        start_all(load)
    for ms, load in zip(parts_of(n), loads):
        wait_all(load)
        p, g = flat(p_buf[ms]), flat(g_buf[ms])
        p_re, p_im = p[:, :tokens], p[:, tokens:]
        re, im = g[:, :tokens], g[:, tokens:]
        both = jnp.concatenate([re * p_re + im * p_im, im * p_re - re * p_im], axis=1)
        y_ref[ms] = times_table(both, inv_ref).reshape(ms.size, channels, 2 * tokens)

    def write(n1, r, value):
        out_ref[r, n1 * tokens : (n1 + 1) * tokens] = value * scale

    outer_inverse(write, n, pl.ds(0, channels), tokens, tw_ref, y_ref)


def add_kernel(a_ref, b_ref, out_ref):
    out_ref[...] = a_ref[...] + b_ref[...]


def load_pairs(n, a_ref, b_ref, a_buf, b_buf, sem):
    loads = [
        copies_of([(a_ref.at[part], a_buf.at[part]), (b_ref.at[part], b_buf.at[part])], sem.at[i])
        for i, part in enumerate(parts_of(n))
    ]
    for load in loads:
        start_all(load)
    return loads


def product_split_kernel(planes, n, a_ref, b_ref, *refs):
    out_refs, (a_buf, b_buf, sem) = refs[:planes], refs[planes:]
    width = n // planes
    z = plane(width)
    for load in load_pairs(n, a_ref, b_ref, a_buf, b_buf, sem):
        wait_all(load)
    for d in range(planes):
        for q in range(width):
            out_refs[d][q] = a_buf[(z ^ d) * width + q] * b_buf[(z ^ d) * width + q]


def product_kernel(planes, n, a_ref, b_ref, after_ref, out_ref, a_buf, b_buf, buf_ref, sem):
    width = n // planes
    parts = [pl.ds(z * width, width) for z in range(planes)]
    loads = [
        copies_of([(a_ref.at[part], a_buf.at[part]), (b_ref.at[part], b_buf.at[part])], sem.at[z])
        for z, part in enumerate(parts)
    ]
    for load in loads:
        start_all(load)
    stores = copies_of([(buf_ref.at[z], out_ref.at[:, z]) for z in range(planes)], sem.at[planes])
    for z, part in enumerate(parts):
        wait_all(loads[z])
        buf_ref[z] = a_buf[part] * b_buf[part]
        stores[z].start()
    wait_all(stores)


def send_kernel(planes, width, x_ref, *refs):
    out_refs, sem = refs[:planes], refs[planes]
    z = plane(width)
    stores = copies_of([(x_ref.at[:, z ^ d], ref) for d, ref in enumerate(out_refs)], sem)
    start_all(stores)
    wait_all(stores)


def merge_kernel(planes, width, *refs):
    in_refs, (after_ref, out_ref, sem) = refs[:planes], refs[planes:]
    stores = copies_of([(ref, out_ref.at[:, d]) for d, ref in enumerate(in_refs)], sem)
    start_all(stores)
    wait_all(stores)


def gate_parts(width, blocks, a_ref, b_ref, outs, a_buf, b_buf, sem):
    stores = []
    for d, (read, first) in enumerate(blocks):
        part = pl.ds(first, width)
        x = read()
        a_buf[part] = x * a_ref[part]
        b_buf[part] = x * b_ref[part]
        pairs = [(buf.at[part], out.at[part]) for buf, out in zip((a_buf, b_buf), outs)]
        stores.extend(copies_of(pairs, sem.at[d]))
        start_all(stores[-2:])
    wait_all(stores)


def gate_kernel(
    planes, width, x_ref, a_ref, b_ref, oa_ref, ob_ref, x_buf, a_in, b_in, a_buf, b_buf, sem
):
    z = plane(width)
    loads = []
    for d in range(planes):
        part = pl.ds((z ^ d) * width, width)
        pairs = [
            (x_ref.at[:, d], x_buf.at[d]),
            (a_ref.at[part], a_in.at[part]),
            (b_ref.at[part], b_in.at[part]),
        ]
        loads.append(copies_of(pairs, sem.at[planes + d]))
        start_all(loads[-1])

    def read(d):
        wait_all(loads[d])
        return x_buf[d]

    blocks = [(lambda d=d: read(d), (z ^ d) * width) for d in range(planes)]
    gate_parts(width, blocks, a_in, b_in, (oa_ref, ob_ref), a_buf, b_buf, sem)


def gate_near_kernel(
    planes, width, near_ref, a_ref, b_ref, oa_ref, ob_ref, x_buf, a_buf, b_buf, sem
):
    part = pl.ds(plane(width) * width, width)
    loads = copies_of(
        [(near_ref, x_buf), (a_ref.at[part], a_buf), (b_ref.at[part], b_buf)], sem.at[0]
    )
    start_all(loads)
    wait_all(loads)
    a_buf[...] = x_buf[...] * a_buf[...]
    b_buf[...] = x_buf[...] * b_buf[...]
    stores = copies_of([(a_buf, oa_ref), (b_buf, ob_ref)], sem.at[1])
    start_all(stores)
    wait_all(stores)


def gate_far_kernel(planes, width, *refs):
    far_refs, refs = refs[: planes - 1], refs[planes - 1 :]
    a_ref, b_ref, done_a, done_b, after_ref, oa_ref, ob_ref, a_buf, b_buf, sem = refs
    z = plane(width)
    part = pl.ds(z * width, width)
    loads = copies_of([(done_a, a_buf.at[part]), (done_b, b_buf.at[part])], sem.at[0])
    start_all(loads)
    blocks = [(lambda d=d: far_refs[d - 1][...], (z ^ d) * width) for d in range(1, planes)]
    stores = []
    for d, (read, first) in enumerate(blocks, 1):
        rows = pl.ds(first, width)
        x = read()
        a_buf[rows] = x * a_ref[rows]
        b_buf[rows] = x * b_ref[rows]
        stores += copies_of([(a_buf.at[rows], oa_ref.at[rows]), (b_buf.at[rows], ob_ref.at[rows])], sem.at[d])
        start_all(stores[-2:])
    wait_all(loads)
    stores += copies_of(
        [(a_buf.at[part], oa_ref.at[part]), (b_buf.at[part], ob_ref.at[part])], sem.at[planes]
    )
    start_all(stores[-2:])
    wait_all(stores)


SPACES = {"v": pltpu.VMEM, "u": pltpu.VMEM, "h": pltpu.HBM, "a": pl.ANY}


def kernel_call(body, ins, outs, scratch, flops=0):
    shapes = [
        jax.ShapeDtypeStruct(shape, jnp.float32) if space == "u" else SPACES[space](shape, jnp.float32)
        for space, shape in outs
    ]

    def run(*args):
        args = [
            pltpu.with_memory_space_constraint(x, pltpu.HBM) if space == "h" else x
            for space, x in zip(ins, args, strict=True)
        ]
        size = sum(math.prod(x.shape) for x in (*args, *shapes))
        return pl.pallas_call(
            body,
            in_specs=[pl.BlockSpec(memory_space=SPACES[space]) for space in ins],
            out_specs=[pl.BlockSpec(memory_space=SPACES[space]) for space, _ in outs],
            out_shape=shapes,
            scratch_shapes=scratch,
            compiler_params=pltpu.CompilerParams(vmem_limit_bytes=VMEM_BYTES),
            cost_estimate=pl.CostEstimate(flops=flops, bytes_accessed=4 * size, transcendentals=0),
        )(*args)

    return run


def tables(n, tokens):
    length = n * tokens
    m = np.arange(n)[:, None] + 0.25
    angle = 2 * np.pi * m * np.arange(tokens)[None, :] / length
    tw = np.stack([np.cos(angle), np.sin(angle)])[:, :, None, :]
    tw = np.broadcast_to(tw, (2, n, ROWS, tokens)).astype(np.float32)
    k = np.arange(tokens)
    inner = 2 * np.pi * ((k[:, None] * k[None, :]) % tokens) / tokens
    c, s = np.cos(inner), np.sin(inner)

    def pair(table):
        hi = table.astype(ml_dtypes.bfloat16)
        lo = (table - hi.astype(np.float64)).astype(ml_dtypes.bfloat16)
        return jnp.asarray(np.concatenate([hi, hi, lo]))

    fwd = pair(np.block([[c, -s], [s, c]]))
    inv = pair(np.block([[c, s], [-s, c]]) / length)
    return jnp.asarray(tw), fwd, inv


def on_device(query_input, key_input, value_input, filters, cotangent):
    n = lax.axis_size("context")
    pair_size = lax.axis_size("dp")
    _, width, tokens = query_input.shape
    channels, length = filters.shape
    scale = 1.0 / math.sqrt(pair_size * length)
    sizes = (n, channels, tokens)
    tw, fwd, inv = tables(n, tokens)
    planes = math.gcd(n, PLANES)
    width = n // planes
    blocks, spectrum = (n, channels, tokens), (n, channels, 2 * tokens)
    one, paired, lags = (width, channels, tokens), (width, planes, channels, tokens), (channels, length)
    flops = 4 * 2 * 2 * tokens * n * channels * tokens
    f32 = jnp.float32
    y = pltpu.VMEM(spectrum, f32)

    def semaphores(*shape):
        return pltpu.SemaphoreType.DMA(shape)

    def part(body, *args):
        return lambda *refs: body(*args, *refs)

    def along_z(xs):
        return [
            lax.ppermute(x, "context", [(i, i ^ (d * width)) for i in range(n)])
            for d, x in enumerate(xs, 1)
        ]

    def within_plane(x):
        members = [[z * width + q for q in range(width)] for z in range(planes)]
        return lax.all_to_all(x, "context", 0, 0, axis_index_groups=members, tiled=True)

    query, key, value, cot = (
        x.reshape(blocks) for x in (query_input, key_input, value_input, cotangent)
    )
    rows, paired_buf = pltpu.VMEM(blocks, f32), pltpu.VMEM(paired, f32)
    by_plane = pltpu.VMEM((planes, *one), f32)
    send = kernel_call(
        part(send_kernel, planes, width), "v", [("h", one)] * planes, [semaphores(planes)]
    )
    merge = kernel_call(
        part(merge_kernel, planes, width), "v" * planes + "a", [("h", paired)], [semaphores(planes)]
    )
    half_sizes = (n, channels // 2, tokens)
    half_spectrum = (n, channels // 2, 2 * tokens)
    def transform_filters(first):
        return kernel_call(
            part(filter_kernel, first, *half_sizes), "hvv", [("h", half_spectrum)],
            [
                pltpu.VMEM((channels // 2, length), f32),
                *[pltpu.VMEM(half_spectrum, f32)] * 2,
                semaphores(2, PARTS),
            ],
            flops // 2,
        )(filters, tw, fwd)[0]

    transform_scratch = [rows, y, y, y, semaphores(4, PARTS, max(PARTS, planes))]
    always = lax.axis_index("context") < n

    def grouped(body, *args):
        shapes = jax.eval_shape(body, *args)

        def never(*args):
            return jax.tree.map(lambda x: jnp.zeros(x.shape, x.dtype), shapes)

        return lax.cond(always, body, never, *args)

    keep_p, *send_p = kernel_call(
        part(product_split_kernel, planes, n), "hh", [("u", one)] * planes,
        [rows, rows, semaphores(PARTS, 2)],
    )(key, value)
    got_p = along_z(send_p)

    def first(cot, query, keep_p):
        (conv_grad,) = kernel_call(
            part(product_kernel, planes, n), "hha", [("h", paired)],
            [rows, rows, by_plane, semaphores(planes + 1, planes)],
        )(cot, query, keep_p)
        return send(within_plane(conv_grad)), transform_filters(0)

    (near_g, *send_g), filt_a = grouped(first, cot, query, keep_p)
    far_g = along_z(send_g)

    def second(keep_p, got_p, send_g, filt_a):
        product_ch = within_plane(*merge(keep_p, *got_p, send_g))
        filt = (filt_a, transform_filters(channels // 2))
        *outs, prod_spec = kernel_call(
            part(conv_kernel, planes, *sizes), "vvvvhh",
            [("h", one)] * planes + [("h", spectrum)], transform_scratch, 2 * flops,
        )(product_ch, tw, fwd, inv, *filt)
        return outs, prod_spec, filt

    (keep_c, *send_c), prod_spec, filt = grouped(second, keep_p, got_p, send_g[0], filt_a)
    got_c = along_z(send_c)

    def third(near_g, far_g, filt, keep_c, prod_spec):
        back_ch, grad_spec = kernel_call(
            part(back_kernel, planes, *sizes), "a" * planes + "vvvhha",
            [("h", paired), ("h", spectrum)], transform_scratch, 2 * flops,
        )(near_g, *far_g, tw, fwd, inv, *filt, keep_c)
        sends = send(within_plane(back_ch))
        (own,) = kernel_call(
            part(filter_grad_kernel, scale, *sizes), "vvhh", [("u", lags)],
            [y, y, y, semaphores(PARTS, 2)], flops,
        )(tw, inv, prod_spec, grad_spec)
        return sends, own

    (near_b, *send_b), own = grouped(third, near_g, far_g, filt, keep_c, prod_spec)
    far_b = along_z(send_b)

    def fourth(keep_c, got_c, query, cot, near_b, value, key, own):
        if pair_size == 2:
            other = lax.ppermute(own, "dp", [(0, 1), (1, 0)])
        else:
            other = lax.psum(own, "dp") - own
        conv_tok = within_plane(*merge(keep_c, *got_c, near_b))
        (grad_filter,) = kernel_call(add_kernel, "vv", [("u", lags)], [])(own, other)
        begun = kernel_call(
            part(gate_near_kernel, planes, width), "ahh", [("h", one)] * 2,
            [pltpu.VMEM(one, f32)] * 3 + [semaphores(2, 3)],
        )(near_b, value, key)
        gated, grad_query = kernel_call(
            part(gate_kernel, planes, width), "ahh", [("h", blocks)] * 2,
            [by_plane, *[rows] * 4, semaphores(2 * planes, 3)],
        )(conv_tok, query, cot)
        return gated, grad_query, begun, grad_filter

    gated, grad_query, begun, grad_filter = grouped(
        fourth, keep_c, got_c, query, cot, near_b, value, key, own
    )
    grad_key, grad_value = kernel_call(
        part(gate_far_kernel, planes, width), "v" * (planes + 1) + "aaa", [("h", blocks)] * 2,
        [rows, rows, semaphores(planes + 1, 2)],
    )(*far_b, value, key, *begun, gated)
    shape = query_input.shape
    return (
        gated.reshape(shape),
        grad_query.reshape(shape),
        grad_key.reshape(shape),
        grad_value.reshape(shape),
        grad_filter,
    )


def solution(mesh):
    in_specs = (
        P("dp", None, "context"),
        P("dp", None, "context"),
        P("dp", None, "context"),
        P("context", None),
        P("dp", None, "context"),
    )
    out_specs = (
        P("dp", None, "context"),
        P("dp", None, "context"),
        P("dp", None, "context"),
        P("dp", None, "context"),
        P("context", None),
    )
    return jax.shard_map(
        on_device, mesh=mesh, in_specs=in_specs, out_specs=out_specs, check_vma=False
    )
```

```python
import math

import jax
import jax.numpy as jnp
import ml_dtypes
import numpy as np
from jax import lax
from jax.experimental import pallas as pl
from jax.experimental.pallas import tpu as pltpu
from jax.sharding import PartitionSpec as P

ROWS = 8
PLANES = 4
PARTS = 4
VMEM_BYTES = 24 * 1024 * 1024


def twist(value, turn):
    re, im = value
    turn = turn % 1.0
    if turn == 0.0:
        return re, im
    if turn == 0.25:
        return im, -re
    if turn == 0.5:
        return -re, -im
    if turn == 0.75:
        return -im, re
    if turn in (0.125, 0.375, 0.625, 0.875):
        half = math.sqrt(0.5)
        a, b = (re + im) * half, (im - re) * half
        return twist((a, b), turn - 0.125)
    c, s = math.cos(2 * math.pi * turn), math.sin(2 * math.pi * turn)
    return re * c + im * s, im * c - re * s


def dft(values, sign):
    n = len(values)
    if n == 1:
        return values
    even, odd = dft(values[0::2], sign), dft(values[1::2], sign)
    out = [None] * n
    for k in range(n // 2):
        a, b = even[k], twist(odd[k], sign * k / n)
        out[k] = (a[0] + b[0], a[1] + b[1])
        out[k + n // 2] = (a[0] - b[0], a[1] - b[1])
    return out


def times_table(x, table_ref):
    hi = x.astype(jnp.bfloat16)
    lo = (x - hi.astype(jnp.float32)).astype(jnp.bfloat16)
    return jnp.dot(
        jnp.concatenate([hi, lo, hi], axis=1), table_ref[...], preferred_element_type=jnp.float32
    )


def outer_forward(read, n, part, tokens, tw_ref, y_ref):
    @pl.loop(part.start // ROWS, (part.start + part.size) // ROWS)
    def _(r):
        rows = pl.ds(pl.multiple_of(r * ROWS, ROWS), ROWS)
        values = []
        for n1 in range(n):
            x = read(n1, rows)
            turn = 2 * math.pi * n1 / (4 * n)
            if n1 == 0:
                values.append((x, jnp.zeros_like(x)))
            else:
                values.append((x * math.cos(turn), x * -math.sin(turn)))
        for m, (re, im) in enumerate(dft(values, 1)):
            c, s = tw_ref[0, m], tw_ref[1, m]
            y_ref[m, rows, :tokens] = re * c + im * s
            y_ref[m, rows, tokens:] = im * c - re * s


def outer_inverse(write, n, part, tokens, tw_ref, y_ref):
    @pl.loop(part.start // ROWS, (part.start + part.size) // ROWS)
    def _(r):
        rows = pl.ds(pl.multiple_of(r * ROWS, ROWS), ROWS)
        values = []
        for m in range(n):
            re, im = y_ref[m, rows, :tokens], y_ref[m, rows, tokens:]
            c, s = tw_ref[0, m], tw_ref[1, m]
            values.append((re * c - im * s, im * c + re * s))
        for n1, (re, im) in enumerate(dft(values, -1)):
            turn = 2 * math.pi * n1 / (4 * n)
            if n1 == 0:
                write(n1, rows, re)
            else:
                write(n1, rows, re * math.cos(turn) - im * math.sin(turn))


def flat(x):
    return x.reshape(x.shape[0] * x.shape[1], x.shape[2])


def start_all(copies):
    for copy in copies:
        copy.start()


def wait_all(copies):
    for copy in copies:
        copy.wait()


def parts_of(size, least=1):
    step = max(least, size // PARTS)
    return [pl.ds(k, step) for k in range(0, size, step)]


def plane(width):
    return lax.axis_index("context") // width


def copies_of(pairs, sem):
    return [pltpu.make_async_copy(src, dst, sem.at[i]) for i, (src, dst) in enumerate(pairs)]


def filter_kernel(
    first, n, channels, tokens, f_ref, tw_ref, fwd_ref, out_ref, f_buf, y_ref, own_ref, sem
):
    rows = parts_of(channels, ROWS)
    loads = copies_of(
        [(f_ref.at[pl.ds(first + part.start, part.size)], f_buf.at[part]) for part in rows],
        sem.at[0],
    )
    start_all(loads)
    for part, load in zip(rows, loads):
        load.wait()
        outer_forward(
            lambda n1, r: f_buf[r, n1 * tokens : (n1 + 1) * tokens], n, part, tokens, tw_ref, y_ref
        )
    stores = copies_of([(own_ref.at[ms], out_ref.at[ms]) for ms in parts_of(n)], sem.at[1])
    for ms, store in zip(parts_of(n), stores):
        own_ref[ms] = times_table(flat(y_ref[ms]), fwd_ref).reshape(ms.size, channels, 2 * tokens)
        store.start()
    wait_all(stores)


def transform(
    sign, n, channels, tokens, read, sources, targets, tw_ref, fwd_hbm, inv_hbm, spec_refs, own_ref,
    buf_ref, spec_buf, own_buf, y_ref, fwd_ref, inv_ref, sem,
):
    half = channels // 2
    rows = [pl.ds(0, half), pl.ds(half, half)]
    loads = [copies_of(sources(part), sem.at[0, i]) for i, part in enumerate(rows)]
    for load in loads:
        start_all(load)
    table_loads = copies_of([(fwd_hbm, fwd_ref), (inv_hbm, inv_ref)], sem.at[2, 1])
    start_all(table_loads)
    spec_loads = [
        copies_of(
            [
                (ref.at[ms], spec_buf.at[ms, pl.ds(j * half, half)])
                for j, ref in enumerate(spec_refs)
            ],
            sem.at[1, i],
        )
        for i, ms in enumerate(parts_of(n))
    ]
    for load in spec_loads:
        start_all(load)
    for part, load in zip(rows, loads):
        wait_all(load)
        outer_forward(read, n, part, tokens, tw_ref, y_ref)
    own_stores = copies_of([(own_buf.at[ms], own_ref.at[ms]) for ms in parts_of(n)], sem.at[2, 0])
    wait_all(table_loads)
    for ms, load, store in zip(parts_of(n), spec_loads, own_stores):
        own = times_table(flat(y_ref[ms]), fwd_ref)
        own_buf[ms] = own.reshape(ms.size, channels, 2 * tokens)
        store.start()
        wait_all(load)
        spec = flat(spec_buf[ms])
        re, im = own[:, :tokens], own[:, tokens:]
        s_re, s_im = spec[:, :tokens], spec[:, tokens:] * sign
        both = jnp.concatenate([re * s_re - im * s_im, re * s_im + im * s_re], axis=1)
        y_ref[ms] = times_table(both, inv_ref).reshape(ms.size, channels, 2 * tokens)

    def write(n1, r, value):
        buf_ref[n1, r] = value

    stores = [copies_of(targets(part), sem.at[3, i]) for i, part in enumerate(rows)]
    for part, store in zip(rows, stores):
        outer_inverse(write, n, part, tokens, tw_ref, y_ref)
        start_all(store)
    for store in (*stores, own_stores):
        wait_all(store)


def conv_kernel(planes, n, channels, tokens, x_ref, *refs):
    tables, spec_refs, refs = refs[:3], refs[3:5], refs[5:]
    out_refs, (own_ref, *scratch) = refs[:planes], refs[planes:]
    buf_ref = scratch[0]
    width = n // planes
    z = plane(width)

    def block(d, part):
        return buf_ref.at[pl.ds((z ^ d) * width, width), part]

    def read(n1, r):
        return x_ref[n1 % width, z ^ (n1 // width), r]

    def sources(part):
        return []

    def targets(part):
        return [(block(d, part), out_refs[d].at[:, part]) for d in range(planes)]

    transform(
        1.0, n, channels, tokens, read, sources, targets, *tables, spec_refs, own_ref, *scratch
    )


def back_kernel(planes, n, channels, tokens, near_ref, *refs):
    far_refs, refs = refs[: planes - 1], refs[planes - 1 :]
    tables, spec_refs, refs = refs[:3], refs[3:5], refs[5:]
    after_ref, out_ref, own_ref, *scratch = refs
    buf_ref = scratch[0]
    width = n // planes
    z = plane(width)

    def block(z, part):
        return buf_ref.at[pl.ds(z * width, width), part]

    def sources(part):
        blocks = enumerate((near_ref, *far_refs))
        return [(ref.at[:, part], block(z ^ d, part)) for d, ref in blocks]

    def read(n1, r):
        return buf_ref[n1, r]

    def targets(part):
        return [(block(z, part), out_ref.at[:, z, part]) for z in range(planes)]

    transform(
        -1.0, n, channels, tokens, read, sources, targets, *tables, spec_refs, own_ref, *scratch
    )


def filter_grad_kernel(
    scale, n, channels, tokens, tw_ref, inv_ref, p_ref, g_ref, out_ref,
    p_buf, g_buf, y_ref, out_buf, sem,
):
    loads = [
        copies_of([(p_ref.at[ms], p_buf.at[ms]), (g_ref.at[ms], g_buf.at[ms])], sem.at[i])
        for i, ms in enumerate(parts_of(n))
    ]
    for load in loads:
        start_all(load)
    for ms, load in zip(parts_of(n), loads):
        wait_all(load)
        p, g = flat(p_buf[ms]), flat(g_buf[ms])
        p_re, p_im = p[:, :tokens], p[:, tokens:]
        re, im = g[:, :tokens], g[:, tokens:]
        both = jnp.concatenate([re * p_re + im * p_im, im * p_re - re * p_im], axis=1)
        y_ref[ms] = times_table(both, inv_ref).reshape(ms.size, channels, 2 * tokens)

    def write(n1, r, value):
        out_buf[r, n1 * tokens : (n1 + 1) * tokens] = value * scale

    rows = parts_of(channels, ROWS)
    stores = copies_of([(out_buf.at[part], out_ref.at[part]) for part in rows], sem.at[PARTS])
    for part, store in zip(rows, stores):
        outer_inverse(write, n, part, tokens, tw_ref, y_ref)
        store.start()
    wait_all(stores)


def load_pairs(n, a_ref, b_ref, a_buf, b_buf, sem):
    loads = [
        copies_of([(a_ref.at[part], a_buf.at[part]), (b_ref.at[part], b_buf.at[part])], sem.at[i])
        for i, part in enumerate(parts_of(n))
    ]
    for load in loads:
        start_all(load)
    return loads


def product_split_kernel(planes, n, a_ref, b_ref, *refs):
    out_refs, (a_buf, b_buf, sem) = refs[:planes], refs[planes:]
    width = n // planes
    z = plane(width)
    for load in load_pairs(n, a_ref, b_ref, a_buf, b_buf, sem):
        wait_all(load)
    for d in range(planes):
        for q in range(width):
            out_refs[d][q] = a_buf[(z ^ d) * width + q] * b_buf[(z ^ d) * width + q]


def product_kernel(planes, n, a_ref, b_ref, after_ref, out_ref, a_buf, b_buf, buf_ref, sem):
    width = n // planes
    parts = [pl.ds(z * width, width) for z in range(planes)]
    loads = [
        copies_of([(a_ref.at[part], a_buf.at[part]), (b_ref.at[part], b_buf.at[part])], sem.at[z])
        for z, part in enumerate(parts)
    ]
    for load in loads:
        start_all(load)
    stores = copies_of([(buf_ref.at[z], out_ref.at[:, z]) for z in range(planes)], sem.at[planes])
    for z, part in enumerate(parts):
        wait_all(loads[z])
        buf_ref[z] = a_buf[part] * b_buf[part]
        stores[z].start()
    wait_all(stores)


def send_kernel(planes, width, x_ref, *refs):
    out_refs, sem = refs[:planes], refs[planes]
    z = plane(width)
    stores = copies_of([(x_ref.at[:, z ^ d], ref) for d, ref in enumerate(out_refs)], sem)
    start_all(stores)
    wait_all(stores)


def merge_kernel(planes, width, *refs):
    in_refs, (after_ref, out_ref, sem) = refs[:planes], refs[planes:]
    stores = copies_of([(ref, out_ref.at[:, d]) for d, ref in enumerate(in_refs)], sem)
    start_all(stores)
    wait_all(stores)


def gate_parts(width, blocks, a_ref, b_ref, outs, a_buf, b_buf, sem):
    stores = []
    for d, (read, first) in enumerate(blocks):
        part = pl.ds(first, width)
        x = read()
        a_buf[part] = x * a_ref[part]
        b_buf[part] = x * b_ref[part]
        pairs = [(buf.at[part], out.at[part]) for buf, out in zip((a_buf, b_buf), outs)]
        stores.extend(copies_of(pairs, sem.at[d]))
        start_all(stores[-2:])
    wait_all(stores)


def gate_kernel(
    planes, width, x_ref, a_ref, b_ref, oa_ref, ob_ref, x_buf, a_in, b_in, a_buf, b_buf, sem
):
    z = plane(width)
    loads = []
    for d in range(planes):
        part = pl.ds((z ^ d) * width, width)
        pairs = [
            (x_ref.at[:, d], x_buf.at[d]),
            (a_ref.at[part], a_in.at[part]),
            (b_ref.at[part], b_in.at[part]),
        ]
        loads.append(copies_of(pairs, sem.at[planes + d]))
        start_all(loads[-1])

    def read(d):
        wait_all(loads[d])
        return x_buf[d]

    blocks = [(lambda d=d: read(d), (z ^ d) * width) for d in range(planes)]
    gate_parts(width, blocks, a_in, b_in, (oa_ref, ob_ref), a_buf, b_buf, sem)


def gate_near_kernel(
    planes, width, near_ref, a_ref, b_ref, oa_ref, ob_ref, x_buf, a_buf, b_buf, sem
):
    part = pl.ds(plane(width) * width, width)
    loads = copies_of(
        [(near_ref, x_buf), (a_ref.at[part], a_buf), (b_ref.at[part], b_buf)], sem.at[0]
    )
    start_all(loads)
    wait_all(loads)
    a_buf[...] = x_buf[...] * a_buf[...]
    b_buf[...] = x_buf[...] * b_buf[...]
    stores = copies_of([(a_buf, oa_ref), (b_buf, ob_ref)], sem.at[1])
    start_all(stores)
    wait_all(stores)


def gate_far_kernel(planes, width, *refs):
    far_refs, refs = refs[: planes - 1], refs[planes - 1 :]
    a_ref, b_ref, done_a, done_b, oa_ref, ob_ref, a_buf, b_buf, sem = refs
    z = plane(width)
    rows = pl.ds(z * width, width)
    stores = copies_of([(done_a, oa_ref.at[rows]), (done_b, ob_ref.at[rows])], sem.at[0])
    start_all(stores)
    for d, far_ref in enumerate(far_refs, 1):
        rows = pl.ds((z ^ d) * width, width)
        x = far_ref[...]
        a_buf[rows] = x * a_ref[rows]
        b_buf[rows] = x * b_ref[rows]
        stores += copies_of([(a_buf.at[rows], oa_ref.at[rows]), (b_buf.at[rows], ob_ref.at[rows])], sem.at[d])
        start_all(stores[-2:])
    wait_all(stores)


SPACES = {"v": pltpu.VMEM, "u": pltpu.VMEM, "h": pltpu.HBM, "a": pl.ANY}


def kernel_call(body, ins, outs, scratch, flops=0):
    shapes = [
        jax.ShapeDtypeStruct(shape, jnp.float32) if space == "u" else SPACES[space](shape, jnp.float32)
        for space, shape in outs
    ]

    def run(*args):
        args = [
            pltpu.with_memory_space_constraint(x, pltpu.HBM) if space == "h" else x
            for space, x in zip(ins, args, strict=True)
        ]
        size = sum(math.prod(x.shape) for x in (*args, *shapes))
        return pl.pallas_call(
            body,
            in_specs=[pl.BlockSpec(memory_space=SPACES[space]) for space in ins],
            out_specs=[pl.BlockSpec(memory_space=SPACES[space]) for space, _ in outs],
            out_shape=shapes,
            scratch_shapes=scratch,
            compiler_params=pltpu.CompilerParams(vmem_limit_bytes=VMEM_BYTES),
            cost_estimate=pl.CostEstimate(flops=flops, bytes_accessed=4 * size, transcendentals=0),
        )(*args)

    return run


def tables(n, tokens):
    length = n * tokens
    m = np.arange(n)[:, None] + 0.25
    angle = 2 * np.pi * m * np.arange(tokens)[None, :] / length
    tw = np.stack([np.cos(angle), np.sin(angle)])[:, :, None, :]
    tw = np.broadcast_to(tw, (2, n, ROWS, tokens)).astype(np.float32)
    k = np.arange(tokens)
    inner = 2 * np.pi * ((k[:, None] * k[None, :]) % tokens) / tokens
    c, s = np.cos(inner), np.sin(inner)

    def pair(table):
        hi = table.astype(ml_dtypes.bfloat16)
        lo = (table - hi.astype(np.float64)).astype(ml_dtypes.bfloat16)
        return jnp.asarray(np.concatenate([hi, hi, lo]))

    fwd = pair(np.block([[c, -s], [s, c]]))
    inv = pair(np.block([[c, s], [-s, c]]) / length)
    return jnp.asarray(tw), fwd, inv


def on_device(query_input, key_input, value_input, filters, cotangent):
    n = lax.axis_size("context")
    pair_size = lax.axis_size("dp")
    _, width, tokens = query_input.shape
    channels, length = filters.shape
    scale = 1.0 / math.sqrt(pair_size * length)
    sizes = (n, channels, tokens)
    tw, fwd, inv = tables(n, tokens)
    planes = math.gcd(n, PLANES)
    width = n // planes
    blocks, spectrum = (n, channels, tokens), (n, channels, 2 * tokens)
    one, paired, lags = (width, channels, tokens), (width, planes, channels, tokens), (channels, length)
    flops = 4 * 2 * 2 * tokens * n * channels * tokens
    f32 = jnp.float32
    y = pltpu.VMEM(spectrum, f32)

    def semaphores(*shape):
        return pltpu.SemaphoreType.DMA(shape)

    def part(body, *args):
        return lambda *refs: body(*args, *refs)

    def along_z(xs):
        return [
            lax.ppermute(x, "context", [(i, i ^ (d * width)) for i in range(n)])
            for d, x in enumerate(xs, 1)
        ]

    def within_plane(x):
        members = [[z * width + q for q in range(width)] for z in range(planes)]
        return lax.all_to_all(x, "context", 0, 0, axis_index_groups=members, tiled=True)

    query, key, value, cot = (
        x.reshape(blocks) for x in (query_input, key_input, value_input, cotangent)
    )
    rows, paired_buf = pltpu.VMEM(blocks, f32), pltpu.VMEM(paired, f32)
    by_plane = pltpu.VMEM((planes, *one), f32)
    send = kernel_call(
        part(send_kernel, planes, width), "v", [("h", one)] * planes, [semaphores(planes)]
    )
    merge = kernel_call(
        part(merge_kernel, planes, width), "v" * planes + "a", [("h", paired)], [semaphores(planes)]
    )
    half_sizes = (n, channels // 2, tokens)
    half_spectrum = (n, channels // 2, 2 * tokens)
    def transform_filters(first):
        return kernel_call(
            part(filter_kernel, first, *half_sizes), "hvv", [("h", half_spectrum)],
            [
                pltpu.VMEM((channels // 2, length), f32),
                *[pltpu.VMEM(half_spectrum, f32)] * 2,
                semaphores(2, PARTS),
            ],
            flops // 2,
        )(filters, tw, fwd)[0]

    table = pltpu.VMEM(fwd.shape, fwd.dtype)
    transform_scratch = [rows, y, y, y, table, table, semaphores(4, PARTS, max(PARTS, planes))]
    always = lax.axis_index("context") < n

    def grouped(body, *args):
        shapes = jax.eval_shape(body, *args)

        def never(*args):
            return jax.tree.map(lambda x: jnp.zeros(x.shape, x.dtype), shapes)

        return lax.cond(always, body, never, *args)

    keep_p, *send_p = kernel_call(
        part(product_split_kernel, planes, n), "hh", [("u", one)] + [("v", one)] * (planes - 1),
        [rows, rows, semaphores(PARTS, 2)],
    )(key, value)
    got_p = along_z(send_p)

    def first(cot, query, keep_p):
        (conv_grad,) = kernel_call(
            part(product_kernel, planes, n), "hha", [("h", paired)],
            [rows, rows, by_plane, semaphores(planes + 1, planes)],
        )(cot, query, keep_p)
        return send(within_plane(conv_grad)), transform_filters(0)

    (near_g, *send_g), filt_a = grouped(first, cot, query, keep_p)
    far_g = along_z(send_g)

    def second(keep_p, got_p, send_g, filt_a):
        product_ch = within_plane(*merge(keep_p, *got_p, send_g))
        filt = (filt_a, transform_filters(channels // 2))
        *outs, prod_spec = kernel_call(
            part(conv_kernel, planes, *sizes), "vvhhhh",
            [("h", one)] * planes + [("h", spectrum)], transform_scratch, 2 * flops,
        )(product_ch, tw, fwd, inv, *filt)
        return outs, prod_spec, filt

    (keep_c, *send_c), prod_spec, filt = grouped(second, keep_p, got_p, send_g[0], filt_a)
    got_c = along_z(send_c)

    def third(near_g, far_g, filt, keep_c, prod_spec):
        back_ch, grad_spec = kernel_call(
            part(back_kernel, planes, *sizes), "a" * planes + "vhhhha",
            [("h", paired), ("h", spectrum)], transform_scratch, 2 * flops,
        )(near_g, *far_g, tw, fwd, inv, *filt, keep_c)
        sends = send(within_plane(back_ch))
        (own,) = kernel_call(
            part(filter_grad_kernel, scale, *sizes), "vvhh", [("h", lags)],
            [y, y, y, pltpu.VMEM(lags, f32), semaphores(PARTS + 1, PARTS)], flops,
        )(tw, inv, prod_spec, grad_spec)
        return sends, own

    (near_b, *send_b), own = grouped(third, near_g, far_g, filt, keep_c, prod_spec)
    far_b = along_z(send_b)

    def fourth(keep_c, got_c, query, cot, near_b, value, key, own):
        if pair_size == 2:
            grad_filter = own + lax.ppermute(own, "dp", [(0, 1), (1, 0)])
        else:
            grad_filter = lax.psum(own, "dp")
        conv_tok = within_plane(*merge(keep_c, *got_c, near_b))
        begun = kernel_call(
            part(gate_near_kernel, planes, width), "ahh", [("h", one)] * 2,
            [pltpu.VMEM(one, f32)] * 3 + [semaphores(2, 3)],
        )(near_b, value, key)
        gated, grad_query = kernel_call(
            part(gate_kernel, planes, width), "ahh", [("h", blocks)] * 2,
            [by_plane, *[rows] * 4, semaphores(2 * planes, 3)],
        )(conv_tok, query, cot)
        return gated, grad_query, begun, grad_filter

    gated, grad_query, begun, grad_filter = grouped(
        fourth, keep_c, got_c, query, cot, near_b, value, key, own
    )
    grad_key, grad_value = kernel_call(
        part(gate_far_kernel, planes, width), "v" * (planes + 3), [("h", blocks)] * 2,
        [rows, rows, semaphores(planes, 2)],
    )(*far_b, value, key, *begun)
    shape = query_input.shape
    return (
        gated.reshape(shape),
        grad_query.reshape(shape),
        grad_key.reshape(shape),
        grad_value.reshape(shape),
        grad_filter,
    )


def solution(mesh):
    in_specs = (
        P("dp", None, "context"),
        P("dp", None, "context"),
        P("dp", None, "context"),
        P("context", None),
        P("dp", None, "context"),
    )
    out_specs = (
        P("dp", None, "context"),
        P("dp", None, "context"),
        P("dp", None, "context"),
        P("dp", None, "context"),
        P("context", None),
    )
    return jax.shard_map(
        on_device, mesh=mesh, in_specs=in_specs, out_specs=out_specs, check_vma=False
    )
```

```python
import math

import jax
import jax.numpy as jnp
import ml_dtypes
import numpy as np
from jax import lax
from jax.experimental import pallas as pl
from jax.experimental.pallas import tpu as pltpu
from jax.sharding import PartitionSpec as P

ROWS = 8
PLANES = 4
PARTS = 4
VMEM_BYTES = 16 * 1024 * 1024


def twist(value, turn):
    re, im = value
    turn = turn % 1.0
    if turn == 0.0:
        return re, im
    if turn == 0.25:
        return im, -re
    if turn == 0.5:
        return -re, -im
    if turn == 0.75:
        return -im, re
    if turn in (0.125, 0.375, 0.625, 0.875):
        half = math.sqrt(0.5)
        a, b = (re + im) * half, (im - re) * half
        return twist((a, b), turn - 0.125)
    c, s = math.cos(2 * math.pi * turn), math.sin(2 * math.pi * turn)
    return re * c + im * s, im * c - re * s


def dft(values, sign):
    n = len(values)
    if n == 1:
        return values
    even, odd = dft(values[0::2], sign), dft(values[1::2], sign)
    out = [None] * n
    for k in range(n // 2):
        a, b = even[k], twist(odd[k], sign * k / n)
        out[k] = (a[0] + b[0], a[1] + b[1])
        out[k + n // 2] = (a[0] - b[0], a[1] - b[1])
    return out


def times_table(x, table_ref):
    hi = x.astype(jnp.bfloat16)
    lo = (x - hi.astype(jnp.float32)).astype(jnp.bfloat16)
    return jnp.dot(
        jnp.concatenate([hi, lo, hi], axis=1), table_ref[...], preferred_element_type=jnp.float32
    )


def outer_forward(read, n, part, tokens, tw_ref, y_ref):
    @pl.loop(part.start // ROWS, (part.start + part.size) // ROWS)
    def _(r):
        rows = pl.ds(pl.multiple_of(r * ROWS, ROWS), ROWS)
        values = []
        for n1 in range(n):
            x = read(n1, rows)
            turn = 2 * math.pi * n1 / (4 * n)
            if n1 == 0:
                values.append((x, jnp.zeros_like(x)))
            else:
                values.append((x * math.cos(turn), x * -math.sin(turn)))
        for m, (re, im) in enumerate(dft(values, 1)):
            c, s = tw_ref[0, m], tw_ref[1, m]
            y_ref[m, rows, :tokens] = re * c + im * s
            y_ref[m, rows, tokens:] = im * c - re * s


def outer_inverse(write, n, part, tokens, tw_ref, y_ref):
    @pl.loop(part.start // ROWS, (part.start + part.size) // ROWS)
    def _(r):
        rows = pl.ds(pl.multiple_of(r * ROWS, ROWS), ROWS)
        values = []
        for m in range(n):
            re, im = y_ref[m, rows, :tokens], y_ref[m, rows, tokens:]
            c, s = tw_ref[0, m], tw_ref[1, m]
            values.append((re * c - im * s, im * c + re * s))
        for n1, (re, im) in enumerate(dft(values, -1)):
            turn = 2 * math.pi * n1 / (4 * n)
            if n1 == 0:
                write(n1, rows, re)
            else:
                write(n1, rows, re * math.cos(turn) - im * math.sin(turn))


def flat(x):
    return x.reshape(x.shape[0] * x.shape[1], x.shape[2])


def start_all(copies):
    for copy in copies:
        copy.start()


def wait_all(copies):
    for copy in copies:
        copy.wait()


def parts_of(size, least=1):
    step = max(least, size // PARTS)
    return [pl.ds(k, step) for k in range(0, size, step)]


def plane(width):
    return lax.axis_index("context") // width


def copies_of(pairs, sem):
    return [pltpu.make_async_copy(src, dst, sem.at[i]) for i, (src, dst) in enumerate(pairs)]


def filter_kernel(
    first, n, channels, tokens, f_ref, tw_ref, fwd_ref, out_ref, f_buf, y_ref, own_ref, sem
):
    rows = parts_of(channels, ROWS)
    loads = copies_of(
        [(f_ref.at[pl.ds(first + part.start, part.size)], f_buf.at[part]) for part in rows],
        sem.at[0],
    )
    start_all(loads)
    for part, load in zip(rows, loads):
        load.wait()
        outer_forward(
            lambda n1, r: f_buf[r, n1 * tokens : (n1 + 1) * tokens], n, part, tokens, tw_ref, y_ref
        )
    stores = copies_of([(own_ref.at[ms], out_ref.at[ms]) for ms in parts_of(n)], sem.at[1])
    for ms, store in zip(parts_of(n), stores):
        own_ref[ms] = times_table(flat(y_ref[ms]), fwd_ref).reshape(ms.size, channels, 2 * tokens)
        store.start()
    wait_all(stores)


def transform(
    sign, n, channels, tokens, read, sources, targets, tw_ref, fwd_hbm, inv_hbm, spec_refs, own_ref,
    buf_ref, spec_buf, own_buf, y_ref, fwd_ref, inv_ref, sem,
):
    half = channels // 2
    rows = [pl.ds(0, half), pl.ds(half, half)]
    loads = [copies_of(sources(part), sem.at[0, i]) for i, part in enumerate(rows)]
    for load in loads:
        start_all(load)
    table_loads = copies_of([(fwd_hbm, fwd_ref), (inv_hbm, inv_ref)], sem.at[2, 1])
    start_all(table_loads)
    spec_loads = [
        copies_of(
            [
                (ref.at[ms], spec_buf.at[ms, pl.ds(j * half, half)])
                for j, ref in enumerate(spec_refs)
            ],
            sem.at[1, i],
        )
        for i, ms in enumerate(parts_of(n))
    ]
    for load in spec_loads:
        start_all(load)
    for part, load in zip(rows, loads):
        wait_all(load)
        outer_forward(read, n, part, tokens, tw_ref, y_ref)
    own_stores = copies_of([(own_buf.at[ms], own_ref.at[ms]) for ms in parts_of(n)], sem.at[2, 0])
    wait_all(table_loads)
    for ms, load, store in zip(parts_of(n), spec_loads, own_stores):
        own = times_table(flat(y_ref[ms]), fwd_ref)
        own_buf[ms] = own.reshape(ms.size, channels, 2 * tokens)
        store.start()
        wait_all(load)
        spec = flat(spec_buf[ms])
        re, im = own[:, :tokens], own[:, tokens:]
        s_re, s_im = spec[:, :tokens], spec[:, tokens:] * sign
        both = jnp.concatenate([re * s_re - im * s_im, re * s_im + im * s_re], axis=1)
        y_ref[ms] = times_table(both, inv_ref).reshape(ms.size, channels, 2 * tokens)

    def write(n1, r, value):
        buf_ref[n1, r] = value

    stores = [copies_of(targets(part), sem.at[3, i]) for i, part in enumerate(rows)]
    for part, store in zip(rows, stores):
        outer_inverse(write, n, part, tokens, tw_ref, y_ref)
        start_all(store)
    for store in (*stores, own_stores):
        wait_all(store)


def conv_kernel(planes, n, channels, tokens, x_ref, *refs):
    tables, spec_refs, refs = refs[:3], refs[3:5], refs[5:]
    out_refs, (own_ref, *scratch) = refs[:planes], refs[planes:]
    buf_ref = scratch[0]
    width = n // planes
    z = plane(width)

    def block(d, part):
        return buf_ref.at[pl.ds((z ^ d) * width, width), part]

    def read(n1, r):
        return x_ref[n1 % width, z ^ (n1 // width), r]

    def sources(part):
        return []

    def targets(part):
        return [(block(d, part), out_refs[d].at[:, part]) for d in range(planes)]

    transform(
        1.0, n, channels, tokens, read, sources, targets, *tables, spec_refs, own_ref, *scratch
    )


def back_kernel(planes, n, channels, tokens, near_ref, *refs):
    far_refs, refs = refs[: planes - 1], refs[planes - 1 :]
    tables, spec_refs, refs = refs[:3], refs[3:5], refs[5:]
    after_ref, out_ref, own_ref, *scratch = refs
    buf_ref = scratch[0]
    width = n // planes
    z = plane(width)

    def block(z, part):
        return buf_ref.at[pl.ds(z * width, width), part]

    def sources(part):
        blocks = enumerate((near_ref, *far_refs))
        return [(ref.at[:, part], block(z ^ d, part)) for d, ref in blocks]

    def read(n1, r):
        return buf_ref[n1, r]

    def targets(part):
        return [(block(z, part), out_ref.at[:, z, part]) for z in range(planes)]

    transform(
        -1.0, n, channels, tokens, read, sources, targets, *tables, spec_refs, own_ref, *scratch
    )


def filter_grad_kernel(
    scale, n, channels, tokens, tw_ref, inv_ref, p_ref, g_ref, out_ref,
    p_buf, g_buf, y_ref, out_buf, sem,
):
    loads = [
        copies_of([(p_ref.at[ms], p_buf.at[ms]), (g_ref.at[ms], g_buf.at[ms])], sem.at[i])
        for i, ms in enumerate(parts_of(n))
    ]
    for load in loads:
        start_all(load)
    for ms, load in zip(parts_of(n), loads):
        wait_all(load)
        p, g = flat(p_buf[ms]), flat(g_buf[ms])
        p_re, p_im = p[:, :tokens], p[:, tokens:]
        re, im = g[:, :tokens], g[:, tokens:]
        both = jnp.concatenate([re * p_re + im * p_im, im * p_re - re * p_im], axis=1)
        y_ref[ms] = times_table(both, inv_ref).reshape(ms.size, channels, 2 * tokens)

    def write(n1, r, value):
        out_buf[r, n1 * tokens : (n1 + 1) * tokens] = value * scale

    rows = parts_of(channels, ROWS)
    stores = copies_of([(out_buf.at[part], out_ref.at[part]) for part in rows], sem.at[PARTS])
    for part, store in zip(rows, stores):
        outer_inverse(write, n, part, tokens, tw_ref, y_ref)
        store.start()
    wait_all(stores)


def product_split_kernel(planes, n, a_ref, b_ref, *refs):
    keep_ref, *send_refs = refs[:planes]
    a_buf, b_buf, keep_buf, sem, keep_sem = refs[planes:]
    width = n // planes
    z = plane(width)
    loads = []
    for d in range(planes):
        part = pl.ds((z ^ d) * width, width)
        loads.append(
            copies_of([(a_ref.at[part], a_buf.at[d]), (b_ref.at[part], b_buf.at[d])], sem.at[d])
        )
        start_all(loads[d])
    keep = pltpu.make_async_copy(keep_buf, keep_ref, keep_sem)
    for d, ref in enumerate((keep_buf, *send_refs)):
        wait_all(loads[d])
        ref[...] = a_buf[d] * b_buf[d]
        if d == 0:
            keep.start()
    keep.wait()


def product_kernel(planes, n, a_ref, b_ref, after_ref, out_ref, a_buf, b_buf, buf_ref, sem):
    width = n // planes
    parts = [pl.ds(z * width, width) for z in range(planes)]
    loads = [
        copies_of([(a_ref.at[part], a_buf.at[part]), (b_ref.at[part], b_buf.at[part])], sem.at[z])
        for z, part in enumerate(parts)
    ]
    for load in loads:
        start_all(load)
    stores = copies_of([(buf_ref.at[z], out_ref.at[:, z]) for z in range(planes)], sem.at[planes])
    for z, part in enumerate(parts):
        wait_all(loads[z])
        buf_ref[z] = a_buf[part] * b_buf[part]
        stores[z].start()
    wait_all(stores)


def send_kernel(planes, width, x_ref, *refs):
    out_refs, sem = refs[:planes], refs[planes]
    z = plane(width)
    stores = copies_of([(x_ref.at[:, z ^ d], ref) for d, ref in enumerate(out_refs)], sem)
    start_all(stores)
    wait_all(stores)


def merge_kernel(planes, width, *refs):
    in_refs, (after_ref, out_ref, sem) = refs[:planes], refs[planes:]
    stores = copies_of([(ref, out_ref.at[:, d]) for d, ref in enumerate(in_refs)], sem)
    start_all(stores)
    wait_all(stores)


def gate_kernel(planes, width, x_ref, a_ref, b_ref, after_ref, oa_ref, ob_ref, a_buf, b_buf, sem):
    z = plane(width)
    stores = []
    for d in range(planes):
        rows = pl.ds((z ^ d) * width, width)
        x = x_ref[:, d]
        a_buf[rows] = x * a_ref[rows]
        b_buf[rows] = x * b_ref[rows]
        stores += copies_of([(a_buf.at[rows], oa_ref.at[rows]), (b_buf.at[rows], ob_ref.at[rows])], sem.at[d])
        start_all(stores[-2:])
    wait_all(stores)


def gate_near_kernel(
    planes, width, near_ref, a_ref, b_ref, oa_ref, ob_ref, x_buf, a_buf, b_buf, sem
):
    part = pl.ds(plane(width) * width, width)
    loads = copies_of(
        [(near_ref, x_buf), (a_ref.at[part], a_buf), (b_ref.at[part], b_buf)], sem.at[0]
    )
    start_all(loads)
    wait_all(loads)
    a_buf[...] = x_buf[...] * a_buf[...]
    b_buf[...] = x_buf[...] * b_buf[...]
    stores = copies_of([(a_buf, oa_ref), (b_buf, ob_ref)], sem.at[1])
    start_all(stores)
    wait_all(stores)


def gate_far_kernel(planes, width, *refs):
    far_refs, refs = refs[: planes - 1], refs[planes - 1 :]
    a_ref, b_ref, done_a, done_b, oa_ref, ob_ref, a_buf, b_buf, sem = refs
    z = plane(width)
    rows = pl.ds(z * width, width)
    stores = copies_of([(done_a, oa_ref.at[rows]), (done_b, ob_ref.at[rows])], sem.at[0])
    start_all(stores)
    for d, far_ref in enumerate(far_refs, 1):
        rows = pl.ds((z ^ d) * width, width)
        x = far_ref[...]
        a_buf[rows] = x * a_ref[rows]
        b_buf[rows] = x * b_ref[rows]
        stores += copies_of([(a_buf.at[rows], oa_ref.at[rows]), (b_buf.at[rows], ob_ref.at[rows])], sem.at[d])
        start_all(stores[-2:])
    wait_all(stores)


SPACES = {"v": pltpu.VMEM, "u": pltpu.VMEM, "h": pltpu.HBM, "a": pl.ANY}


def kernel_call(body, ins, outs, scratch, flops=0):
    shapes = [
        jax.ShapeDtypeStruct(shape, jnp.float32) if space == "u" else SPACES[space](shape, jnp.float32)
        for space, shape in outs
    ]

    def run(*args):
        args = [
            pltpu.with_memory_space_constraint(x, pltpu.HBM) if space == "h" else x
            for space, x in zip(ins, args, strict=True)
        ]
        size = sum(math.prod(x.shape) for x in (*args, *shapes))
        return pl.pallas_call(
            body,
            in_specs=[pl.BlockSpec(memory_space=SPACES[space]) for space in ins],
            out_specs=[pl.BlockSpec(memory_space=SPACES[space]) for space, _ in outs],
            out_shape=shapes,
            scratch_shapes=scratch,
            compiler_params=pltpu.CompilerParams(vmem_limit_bytes=VMEM_BYTES),
            cost_estimate=pl.CostEstimate(flops=flops, bytes_accessed=4 * size, transcendentals=0),
        )(*args)

    return run


def tables(n, tokens):
    length = n * tokens
    m = np.arange(n)[:, None] + 0.25
    angle = 2 * np.pi * m * np.arange(tokens)[None, :] / length
    tw = np.stack([np.cos(angle), np.sin(angle)])[:, :, None, :]
    tw = np.broadcast_to(tw, (2, n, ROWS, tokens)).astype(np.float32)
    k = np.arange(tokens)
    inner = 2 * np.pi * ((k[:, None] * k[None, :]) % tokens) / tokens
    c, s = np.cos(inner), np.sin(inner)

    def pair(table):
        hi = table.astype(ml_dtypes.bfloat16)
        lo = (table - hi.astype(np.float64)).astype(ml_dtypes.bfloat16)
        return jnp.asarray(np.concatenate([hi, hi, lo]))

    fwd = pair(np.block([[c, -s], [s, c]]))
    inv = pair(np.block([[c, s], [-s, c]]) / length)
    return jnp.asarray(tw), fwd, inv


def on_device(query_input, key_input, value_input, filters, cotangent):
    n = lax.axis_size("context")
    pair_size = lax.axis_size("dp")
    _, width, tokens = query_input.shape
    channels, length = filters.shape
    scale = 1.0 / math.sqrt(pair_size * length)
    sizes = (n, channels, tokens)
    tw, fwd, inv = tables(n, tokens)
    planes = math.gcd(n, PLANES)
    width = n // planes
    blocks, spectrum = (n, channels, tokens), (n, channels, 2 * tokens)
    one, paired, lags = (width, channels, tokens), (width, planes, channels, tokens), (channels, length)
    flops = 4 * 2 * 2 * tokens * n * channels * tokens
    f32 = jnp.float32
    y = pltpu.VMEM(spectrum, f32)

    def semaphores(*shape):
        return pltpu.SemaphoreType.DMA(shape)

    def part(body, *args):
        return lambda *refs: body(*args, *refs)

    def along_z(xs):
        return [
            lax.ppermute(x, "context", [(i, i ^ (d * width)) for i in range(n)])
            for d, x in enumerate(xs, 1)
        ]

    def within_plane(x):
        members = [[z * width + q for q in range(width)] for z in range(planes)]
        return lax.all_to_all(x, "context", 0, 0, axis_index_groups=members, tiled=True)

    query, key, value, cot = (
        x.reshape(blocks) for x in (query_input, key_input, value_input, cotangent)
    )
    rows, paired_buf = pltpu.VMEM(blocks, f32), pltpu.VMEM(paired, f32)
    by_plane = pltpu.VMEM((planes, *one), f32)
    send = kernel_call(
        part(send_kernel, planes, width), "v", [("h", one)] * planes, [semaphores(planes)]
    )
    merge = kernel_call(
        part(merge_kernel, planes, width), "v" * planes + "a", [("h", paired)], [semaphores(planes)]
    )
    half_sizes = (n, channels // 2, tokens)
    half_spectrum = (n, channels // 2, 2 * tokens)
    def transform_filters(first):
        return kernel_call(
            part(filter_kernel, first, *half_sizes), "hvv", [("h", half_spectrum)],
            [
                pltpu.VMEM((channels // 2, length), f32),
                *[pltpu.VMEM(half_spectrum, f32)] * 2,
                semaphores(2, PARTS),
            ],
            flops // 2,
        )(filters, tw, fwd)[0]

    table = pltpu.VMEM(fwd.shape, fwd.dtype)
    transform_scratch = [rows, y, y, y, table, table, semaphores(4, PARTS, max(PARTS, planes))]
    always = lax.axis_index("context") < n

    def grouped(body, *args):
        shapes = jax.eval_shape(body, *args)

        def never(*args):
            return jax.tree.map(lambda x: jnp.zeros(x.shape, x.dtype), shapes)

        return lax.cond(always, body, never, *args)

    keep_p, *send_p = kernel_call(
        part(product_split_kernel, planes, n), "hh", [("h", one)] + [("v", one)] * (planes - 1),
        [by_plane, by_plane, pltpu.VMEM(one, f32), semaphores(planes, 2), pltpu.SemaphoreType.DMA],
    )(key, value)
    got_p = along_z(send_p)

    def first(cot, query, keep_p):
        (conv_grad,) = kernel_call(
            part(product_kernel, planes, n), "hha", [("h", paired)],
            [rows, rows, by_plane, semaphores(planes + 1, planes)],
        )(cot, query, keep_p)
        return send(within_plane(conv_grad)), transform_filters(0)

    (near_g, *send_g), filt_a = grouped(first, cot, query, keep_p)
    far_g = along_z(send_g)

    def second(keep_p, got_p, send_g, filt_a):
        product_ch = within_plane(*merge(keep_p, *got_p, send_g))
        filt = (filt_a, transform_filters(channels // 2))
        *outs, prod_spec = kernel_call(
            part(conv_kernel, planes, *sizes), "vvhhhh",
            [("h", one)] * planes + [("h", spectrum)], transform_scratch, 2 * flops,
        )(product_ch, tw, fwd, inv, *filt)
        return outs, prod_spec, filt

    (keep_c, *send_c), prod_spec, filt = grouped(second, keep_p, got_p, send_g[0], filt_a)
    got_c = along_z(send_c)

    def third(near_g, far_g, filt, keep_c, prod_spec):
        back_ch, grad_spec = kernel_call(
            part(back_kernel, planes, *sizes), "a" * planes + "vhhhha",
            [("h", paired), ("h", spectrum)], transform_scratch, 2 * flops,
        )(near_g, *far_g, tw, fwd, inv, *filt, keep_c)
        sends = send(within_plane(back_ch))
        (own,) = kernel_call(
            part(filter_grad_kernel, scale, *sizes), "vvhh", [("h", lags)],
            [y, y, y, pltpu.VMEM(lags, f32), semaphores(PARTS + 1, PARTS)], flops,
        )(tw, inv, prod_spec, grad_spec)
        return sends, own

    (near_b, *send_b), own = grouped(third, near_g, far_g, filt, keep_c, prod_spec)
    far_b = along_z(send_b)

    def fourth(keep_c, got_c, query, cot, near_b, value, key, own):
        if pair_size == 2:
            grad_filter = own + lax.ppermute(own, "dp", [(0, 1), (1, 0)])
        else:
            grad_filter = lax.psum(own, "dp")
        conv_tok = within_plane(*merge(keep_c, *got_c, near_b))
        begun = kernel_call(
            part(gate_near_kernel, planes, width), "ahh", [("h", one)] * 2,
            [pltpu.VMEM(one, f32)] * 3 + [semaphores(2, 3)],
        )(near_b, value, key)
        gated, grad_query = kernel_call(
            part(gate_kernel, planes, width), "vvva", [("h", blocks)] * 2,
            [rows, rows, semaphores(planes, 2)],
        )(conv_tok, query, cot, grad_filter)
        return gated, grad_query, begun, grad_filter

    gated, grad_query, begun, grad_filter = grouped(
        fourth, keep_c, got_c, query, cot, near_b, value, key, own
    )
    grad_key, grad_value = kernel_call(
        part(gate_far_kernel, planes, width), "v" * (planes + 3), [("h", blocks)] * 2,
        [rows, rows, semaphores(planes, 2)],
    )(*far_b, value, key, *begun)
    shape = query_input.shape
    return (
        gated.reshape(shape),
        grad_query.reshape(shape),
        grad_key.reshape(shape),
        grad_value.reshape(shape),
        grad_filter,
    )


def solution(mesh):
    in_specs = (
        P("dp", None, "context"),
        P("dp", None, "context"),
        P("dp", None, "context"),
        P("context", None),
        P("dp", None, "context"),
    )
    out_specs = (
        P("dp", None, "context"),
        P("dp", None, "context"),
        P("dp", None, "context"),
        P("dp", None, "context"),
        P("context", None),
    )
    return jax.shard_map(
        on_device, mesh=mesh, in_specs=in_specs, out_specs=out_specs, check_vma=False
    )
```

```python
import math

import jax
import jax.numpy as jnp
import ml_dtypes
import numpy as np
from jax import lax
from jax.experimental import pallas as pl
from jax.experimental.pallas import tpu as pltpu
from jax.sharding import PartitionSpec as P

ROWS = 8
PLANES = 4
PARTS = 4
VMEM_BYTES = 16 * 1024 * 1024


def twist(value, turn):
    re, im = value
    turn = turn % 1.0
    if turn == 0.0:
        return re, im
    if turn == 0.25:
        return im, -re
    if turn == 0.5:
        return -re, -im
    if turn == 0.75:
        return -im, re
    if turn in (0.125, 0.375, 0.625, 0.875):
        half = math.sqrt(0.5)
        a, b = (re + im) * half, (im - re) * half
        return twist((a, b), turn - 0.125)
    c, s = math.cos(2 * math.pi * turn), math.sin(2 * math.pi * turn)
    return re * c + im * s, im * c - re * s


def dft(values, sign):
    n = len(values)
    if n == 1:
        return values
    even, odd = dft(values[0::2], sign), dft(values[1::2], sign)
    out = [None] * n
    for k in range(n // 2):
        a, b = even[k], twist(odd[k], sign * k / n)
        out[k] = (a[0] + b[0], a[1] + b[1])
        out[k + n // 2] = (a[0] - b[0], a[1] - b[1])
    return out


def times_table(x, table_ref):
    hi = x.astype(jnp.bfloat16)
    lo = (x - hi.astype(jnp.float32)).astype(jnp.bfloat16)
    return jnp.dot(
        jnp.concatenate([hi, lo, hi], axis=1), table_ref[...], preferred_element_type=jnp.float32
    )


def outer_forward(read, n, part, tokens, tw_ref, y_ref):
    @pl.loop(part.start // ROWS, (part.start + part.size) // ROWS)
    def _(r):
        rows = pl.ds(pl.multiple_of(r * ROWS, ROWS), ROWS)
        values = []
        for n1 in range(n):
            x = read(n1, rows)
            turn = 2 * math.pi * n1 / (4 * n)
            if n1 == 0:
                values.append((x, jnp.zeros_like(x)))
            else:
                values.append((x * math.cos(turn), x * -math.sin(turn)))
        for m, (re, im) in enumerate(dft(values, 1)):
            c, s = tw_ref[0, m], tw_ref[1, m]
            y_ref[m, rows, :tokens] = re * c + im * s
            y_ref[m, rows, tokens:] = im * c - re * s


def outer_inverse(write, n, part, tokens, tw_ref, y_ref):
    @pl.loop(part.start // ROWS, (part.start + part.size) // ROWS)
    def _(r):
        rows = pl.ds(pl.multiple_of(r * ROWS, ROWS), ROWS)
        values = []
        for m in range(n):
            re, im = y_ref[m, rows, :tokens], y_ref[m, rows, tokens:]
            c, s = tw_ref[0, m], tw_ref[1, m]
            values.append((re * c - im * s, im * c + re * s))
        for n1, (re, im) in enumerate(dft(values, -1)):
            turn = 2 * math.pi * n1 / (4 * n)
            if n1 == 0:
                write(n1, rows, re)
            else:
                write(n1, rows, re * math.cos(turn) - im * math.sin(turn))


def flat(x):
    return x.reshape(x.shape[0] * x.shape[1], x.shape[2])


def start_all(copies):
    for copy in copies:
        copy.start()


def wait_all(copies):
    for copy in copies:
        copy.wait()


def parts_of(size, least=1):
    step = max(least, size // PARTS)
    return [pl.ds(k, step) for k in range(0, size, step)]


def plane(width):
    return lax.axis_index("context") // width


def copies_of(pairs, sem):
    return [pltpu.make_async_copy(src, dst, sem.at[i]) for i, (src, dst) in enumerate(pairs)]


def filter_kernel(
    first, n, channels, tokens, f_ref, tw_ref, fwd_ref, out_ref, f_buf, y_ref, sem
):
    rows = parts_of(channels, ROWS)
    loads = copies_of(
        [(f_ref.at[pl.ds(first + part.start, part.size)], f_buf.at[part]) for part in rows],
        sem,
    )
    start_all(loads)
    for part, load in zip(rows, loads):
        load.wait()
        outer_forward(
            lambda n1, r: f_buf[r, n1 * tokens : (n1 + 1) * tokens], n, part, tokens, tw_ref, y_ref
        )
    for ms in parts_of(n):
        out_ref[ms] = times_table(flat(y_ref[ms]), fwd_ref).reshape(ms.size, channels, 2 * tokens)


def transform(
    sign, n, channels, tokens, read, sources, targets, tw_ref, fwd_hbm, inv_hbm, spec_refs, own_ref,
    buf_ref, y_ref, fwd_ref, inv_ref, sem,
):
    half = channels // 2
    rows = [pl.ds(0, half), pl.ds(half, half)]
    loads = [copies_of(sources(part), sem.at[0, i]) for i, part in enumerate(rows)]
    for load in loads:
        start_all(load)
    table_loads = copies_of([(fwd_hbm, fwd_ref), (inv_hbm, inv_ref)], sem.at[2, 1])
    start_all(table_loads)
    for part, load in zip(rows, loads):
        wait_all(load)
        outer_forward(read, n, part, tokens, tw_ref, y_ref)
    wait_all(table_loads)
    stores = [copies_of(targets(part), sem.at[3, i]) for i, part in enumerate(rows)]

    def write(n1, r, value):
        buf_ref[n1, r] = value

    for j, part in enumerate(rows):
        for ms in (pl.ds(0, n // 2), pl.ds(n // 2, n // 2)):
            shape = (n // 2, half, 2 * tokens)
            own = times_table(flat(y_ref[ms, part]), fwd_ref)
            own_ref[ms, part] = own.reshape(shape)
            spec = flat(spec_refs[j][ms])
            re, im = own[:, :tokens], own[:, tokens:]
            s_re, s_im = spec[:, :tokens], spec[:, tokens:] * sign
            both = jnp.concatenate([re * s_re - im * s_im, re * s_im + im * s_re], axis=1)
            y_ref[ms, part] = times_table(both, inv_ref).reshape(shape)
        outer_inverse(write, n, part, tokens, tw_ref, y_ref)
        start_all(stores[j])
    for store in stores:
        wait_all(store)


def conv_kernel(planes, n, channels, tokens, x_ref, *refs):
    tables, spec_refs, refs = refs[:3], refs[3:5], refs[5:]
    out_refs, (own_ref, *scratch) = refs[:planes], refs[planes:]
    buf_ref = scratch[0]
    width = n // planes
    z = plane(width)

    def block(d, part):
        return buf_ref.at[pl.ds((z ^ d) * width, width), part]

    def read(n1, r):
        return x_ref[n1 % width, z ^ (n1 // width), r]

    def sources(part):
        return []

    def targets(part):
        return [(block(d, part), out_refs[d].at[:, part]) for d in range(planes)]

    transform(
        1.0, n, channels, tokens, read, sources, targets, *tables, spec_refs, own_ref, *scratch
    )


def back_kernel(planes, n, channels, tokens, near_ref, *refs):
    far_refs, refs = refs[: planes - 1], refs[planes - 1 :]
    tables, spec_refs, refs = refs[:3], refs[3:5], refs[5:]
    after_ref, out_ref, own_ref, *scratch = refs
    buf_ref = scratch[0]
    width = n // planes
    z = plane(width)

    def block(z, part):
        return buf_ref.at[pl.ds(z * width, width), part]

    def sources(part):
        blocks = enumerate((near_ref, *far_refs))
        return [(ref.at[:, part], block(z ^ d, part)) for d, ref in blocks]

    def read(n1, r):
        return buf_ref[n1, r]

    def targets(part):
        return [(block(z, part), out_ref.at[:, z, part]) for z in range(planes)]

    transform(
        -1.0, n, channels, tokens, read, sources, targets, *tables, spec_refs, own_ref, *scratch
    )


def filter_grad_kernel(
    scale, n, channels, tokens, tw_ref, inv_ref, p_ref, g_ref, out_ref,
    y_ref, out_buf, sem,
):
    for ms in parts_of(n):
        p, g = flat(p_ref[ms]), flat(g_ref[ms])
        p_re, p_im = p[:, :tokens], p[:, tokens:]
        re, im = g[:, :tokens], g[:, tokens:]
        both = jnp.concatenate([re * p_re + im * p_im, im * p_re - re * p_im], axis=1)
        y_ref[ms] = times_table(both, inv_ref).reshape(ms.size, channels, 2 * tokens)

    def write(n1, r, value):
        out_buf[r, n1 * tokens : (n1 + 1) * tokens] = value * scale

    rows = parts_of(channels, ROWS)
    stores = copies_of([(out_buf.at[part], out_ref.at[part]) for part in rows], sem)
    for part, store in zip(rows, stores):
        outer_inverse(write, n, part, tokens, tw_ref, y_ref)
        store.start()
    wait_all(stores)


def product_kernel(planes, n, a_ref, b_ref, c_ref, d_ref, *refs):
    keep_ref, *send_refs, last_ref = refs[: planes + 1]
    a_buf, b_buf, c_buf, d_buf, keep_buf, sem, last_sem, keep_sem = refs[planes + 1 :]
    width = n // planes
    z = plane(width)
    loads, last_loads = [], []
    for d in range(planes):
        part = pl.ds((z ^ d) * width, width)
        loads.append(
            copies_of([(a_ref.at[part], a_buf.at[d]), (b_ref.at[part], b_buf.at[d])], sem.at[d])
        )
        start_all(loads[d])
    for p in range(planes):
        part = pl.ds(p * width, width)
        pairs = [(c_ref.at[part], c_buf.at[p]), (d_ref.at[part], d_buf.at[p])]
        last_loads.append(copies_of(pairs, last_sem.at[p]))
        start_all(last_loads[p])
    stores = [pltpu.make_async_copy(keep_buf, keep_ref, keep_sem.at[planes])]
    for d, ref in enumerate((keep_buf, *send_refs)):
        wait_all(loads[d])
        ref[...] = a_buf[d] * b_buf[d]
        if d == 0:
            stores[0].start()
    for p in range(planes):
        wait_all(last_loads[p])
        c_buf[p] = c_buf[p] * d_buf[p]
        stores.append(pltpu.make_async_copy(c_buf.at[p], last_ref.at[:, p], keep_sem.at[p]))
        stores[-1].start()
    wait_all(stores)


def send_kernel(planes, width, x_ref, *refs):
    out_refs, sem = refs[:planes], refs[planes]
    z = plane(width)
    stores = copies_of([(x_ref.at[:, z ^ d], ref) for d, ref in enumerate(out_refs)], sem)
    start_all(stores)
    wait_all(stores)


def merge_kernel(planes, width, *refs):
    in_refs, (after_ref, out_ref, sem) = refs[:planes], refs[planes:]
    stores = copies_of([(ref, out_ref.at[:, d]) for d, ref in enumerate(in_refs)], sem)
    start_all(stores)
    wait_all(stores)


def gate_kernel(planes, width, x_ref, a_ref, b_ref, after_ref, oa_ref, ob_ref, a_buf, b_buf, sem):
    z = plane(width)
    stores = []
    for d in range(planes):
        rows = pl.ds((z ^ d) * width, width)
        x = x_ref[:, d]
        a_buf[rows] = x * a_ref[rows]
        b_buf[rows] = x * b_ref[rows]
        stores += copies_of([(a_buf.at[rows], oa_ref.at[rows]), (b_buf.at[rows], ob_ref.at[rows])], sem.at[d])
        start_all(stores[-2:])
    wait_all(stores)


def gate_near_kernel(planes, width, near_ref, *refs):
    in_refs, (oa_ref, ob_ref, *out_refs, x_buf, sem) = refs[:4], refs[4:]
    part = pl.ds(plane(width) * width, width)
    loads = copies_of([(near_ref, x_buf), *zip(in_refs, out_refs)], sem)
    start_all(loads)
    wait_all(loads)
    oa_ref[...] = x_buf[...] * out_refs[0][part]
    ob_ref[...] = x_buf[...] * out_refs[1][part]


def gate_far_kernel(planes, width, *refs):
    far_refs, refs = refs[: planes - 1], refs[planes - 1 :]
    a_ref, b_ref, done_a, done_b, oa_ref, ob_ref, a_buf, b_buf, sem = refs
    z = plane(width)
    rows = pl.ds(z * width, width)
    stores = copies_of([(done_a, oa_ref.at[rows]), (done_b, ob_ref.at[rows])], sem.at[0])
    start_all(stores)
    for d, far_ref in enumerate(far_refs, 1):
        rows = pl.ds((z ^ d) * width, width)
        x = far_ref[...]
        a_buf[rows] = x * a_ref[rows]
        b_buf[rows] = x * b_ref[rows]
        stores += copies_of([(a_buf.at[rows], oa_ref.at[rows]), (b_buf.at[rows], ob_ref.at[rows])], sem.at[d])
        start_all(stores[-2:])
    wait_all(stores)


SPACES = {"v": pltpu.VMEM, "u": pltpu.VMEM, "h": pltpu.HBM, "a": pl.ANY}


def kernel_call(body, ins, outs, scratch, flops=0):
    shapes = [
        jax.ShapeDtypeStruct(shape, jnp.float32) if space == "u" else SPACES[space](shape, jnp.float32)
        for space, shape in outs
    ]

    def run(*args):
        args = [
            pltpu.with_memory_space_constraint(x, pltpu.HBM) if space == "h" else x
            for space, x in zip(ins, args, strict=True)
        ]
        size = sum(math.prod(x.shape) for x in (*args, *shapes))
        return pl.pallas_call(
            body,
            in_specs=[pl.BlockSpec(memory_space=SPACES[space]) for space in ins],
            out_specs=[pl.BlockSpec(memory_space=SPACES[space]) for space, _ in outs],
            out_shape=shapes,
            scratch_shapes=scratch,
            compiler_params=pltpu.CompilerParams(vmem_limit_bytes=VMEM_BYTES),
            cost_estimate=pl.CostEstimate(flops=flops, bytes_accessed=4 * size, transcendentals=0),
        )(*args)

    return run


def tables(n, tokens):
    length = n * tokens
    m = np.arange(n)[:, None] + 0.25
    angle = 2 * np.pi * m * np.arange(tokens)[None, :] / length
    tw = np.stack([np.cos(angle), np.sin(angle)])[:, :, None, :]
    tw = np.broadcast_to(tw, (2, n, ROWS, tokens)).astype(np.float32)
    k = np.arange(tokens)
    inner = 2 * np.pi * ((k[:, None] * k[None, :]) % tokens) / tokens
    c, s = np.cos(inner), np.sin(inner)

    def pair(table):
        hi = table.astype(ml_dtypes.bfloat16)
        lo = (table - hi.astype(np.float64)).astype(ml_dtypes.bfloat16)
        return jnp.asarray(np.concatenate([hi, hi, lo]))

    fwd = pair(np.block([[c, -s], [s, c]]))
    inv = pair(np.block([[c, s], [-s, c]]) / length)
    return jnp.asarray(tw), fwd, inv


def on_device(query_input, key_input, value_input, filters, cotangent):
    n = lax.axis_size("context")
    pair_size = lax.axis_size("dp")
    _, width, tokens = query_input.shape
    channels, length = filters.shape
    scale = 1.0 / math.sqrt(pair_size * length)
    sizes = (n, channels, tokens)
    tw, fwd, inv = tables(n, tokens)
    planes = math.gcd(n, PLANES)
    width = n // planes
    blocks, spectrum = (n, channels, tokens), (n, channels, 2 * tokens)
    one, paired, lags = (width, channels, tokens), (width, planes, channels, tokens), (channels, length)
    flops = 4 * 2 * 2 * tokens * n * channels * tokens
    f32 = jnp.float32
    y = pltpu.VMEM(spectrum, f32)

    def semaphores(*shape):
        return pltpu.SemaphoreType.DMA(shape)

    def part(body, *args):
        return lambda *refs: body(*args, *refs)

    def along_z(xs):
        return [
            lax.ppermute(x, "context", [(i, i ^ (d * width)) for i in range(n)])
            for d, x in enumerate(xs, 1)
        ]

    def within_plane(x):
        members = [[z * width + q for q in range(width)] for z in range(planes)]
        return lax.all_to_all(x, "context", 0, 0, axis_index_groups=members, tiled=True)

    query, key, value, cot = (
        x.reshape(blocks) for x in (query_input, key_input, value_input, cotangent)
    )
    rows, paired_buf = pltpu.VMEM(blocks, f32), pltpu.VMEM(paired, f32)
    by_plane = pltpu.VMEM((planes, *one), f32)
    send = kernel_call(
        part(send_kernel, planes, width), "v", [("v", one)] * planes, [semaphores(planes)]
    )
    merge = kernel_call(
        part(merge_kernel, planes, width), "v" * planes + "a", [("h", paired)], [semaphores(planes)]
    )
    half_sizes = (n, channels // 2, tokens)
    half_spectrum = (n, channels // 2, 2 * tokens)
    def transform_filters(first):
        return kernel_call(
            part(filter_kernel, first, *half_sizes), "hvv", [("v", half_spectrum)],
            [
                pltpu.VMEM((channels // 2, length), f32),
                pltpu.VMEM(half_spectrum, f32),
                semaphores(PARTS),
            ],
            flops // 2,
        )(filters, tw, fwd)[0]

    table = pltpu.VMEM(fwd.shape, fwd.dtype)
    transform_scratch = [rows, y, table, table, semaphores(4, PARTS, max(PARTS, planes))]
    always = lax.axis_index("context") < n

    def grouped(body, *args):
        shapes = jax.eval_shape(body, *args)

        def never(*args):
            return jax.tree.map(lambda x: jnp.zeros(x.shape, x.dtype), shapes)

        return lax.cond(always, body, never, *args)

    keep_p, *send_p, conv_grad = kernel_call(
        part(product_kernel, planes, n), "hhhh",
        [("v", one)] * planes + [("h", paired)],
        [
            *[by_plane] * 4, pltpu.VMEM(one, f32),
            semaphores(planes, 2), semaphores(planes, 2), semaphores(planes + 1),
        ],
    )(key, value, cot, query)
    got_p = along_z(send_p)

    def first(conv_grad):
        return send(within_plane(conv_grad)), transform_filters(0)

    (near_g, *send_g), filt_a = grouped(first, conv_grad)
    far_g = along_z(send_g)

    def second(keep_p, got_p, send_g, filt_a):
        product_ch = within_plane(*merge(keep_p, *got_p, send_g))
        filt = (filt_a, transform_filters(channels // 2))
        *outs, prod_spec = kernel_call(
            part(conv_kernel, planes, *sizes), "vvhhvv",
            [("v", one)] * planes + [("v", spectrum)], transform_scratch, 2 * flops,
        )(product_ch, tw, fwd, inv, *filt)
        return outs, prod_spec, filt

    (keep_c, *send_c), prod_spec, filt = grouped(second, keep_p, got_p, send_g[0], filt_a)
    got_c = along_z(send_c)

    def third(near_g, far_g, filt, keep_c, prod_spec):
        back_ch, grad_spec = kernel_call(
            part(back_kernel, planes, *sizes), "a" * planes + "vhhvva",
            [("h", paired), ("v", spectrum)], transform_scratch, 2 * flops,
        )(near_g, *far_g, tw, fwd, inv, *filt, keep_c)
        sends = send(within_plane(back_ch))
        (own,) = kernel_call(
            part(filter_grad_kernel, scale, *sizes), "vvvv", [("h", lags)],
            [y, pltpu.VMEM(lags, f32), semaphores(PARTS)], flops,
        )(tw, inv, prod_spec, grad_spec)
        return sends, own

    (near_b, *send_b), own = grouped(third, near_g, far_g, filt, keep_c, prod_spec)
    far_b = along_z(send_b)

    def fourth(keep_c, got_c, query, cot, near_b, value, key, own):
        if pair_size == 2:
            grad_filter = own + lax.ppermute(own, "dp", [(0, 1), (1, 0)])
        else:
            grad_filter = lax.psum(own, "dp")
        conv_tok = within_plane(*merge(keep_c, *got_c, near_b))
        *begun, value, key, query, cot = kernel_call(
            part(gate_near_kernel, planes, width), "ahhhh", [("v", one)] * 2 + [("v", blocks)] * 4,
            [pltpu.VMEM(one, f32), semaphores(5)],
        )(near_b, value, key, query, cot)
        gated, grad_query = kernel_call(
            part(gate_kernel, planes, width), "vvva", [("h", blocks)] * 2,
            [rows, rows, semaphores(planes, 2)],
        )(conv_tok, query, cot, grad_filter)
        return gated, grad_query, (value, key, *begun), grad_filter

    gated, grad_query, begun, grad_filter = grouped(
        fourth, keep_c, got_c, query, cot, near_b, value, key, own
    )
    grad_key, grad_value = kernel_call(
        part(gate_far_kernel, planes, width), "v" * (planes + 3), [("h", blocks)] * 2,
        [rows, rows, semaphores(planes, 2)],
    )(*far_b, *begun)
    shape = query_input.shape
    return (
        gated.reshape(shape),
        grad_query.reshape(shape),
        grad_key.reshape(shape),
        grad_value.reshape(shape),
        grad_filter,
    )


def solution(mesh):
    in_specs = (
        P("dp", None, "context"),
        P("dp", None, "context"),
        P("dp", None, "context"),
        P("context", None),
        P("dp", None, "context"),
    )
    out_specs = (
        P("dp", None, "context"),
        P("dp", None, "context"),
        P("dp", None, "context"),
        P("dp", None, "context"),
        P("context", None),
    )
    return jax.shard_map(
        on_device, mesh=mesh, in_specs=in_specs, out_specs=out_specs, check_vma=False
    )
```

```python
import math

import jax
import jax.numpy as jnp
import ml_dtypes
import numpy as np
from jax import lax
from jax.experimental import pallas as pl
from jax.experimental.pallas import tpu as pltpu
from jax.sharding import PartitionSpec as P

ROWS = 8
PLANES = 4
PARTS = 4
VMEM_BYTES = 16 * 1024 * 1024


def twist(value, turn):
    re, im = value
    turn = turn % 1.0
    if turn == 0.0:
        return re, im
    if turn == 0.25:
        return im, -re
    if turn == 0.5:
        return -re, -im
    if turn == 0.75:
        return -im, re
    if turn in (0.125, 0.375, 0.625, 0.875):
        half = math.sqrt(0.5)
        a, b = (re + im) * half, (im - re) * half
        return twist((a, b), turn - 0.125)
    c, s = math.cos(2 * math.pi * turn), math.sin(2 * math.pi * turn)
    return re * c + im * s, im * c - re * s


def dft(values, sign):
    n = len(values)
    if n == 1:
        return values
    even, odd = dft(values[0::2], sign), dft(values[1::2], sign)
    out = [None] * n
    for k in range(n // 2):
        a, b = even[k], twist(odd[k], sign * k / n)
        out[k] = (a[0] + b[0], a[1] + b[1])
        out[k + n // 2] = (a[0] - b[0], a[1] - b[1])
    return out


def times_table(x, table_ref):
    hi = x.astype(jnp.bfloat16)
    lo = (x - hi.astype(jnp.float32)).astype(jnp.bfloat16)
    return jnp.dot(
        jnp.concatenate([hi, lo, hi], axis=1), table_ref[...], preferred_element_type=jnp.float32
    )


def outer_forward(read, n, part, tokens, tw_ref, y_ref):
    @pl.loop(part.start // ROWS, (part.start + part.size) // ROWS, unroll=min(2, part.size // ROWS))
    def _(r):
        rows = pl.ds(pl.multiple_of(r * ROWS, ROWS), ROWS)
        values = []
        for n1 in range(n):
            x = read(n1, rows)
            turn = 2 * math.pi * n1 / (4 * n)
            if n1 == 0:
                values.append((x, jnp.zeros_like(x)))
            else:
                values.append((x * math.cos(turn), x * -math.sin(turn)))
        for m, (re, im) in enumerate(dft(values, 1)):
            c, s = tw_ref[0, m], tw_ref[1, m]
            y_ref[m, rows, :tokens] = re * c + im * s
            y_ref[m, rows, tokens:] = im * c - re * s


def outer_inverse(write, n, part, tokens, tw_ref, y_ref):
    @pl.loop(part.start // ROWS, (part.start + part.size) // ROWS, unroll=min(2, part.size // ROWS))
    def _(r):
        rows = pl.ds(pl.multiple_of(r * ROWS, ROWS), ROWS)
        values = []
        for m in range(n):
            re, im = y_ref[m, rows, :tokens], y_ref[m, rows, tokens:]
            c, s = tw_ref[0, m], tw_ref[1, m]
            values.append((re * c - im * s, im * c + re * s))
        for n1, (re, im) in enumerate(dft(values, -1)):
            turn = 2 * math.pi * n1 / (4 * n)
            if n1 == 0:
                write(n1, rows, re)
            else:
                write(n1, rows, re * math.cos(turn) - im * math.sin(turn))


def flat(x):
    return x.reshape(x.shape[0] * x.shape[1], x.shape[2])


def start_all(copies):
    for copy in copies:
        copy.start()


def wait_all(copies):
    for copy in copies:
        copy.wait()


def parts_of(size, least=1):
    step = max(least, size // PARTS)
    return [pl.ds(k, step) for k in range(0, size, step)]


def plane(width):
    return lax.axis_index("context") // width


def copies_of(pairs, sem):
    return [pltpu.make_async_copy(src, dst, sem.at[i]) for i, (src, dst) in enumerate(pairs)]


def filter_kernel(
    first, n, channels, tokens, f_ref, tw_ref, fwd_ref, out_ref, f_buf, y_ref, own_ref, sem
):
    rows = parts_of(channels, ROWS)
    loads = copies_of(
        [(f_ref.at[pl.ds(first + part.start, part.size)], f_buf.at[part]) for part in rows],
        sem.at[0],
    )
    start_all(loads)
    for part, load in zip(rows, loads):
        load.wait()
        outer_forward(
            lambda n1, r: f_buf[r, n1 * tokens : (n1 + 1) * tokens], n, part, tokens, tw_ref, y_ref
        )
    stores = copies_of([(own_ref.at[ms], out_ref.at[ms]) for ms in parts_of(n)], sem.at[1])
    for ms, store in zip(parts_of(n), stores):
        own_ref[ms] = times_table(flat(y_ref[ms]), fwd_ref).reshape(ms.size, channels, 2 * tokens)
        store.start()
    wait_all(stores)


def transform(
    sign, n, channels, tokens, read, sources, targets, tw_ref, fwd_hbm, inv_hbm, spec_refs, own_ref,
    buf_ref, spec_buf, own_buf, y_ref, fwd_ref, inv_ref, sem,
):
    half = channels // 2
    rows = [pl.ds(0, half), pl.ds(half, half)]
    loads = [copies_of(sources(part), sem.at[0, i]) for i, part in enumerate(rows)]
    for load in loads:
        start_all(load)
    table_loads = copies_of([(fwd_hbm, fwd_ref), (inv_hbm, inv_ref)], sem.at[2, 1])
    start_all(table_loads)
    spec_loads = [
        copies_of(
            [
                (ref.at[ms], spec_buf.at[ms, pl.ds(j * half, half)])
                for j, ref in enumerate(spec_refs)
            ],
            sem.at[1, i],
        )
        for i, ms in enumerate(parts_of(n))
    ]
    for load in spec_loads:
        start_all(load)
    for part, load in zip(rows, loads):
        wait_all(load)
        outer_forward(read, n, part, tokens, tw_ref, y_ref)
    own_stores = copies_of([(own_buf.at[ms], own_ref.at[ms]) for ms in parts_of(n)], sem.at[2, 0])
    wait_all(table_loads)
    for ms, load, store in zip(parts_of(n), spec_loads, own_stores):
        own = times_table(flat(y_ref[ms]), fwd_ref)
        own_buf[ms] = own.reshape(ms.size, channels, 2 * tokens)
        store.start()
        wait_all(load)
        spec = flat(spec_buf[ms])
        re, im = own[:, :tokens], own[:, tokens:]
        s_re, s_im = spec[:, :tokens], spec[:, tokens:] * sign
        both = jnp.concatenate([re * s_re - im * s_im, re * s_im + im * s_re], axis=1)
        y_ref[ms] = times_table(both, inv_ref).reshape(ms.size, channels, 2 * tokens)

    def write(n1, r, value):
        buf_ref[n1, r] = value

    stores = [copies_of(targets(part), sem.at[3, i]) for i, part in enumerate(rows)]
    for part, store in zip(rows, stores):
        outer_inverse(write, n, part, tokens, tw_ref, y_ref)
        start_all(store)
    for store in (*stores, own_stores):
        wait_all(store)


def conv_kernel(planes, n, channels, tokens, x_ref, *refs):
    tables, spec_refs, refs = refs[:3], refs[3:5], refs[5:]
    out_refs, (own_ref, *scratch) = refs[:planes], refs[planes:]
    buf_ref = scratch[0]
    width = n // planes
    z = plane(width)

    def block(d, part):
        return buf_ref.at[pl.ds((z ^ d) * width, width), part]

    def read(n1, r):
        return x_ref[n1 % width, z ^ (n1 // width), r]

    def sources(part):
        return []

    def targets(part):
        return [(block(d, part), out_refs[d].at[:, part]) for d in range(planes)]

    transform(
        1.0, n, channels, tokens, read, sources, targets, *tables, spec_refs, own_ref, *scratch
    )


def back_kernel(planes, n, channels, tokens, near_ref, *refs):
    far_refs, refs = refs[: planes - 1], refs[planes - 1 :]
    tables, spec_refs, refs = refs[:3], refs[3:5], refs[5:]
    after_ref, out_ref, own_ref, *scratch = refs
    buf_ref = scratch[0]
    width = n // planes
    z = plane(width)

    def block(z, part):
        return buf_ref.at[pl.ds(z * width, width), part]

    def sources(part):
        blocks = enumerate((near_ref, *far_refs))
        return [(ref.at[:, part], block(z ^ d, part)) for d, ref in blocks]

    def read(n1, r):
        return buf_ref[n1, r]

    def targets(part):
        return [(block(z, part), out_ref.at[:, z, part]) for z in range(planes)]

    transform(
        -1.0, n, channels, tokens, read, sources, targets, *tables, spec_refs, own_ref, *scratch
    )


def filter_grad_kernel(
    scale, n, channels, tokens, tw_ref, inv_ref, p_ref, g_ref, out_ref,
    p_buf, g_buf, y_ref, out_buf, sem,
):
    loads = [
        copies_of([(p_ref.at[ms], p_buf.at[ms]), (g_ref.at[ms], g_buf.at[ms])], sem.at[i])
        for i, ms in enumerate(parts_of(n))
    ]
    for load in loads:
        start_all(load)
    for ms, load in zip(parts_of(n), loads):
        wait_all(load)
        p, g = flat(p_buf[ms]), flat(g_buf[ms])
        p_re, p_im = p[:, :tokens], p[:, tokens:]
        re, im = g[:, :tokens], g[:, tokens:]
        both = jnp.concatenate([re * p_re + im * p_im, im * p_re - re * p_im], axis=1)
        y_ref[ms] = times_table(both, inv_ref).reshape(ms.size, channels, 2 * tokens)

    def write(n1, r, value):
        out_buf[r, n1 * tokens : (n1 + 1) * tokens] = value * scale

    rows = parts_of(channels, ROWS)
    stores = copies_of([(out_buf.at[part], out_ref.at[part]) for part in rows], sem.at[PARTS])
    for part, store in zip(rows, stores):
        outer_inverse(write, n, part, tokens, tw_ref, y_ref)
        store.start()
    wait_all(stores)


def product_split_kernel(planes, n, a_ref, b_ref, *refs):
    keep_ref, *send_refs = refs[:planes]
    a_buf, b_buf, keep_buf, sem, keep_sem = refs[planes:]
    width = n // planes
    z = plane(width)
    loads = []
    for d in range(planes):
        part = pl.ds((z ^ d) * width, width)
        loads.append(
            copies_of([(a_ref.at[part], a_buf.at[d]), (b_ref.at[part], b_buf.at[d])], sem.at[d])
        )
        start_all(loads[d])
    keep = pltpu.make_async_copy(keep_buf, keep_ref, keep_sem)
    for d, ref in enumerate((keep_buf, *send_refs)):
        wait_all(loads[d])
        ref[...] = a_buf[d] * b_buf[d]
        if d == 0:
            keep.start()
    keep.wait()


def product_kernel(planes, n, a_ref, b_ref, after_ref, out_ref, a_buf, b_buf, buf_ref, sem):
    width = n // planes
    parts = [pl.ds(z * width, width) for z in range(planes)]
    loads = [
        copies_of([(a_ref.at[part], a_buf.at[part]), (b_ref.at[part], b_buf.at[part])], sem.at[z])
        for z, part in enumerate(parts)
    ]
    for load in loads:
        start_all(load)
    stores = copies_of([(buf_ref.at[z], out_ref.at[:, z]) for z in range(planes)], sem.at[planes])
    for z, part in enumerate(parts):
        wait_all(loads[z])
        buf_ref[z] = a_buf[part] * b_buf[part]
        stores[z].start()
    wait_all(stores)


def send_kernel(planes, width, x_ref, *refs):
    out_refs, sem = refs[:planes], refs[planes]
    z = plane(width)
    stores = copies_of([(x_ref.at[:, z ^ d], ref) for d, ref in enumerate(out_refs)], sem)
    start_all(stores)
    wait_all(stores)


def merge_kernel(planes, width, *refs):
    in_refs, (after_ref, out_ref, sem) = refs[:planes], refs[planes:]
    stores = copies_of([(ref, out_ref.at[:, d]) for d, ref in enumerate(in_refs)], sem)
    start_all(stores)
    wait_all(stores)


def load_rows(planes, width, refs, bufs, sem):
    z = plane(width)
    loads = []
    for d in range(planes):
        rows = pl.ds((z ^ d) * width, width)
        loads.append(copies_of([(ref.at[rows], buf.at[d]) for ref, buf in zip(refs, bufs)], sem.at[d]))
        start_all(loads[d])
    return loads


def gate_kernel(
    planes, width, x_ref, a_ref, b_ref, after_ref, oa_ref, ob_ref, a_buf, b_buf, load_sem, sem
):
    z = plane(width)
    loads = load_rows(planes, width, (a_ref, b_ref), (a_buf, b_buf), load_sem)
    stores = []
    for d in range(planes):
        rows = pl.ds((z ^ d) * width, width)
        x = x_ref[:, d]
        wait_all(loads[d])
        a_buf[d] = x * a_buf[d]
        b_buf[d] = x * b_buf[d]
        stores += copies_of([(a_buf.at[d], oa_ref.at[rows]), (b_buf.at[d], ob_ref.at[rows])], sem.at[d])
        start_all(stores[-2:])
    wait_all(stores)


def gate_near_kernel(
    planes, width, near_ref, a_ref, b_ref, oa_ref, ob_ref, x_buf, a_buf, b_buf, sem
):
    part = pl.ds(plane(width) * width, width)
    loads = copies_of(
        [(near_ref, x_buf), (a_ref.at[part], a_buf), (b_ref.at[part], b_buf)], sem.at[0]
    )
    start_all(loads)
    wait_all(loads)
    a_buf[...] = x_buf[...] * a_buf[...]
    b_buf[...] = x_buf[...] * b_buf[...]
    stores = copies_of([(a_buf, oa_ref), (b_buf, ob_ref)], sem.at[1])
    start_all(stores)
    wait_all(stores)


def gate_far_kernel(planes, width, *refs):
    far_refs, refs = refs[: planes - 1], refs[planes - 1 :]
    a_ref, b_ref, done_a, done_b, oa_ref, ob_ref, a_buf, b_buf, load_sem, sem = refs
    z = plane(width)
    loads = load_rows(planes, width, (a_ref, b_ref), (a_buf, b_buf), load_sem)
    rows = pl.ds(z * width, width)
    stores = copies_of([(done_a, oa_ref.at[rows]), (done_b, ob_ref.at[rows])], sem.at[0])
    start_all(stores)
    for d, far_ref in enumerate(far_refs, 1):
        rows = pl.ds((z ^ d) * width, width)
        x = far_ref[...]
        wait_all(loads[d])
        a_buf[d] = x * a_buf[d]
        b_buf[d] = x * b_buf[d]
        stores += copies_of([(a_buf.at[d], oa_ref.at[rows]), (b_buf.at[d], ob_ref.at[rows])], sem.at[d])
        start_all(stores[-2:])
    wait_all(loads[0])
    wait_all(stores)


SPACES = {"v": pltpu.VMEM, "u": pltpu.VMEM, "h": pltpu.HBM, "a": pl.ANY}


def kernel_call(body, ins, outs, scratch, flops=0):
    shapes = [
        jax.ShapeDtypeStruct(shape, jnp.float32) if space == "u" else SPACES[space](shape, jnp.float32)
        for space, shape in outs
    ]

    def run(*args):
        args = [
            pltpu.with_memory_space_constraint(x, pltpu.HBM) if space == "h" else x
            for space, x in zip(ins, args, strict=True)
        ]
        size = sum(math.prod(x.shape) for x in (*args, *shapes))
        return pl.pallas_call(
            body,
            in_specs=[pl.BlockSpec(memory_space=SPACES[space]) for space in ins],
            out_specs=[pl.BlockSpec(memory_space=SPACES[space]) for space, _ in outs],
            out_shape=shapes,
            scratch_shapes=scratch,
            compiler_params=pltpu.CompilerParams(vmem_limit_bytes=VMEM_BYTES),
            cost_estimate=pl.CostEstimate(flops=flops, bytes_accessed=4 * size, transcendentals=0),
        )(*args)

    return run


def tables(n, tokens):
    length = n * tokens
    m = np.arange(n)[:, None] + 0.25
    angle = 2 * np.pi * m * np.arange(tokens)[None, :] / length
    tw = np.stack([np.cos(angle), np.sin(angle)])[:, :, None, :]
    tw = np.broadcast_to(tw, (2, n, ROWS, tokens)).astype(np.float32)
    k = np.arange(tokens)
    inner = 2 * np.pi * ((k[:, None] * k[None, :]) % tokens) / tokens
    c, s = np.cos(inner), np.sin(inner)

    def pair(table):
        hi = table.astype(ml_dtypes.bfloat16)
        lo = (table - hi.astype(np.float64)).astype(ml_dtypes.bfloat16)
        return jnp.asarray(np.concatenate([hi, hi, lo]))

    fwd = pair(np.block([[c, -s], [s, c]]))
    inv = pair(np.block([[c, s], [-s, c]]) / length)
    return jnp.asarray(tw), fwd, inv


def on_device(query_input, key_input, value_input, filters, cotangent):
    n = lax.axis_size("context")
    pair_size = lax.axis_size("dp")
    _, width, tokens = query_input.shape
    channels, length = filters.shape
    scale = 1.0 / math.sqrt(pair_size * length)
    sizes = (n, channels, tokens)
    tw, fwd, inv = tables(n, tokens)
    planes = math.gcd(n, PLANES)
    width = n // planes
    blocks, spectrum = (n, channels, tokens), (n, channels, 2 * tokens)
    one, paired, lags = (width, channels, tokens), (width, planes, channels, tokens), (channels, length)
    flops = 4 * 2 * 2 * tokens * n * channels * tokens
    f32 = jnp.float32
    y = pltpu.VMEM(spectrum, f32)

    def semaphores(*shape):
        return pltpu.SemaphoreType.DMA(shape)

    def part(body, *args):
        return lambda *refs: body(*args, *refs)

    def along_z(xs):
        return [
            lax.ppermute(x, "context", [(i, i ^ (d * width)) for i in range(n)])
            for d, x in enumerate(xs, 1)
        ]

    def within_plane(x):
        members = [[z * width + q for q in range(width)] for z in range(planes)]
        return lax.all_to_all(x, "context", 0, 0, axis_index_groups=members, tiled=True)

    query, key, value, cot = (
        x.reshape(blocks) for x in (query_input, key_input, value_input, cotangent)
    )
    rows, paired_buf = pltpu.VMEM(blocks, f32), pltpu.VMEM(paired, f32)
    by_plane = pltpu.VMEM((planes, *one), f32)
    send = kernel_call(
        part(send_kernel, planes, width), "v", [("h", one)] * planes, [semaphores(planes)]
    )
    merge = kernel_call(
        part(merge_kernel, planes, width), "v" * planes + "a", [("h", paired)], [semaphores(planes)]
    )
    half_sizes = (n, channels // 2, tokens)
    half_spectrum = (n, channels // 2, 2 * tokens)
    def transform_filters(first):
        return kernel_call(
            part(filter_kernel, first, *half_sizes), "avv", [("h", half_spectrum)],
            [
                pltpu.VMEM((channels // 2, length), f32),
                *[pltpu.VMEM(half_spectrum, f32)] * 2,
                semaphores(2, PARTS),
            ],
            flops // 2,
        )(filters, tw, fwd)[0]

    table = pltpu.VMEM(fwd.shape, fwd.dtype)
    transform_scratch = [rows, y, y, y, table, table, semaphores(4, PARTS, max(PARTS, planes))]
    always = lax.axis_index("context") < n

    def grouped(body, *args):
        shapes = jax.eval_shape(body, *args)

        def never(*args):
            return jax.tree.map(lambda x: jnp.zeros(x.shape, x.dtype), shapes)

        return lax.cond(always, body, never, *args)

    keep_p, *send_p = kernel_call(
        part(product_split_kernel, planes, n), "hh", [("h", one)] + [("v", one)] * (planes - 1),
        [by_plane, by_plane, pltpu.VMEM(one, f32), semaphores(planes, 2), pltpu.SemaphoreType.DMA],
    )(key, value)
    got_p = along_z(send_p)

    def first(cot, query, keep_p):
        (conv_grad,) = kernel_call(
            part(product_kernel, planes, n), "hha", [("h", paired)],
            [rows, rows, by_plane, semaphores(planes + 1, planes)],
        )(cot, query, keep_p)
        return send(within_plane(conv_grad)), transform_filters(0)

    (near_g, *send_g), filt_a = grouped(first, cot, query, keep_p)
    far_g = along_z(send_g)

    def second(keep_p, got_p, send_g, filt_a):
        product_ch = within_plane(*merge(keep_p, *got_p, send_g))
        filt = (filt_a, transform_filters(channels // 2))
        *outs, prod_spec = kernel_call(
            part(conv_kernel, planes, *sizes), "vvaahh",
            [("h", one)] * planes + [("h", spectrum)], transform_scratch, 2 * flops,
        )(product_ch, tw, fwd, inv, *filt)
        return outs, prod_spec, filt

    (keep_c, *send_c), prod_spec, filt = grouped(second, keep_p, got_p, send_g[0], filt_a)
    got_c = along_z(send_c)

    def third(near_g, far_g, filt, keep_c, prod_spec):
        back_ch, grad_spec = kernel_call(
            part(back_kernel, planes, *sizes), "a" * planes + "vaahha",
            [("h", paired), ("h", spectrum)], transform_scratch, 2 * flops,
        )(near_g, *far_g, tw, fwd, inv, *filt, keep_c)
        sends = send(within_plane(back_ch))
        (own,) = kernel_call(
            part(filter_grad_kernel, scale, *sizes), "vvhh", [("h", lags)],
            [y, y, y, pltpu.VMEM(lags, f32), semaphores(PARTS + 1, PARTS)], flops,
        )(tw, inv, prod_spec, grad_spec)
        return sends, own

    (near_b, *send_b), own = grouped(third, near_g, far_g, filt, keep_c, prod_spec)
    far_b = along_z(send_b)

    def fourth(keep_c, got_c, query, cot, near_b, value, key, own):
        if pair_size == 2:
            grad_filter = own + lax.ppermute(own, "dp", [(0, 1), (1, 0)])
        else:
            grad_filter = lax.psum(own, "dp")
        conv_tok = within_plane(*merge(keep_c, *got_c, near_b))
        begun = kernel_call(
            part(gate_near_kernel, planes, width), "ahh", [("h", one)] * 2,
            [pltpu.VMEM(one, f32)] * 3 + [semaphores(2, 3)],
        )(near_b, value, key)
        gated, grad_query = kernel_call(
            part(gate_kernel, planes, width), "vaaa", [("h", blocks)] * 2,
            [by_plane, by_plane, semaphores(planes, 2), semaphores(planes, 2)],
        )(conv_tok, query, cot, grad_filter)
        return gated, grad_query, begun, grad_filter

    gated, grad_query, begun, grad_filter = grouped(
        fourth, keep_c, got_c, query, cot, near_b, value, key, own
    )
    grad_key, grad_value = kernel_call(
        part(gate_far_kernel, planes, width), "v" * (planes - 1) + "aavv", [("h", blocks)] * 2,
        [by_plane, by_plane, semaphores(planes, 2), semaphores(planes, 2)],
    )(*far_b, value, key, *begun)
    shape = query_input.shape
    return (
        gated.reshape(shape),
        grad_query.reshape(shape),
        grad_key.reshape(shape),
        grad_value.reshape(shape),
        grad_filter,
    )


def solution(mesh):
    in_specs = (
        P("dp", None, "context"),
        P("dp", None, "context"),
        P("dp", None, "context"),
        P("context", None),
        P("dp", None, "context"),
    )
    out_specs = (
        P("dp", None, "context"),
        P("dp", None, "context"),
        P("dp", None, "context"),
        P("dp", None, "context"),
        P("context", None),
    )
    return jax.shard_map(
        on_device, mesh=mesh, in_specs=in_specs, out_specs=out_specs, check_vma=False
    )
```

```python
import math

import jax
import jax.numpy as jnp
import ml_dtypes
import numpy as np
from jax import lax
from jax.experimental import pallas as pl
from jax.experimental.pallas import tpu as pltpu
from jax.sharding import PartitionSpec as P

ROWS = 8
PLANES = 4
PARTS = 4
VMEM_BYTES = 16 * 1024 * 1024


def twist(value, turn):
    re, im = value
    turn = turn % 1.0
    if turn == 0.0:
        return re, im
    if turn == 0.25:
        return im, -re
    if turn == 0.5:
        return -re, -im
    if turn == 0.75:
        return -im, re
    if turn in (0.125, 0.375, 0.625, 0.875):
        half = math.sqrt(0.5)
        a, b = (re + im) * half, (im - re) * half
        return twist((a, b), turn - 0.125)
    c, s = math.cos(2 * math.pi * turn), math.sin(2 * math.pi * turn)
    return re * c + im * s, im * c - re * s


def dft(values, sign):
    n = len(values)
    if n == 1:
        return values
    even, odd = dft(values[0::2], sign), dft(values[1::2], sign)
    out = [None] * n
    for k in range(n // 2):
        a, b = even[k], twist(odd[k], sign * k / n)
        out[k] = (a[0] + b[0], a[1] + b[1])
        out[k + n // 2] = (a[0] - b[0], a[1] - b[1])
    return out


def times_table(x, table_ref):
    hi = x.astype(jnp.bfloat16)
    lo = (x - hi.astype(jnp.float32)).astype(jnp.bfloat16)
    return jnp.dot(
        jnp.concatenate([hi, lo, hi], axis=1), table_ref[...], preferred_element_type=jnp.float32
    )


def outer_forward(read, n, part, tokens, tw_ref, y_ref):
    @pl.loop(part.start // ROWS, (part.start + part.size) // ROWS, unroll=min(2, part.size // ROWS))
    def _(r):
        rows = pl.ds(pl.multiple_of(r * ROWS, ROWS), ROWS)
        values = []
        for n1 in range(n):
            x = read(n1, rows)
            turn = 2 * math.pi * n1 / (4 * n)
            if n1 == 0:
                values.append((x, jnp.zeros_like(x)))
            else:
                values.append((x * math.cos(turn), x * -math.sin(turn)))
        for m, (re, im) in enumerate(dft(values, 1)):
            c, s = tw_ref[0, m], tw_ref[1, m]
            y_ref[m, rows, :tokens] = re * c + im * s
            y_ref[m, rows, tokens:] = im * c - re * s


def outer_inverse(write, n, part, tokens, tw_ref, y_ref):
    @pl.loop(part.start // ROWS, (part.start + part.size) // ROWS, unroll=min(2, part.size // ROWS))
    def _(r):
        rows = pl.ds(pl.multiple_of(r * ROWS, ROWS), ROWS)
        values = []
        for m in range(n):
            re, im = y_ref[m, rows, :tokens], y_ref[m, rows, tokens:]
            c, s = tw_ref[0, m], tw_ref[1, m]
            values.append((re * c - im * s, im * c + re * s))
        for n1, (re, im) in enumerate(dft(values, -1)):
            turn = 2 * math.pi * n1 / (4 * n)
            if n1 == 0:
                write(n1, rows, re)
            else:
                write(n1, rows, re * math.cos(turn) - im * math.sin(turn))


def flat(x):
    return x.reshape(x.shape[0] * x.shape[1], x.shape[2])


def start_all(copies):
    for copy in copies:
        copy.start()


def wait_all(copies):
    for copy in copies:
        copy.wait()


def parts_of(size, least=1):
    step = max(least, size // PARTS)
    return [pl.ds(k, step) for k in range(0, size, step)]


def plane(width):
    return lax.axis_index("context") // width


def copies_of(pairs, sem):
    return [pltpu.make_async_copy(src, dst, sem.at[i]) for i, (src, dst) in enumerate(pairs)]


def filter_kernel(
    first, n, channels, tokens, f_ref, tw_ref, fwd_ref, out_ref, f_buf, y_ref, own_ref, sem
):
    rows = parts_of(channels, ROWS)
    loads = copies_of(
        [(f_ref.at[pl.ds(first + part.start, part.size)], f_buf.at[part]) for part in rows],
        sem.at[0],
    )
    start_all(loads)
    for part, load in zip(rows, loads):
        load.wait()
        outer_forward(
            lambda n1, r: f_buf[r, n1 * tokens : (n1 + 1) * tokens], n, part, tokens, tw_ref, y_ref
        )
    stores = copies_of([(own_ref.at[ms], out_ref.at[ms]) for ms in parts_of(n)], sem.at[1])
    for ms, store in zip(parts_of(n), stores):
        own_ref[ms] = times_table(flat(y_ref[ms]), fwd_ref).reshape(ms.size, channels, 2 * tokens)
        store.start()
    wait_all(stores)


def transform(
    sign, n, channels, tokens, read, sources, targets, tw_ref, fwd_hbm, inv_hbm, spec_refs, own_ref,
    buf_ref, spec_buf, own_buf, y_ref, fwd_ref, inv_ref, sem,
):
    half = channels // 2
    groups = [pl.ds(0, n // 2), pl.ds(n // 2, n // 2)]
    rows = [pl.ds(0, half), pl.ds(half, half)]
    loads = [copies_of(sources(part), sem.at[0, i]) for i, part in enumerate(rows)]
    for load in loads:
        start_all(load)
    table_loads = copies_of([(fwd_hbm, fwd_ref), (inv_hbm, inv_ref)], sem.at[2, 1])
    start_all(table_loads)
    spec_loads = [
        copies_of(
            [
                (ref.at[ms], spec_buf.at[ms, pl.ds(j * half, half)])
                for j, ref in enumerate(spec_refs)
            ],
            sem.at[1, i],
        )
        for i, ms in enumerate(groups)
    ]
    for load in spec_loads:
        start_all(load)
    for part, load in zip(rows, loads):
        wait_all(load)
        outer_forward(read, n, part, tokens, tw_ref, y_ref)
    own_stores = copies_of([(own_buf.at[ms], own_ref.at[ms]) for ms in groups], sem.at[2, 0])
    wait_all(table_loads)
    for ms, load, store in zip(groups, spec_loads, own_stores):
        own = times_table(flat(y_ref[ms]), fwd_ref)
        own_buf[ms] = own.reshape(ms.size, channels, 2 * tokens)
        store.start()
        wait_all(load)
        spec = flat(spec_buf[ms])
        re, im = own[:, :tokens], own[:, tokens:]
        s_re, s_im = spec[:, :tokens], spec[:, tokens:] * sign
        both = jnp.concatenate([re * s_re - im * s_im, re * s_im + im * s_re], axis=1)
        y_ref[ms] = times_table(both, inv_ref).reshape(ms.size, channels, 2 * tokens)

    def write(n1, r, value):
        buf_ref[n1, r] = value

    stores = [copies_of(targets(part), sem.at[3, i]) for i, part in enumerate(rows)]
    for part, store in zip(rows, stores):
        outer_inverse(write, n, part, tokens, tw_ref, y_ref)
        start_all(store)
    for store in (*stores, own_stores):
        wait_all(store)


def conv_kernel(planes, n, channels, tokens, x_ref, *refs):
    tables, spec_refs, refs = refs[:3], refs[3:5], refs[5:]
    out_refs, (own_ref, *scratch) = refs[:planes], refs[planes:]
    buf_ref = scratch[0]
    width = n // planes
    z = plane(width)

    def block(d, part):
        return buf_ref.at[pl.ds((z ^ d) * width, width), part]

    def read(n1, r):
        return x_ref[n1 % width, z ^ (n1 // width), r]

    def sources(part):
        return []

    def targets(part):
        return [(block(d, part), out_refs[d].at[:, part]) for d in range(planes)]

    transform(
        1.0, n, channels, tokens, read, sources, targets, *tables, spec_refs, own_ref, *scratch
    )


def back_kernel(planes, n, channels, tokens, near_ref, *refs):
    far_refs, refs = refs[: planes - 1], refs[planes - 1 :]
    tables, spec_refs, refs = refs[:3], refs[3:5], refs[5:]
    after_ref, out_ref, own_ref, *scratch = refs
    buf_ref = scratch[0]
    width = n // planes
    z = plane(width)

    def block(z, part):
        return buf_ref.at[pl.ds(z * width, width), part]

    def sources(part):
        blocks = enumerate((near_ref, *far_refs))
        return [(ref.at[:, part], block(z ^ d, part)) for d, ref in blocks]

    def read(n1, r):
        return buf_ref[n1, r]

    def targets(part):
        return [(block(z, part), out_ref.at[:, z, part]) for z in range(planes)]

    transform(
        -1.0, n, channels, tokens, read, sources, targets, *tables, spec_refs, own_ref, *scratch
    )


def filter_grad_kernel(
    scale, n, channels, tokens, tw_ref, inv_ref, p_ref, g_ref, out_ref,
    p_buf, g_buf, y_ref, out_buf, sem,
):
    loads = [
        copies_of([(p_ref.at[ms], p_buf.at[ms]), (g_ref.at[ms], g_buf.at[ms])], sem.at[i])
        for i, ms in enumerate(parts_of(n))
    ]
    for load in loads:
        start_all(load)
    for ms, load in zip(parts_of(n), loads):
        wait_all(load)
        p, g = flat(p_buf[ms]), flat(g_buf[ms])
        p_re, p_im = p[:, :tokens], p[:, tokens:]
        re, im = g[:, :tokens], g[:, tokens:]
        both = jnp.concatenate([re * p_re + im * p_im, im * p_re - re * p_im], axis=1)
        y_ref[ms] = times_table(both, inv_ref).reshape(ms.size, channels, 2 * tokens)

    def write(n1, r, value):
        out_buf[r, n1 * tokens : (n1 + 1) * tokens] = value * scale

    rows = parts_of(channels, ROWS)
    stores = copies_of([(out_buf.at[part], out_ref.at[part]) for part in rows], sem.at[PARTS])
    for part, store in zip(rows, stores):
        outer_inverse(write, n, part, tokens, tw_ref, y_ref)
        store.start()
    wait_all(stores)


def product_split_kernel(planes, n, a_ref, b_ref, *refs):
    keep_ref, *send_refs = refs[:planes]
    a_buf, b_buf, keep_buf, sem, keep_sem = refs[planes:]
    width = n // planes
    z = plane(width)
    loads = []
    for d in range(planes):
        part = pl.ds((z ^ d) * width, width)
        loads.append(
            copies_of([(a_ref.at[part], a_buf.at[d]), (b_ref.at[part], b_buf.at[d])], sem.at[d])
        )
        start_all(loads[d])
    keep = pltpu.make_async_copy(keep_buf, keep_ref, keep_sem)
    for d, ref in enumerate((keep_buf, *send_refs)):
        wait_all(loads[d])
        ref[...] = a_buf[d] * b_buf[d]
        if d == 0:
            keep.start()
    keep.wait()


def product_kernel(planes, n, a_ref, b_ref, after_ref, out_ref, a_buf, b_buf, buf_ref, sem):
    width = n // planes
    parts = [pl.ds(z * width, width) for z in range(planes)]
    loads = [
        copies_of([(a_ref.at[part], a_buf.at[part]), (b_ref.at[part], b_buf.at[part])], sem.at[z])
        for z, part in enumerate(parts)
    ]
    for load in loads:
        start_all(load)
    stores = copies_of([(buf_ref.at[z], out_ref.at[:, z]) for z in range(planes)], sem.at[planes])
    for z, part in enumerate(parts):
        wait_all(loads[z])
        buf_ref[z] = a_buf[part] * b_buf[part]
        stores[z].start()
    wait_all(stores)


def send_kernel(planes, width, x_ref, *refs):
    out_refs, sem = refs[:planes], refs[planes]
    z = plane(width)
    stores = copies_of([(x_ref.at[:, z ^ d], ref) for d, ref in enumerate(out_refs)], sem)
    start_all(stores)
    wait_all(stores)


def merge_kernel(planes, width, *refs):
    in_refs, (after_ref, out_ref, sem) = refs[:planes], refs[planes:]
    stores = copies_of([(ref, out_ref.at[:, d]) for d, ref in enumerate(in_refs)], sem)
    start_all(stores)
    wait_all(stores)


def load_rows(distances, width, refs, bufs, sem):
    z = plane(width)
    loads = {}
    for d in distances:
        rows = pl.ds((z ^ d) * width, width)
        loads[d] = copies_of([(ref.at[rows], buf.at[d]) for ref, buf in zip(refs, bufs)], sem.at[d])
        start_all(loads[d])
    return loads


def gate_kernel(
    planes, width, x_ref, a_ref, b_ref, after_ref, oa_ref, ob_ref, a_buf, b_buf, load_sem, sem
):
    z = plane(width)
    loads = load_rows(range(planes), width, (a_ref, b_ref), (a_buf, b_buf), load_sem)
    stores = []
    for d in range(planes):
        rows = pl.ds((z ^ d) * width, width)
        x = x_ref[:, d]
        wait_all(loads[d])
        a_buf[d] = x * a_buf[d]
        b_buf[d] = x * b_buf[d]
        stores += copies_of([(a_buf.at[d], oa_ref.at[rows]), (b_buf.at[d], ob_ref.at[rows])], sem.at[d])
        start_all(stores[-2:])
    wait_all(stores)


def gate_near_kernel(
    planes, width, near_ref, a_ref, b_ref, oa_ref, ob_ref, x_buf, a_buf, b_buf, sem
):
    part = pl.ds(plane(width) * width, width)
    loads = copies_of(
        [(near_ref, x_buf), (a_ref.at[part], a_buf), (b_ref.at[part], b_buf)], sem.at[0]
    )
    start_all(loads)
    wait_all(loads)
    a_buf[...] = x_buf[...] * a_buf[...]
    b_buf[...] = x_buf[...] * b_buf[...]
    stores = copies_of([(a_buf, oa_ref), (b_buf, ob_ref)], sem.at[1])
    start_all(stores)
    wait_all(stores)


def gate_far_kernel(planes, width, *refs):
    far_refs, refs = refs[: planes - 1], refs[planes - 1 :]
    a_ref, b_ref, done_a, done_b, oa_ref, ob_ref, a_buf, b_buf, load_sem, sem = refs
    z = plane(width)
    loads = load_rows(range(1, planes), width, (a_ref, b_ref), (a_buf, b_buf), load_sem)
    rows = pl.ds(z * width, width)
    stores = copies_of([(done_a, oa_ref.at[rows]), (done_b, ob_ref.at[rows])], sem.at[0])
    start_all(stores)
    for d, far_ref in enumerate(far_refs, 1):
        rows = pl.ds((z ^ d) * width, width)
        x = far_ref[...]
        wait_all(loads[d])
        a_buf[d] = x * a_buf[d]
        b_buf[d] = x * b_buf[d]
        stores += copies_of([(a_buf.at[d], oa_ref.at[rows]), (b_buf.at[d], ob_ref.at[rows])], sem.at[d])
        start_all(stores[-2:])
    wait_all(stores)


SPACES = {"v": pltpu.VMEM, "u": pltpu.VMEM, "h": pltpu.HBM, "a": pl.ANY}


def kernel_call(body, ins, outs, scratch, flops=0):
    shapes = [
        jax.ShapeDtypeStruct(shape, jnp.float32) if space == "u" else SPACES[space](shape, jnp.float32)
        for space, shape in outs
    ]

    def run(*args):
        args = [
            pltpu.with_memory_space_constraint(x, pltpu.HBM) if space == "h" else x
            for space, x in zip(ins, args, strict=True)
        ]
        size = sum(math.prod(x.shape) for x in (*args, *shapes))
        return pl.pallas_call(
            body,
            in_specs=[pl.BlockSpec(memory_space=SPACES[space]) for space in ins],
            out_specs=[pl.BlockSpec(memory_space=SPACES[space]) for space, _ in outs],
            out_shape=shapes,
            scratch_shapes=scratch,
            compiler_params=pltpu.CompilerParams(vmem_limit_bytes=VMEM_BYTES),
            cost_estimate=pl.CostEstimate(flops=flops, bytes_accessed=4 * size, transcendentals=0),
        )(*args)

    return run


def tables(n, tokens):
    length = n * tokens
    m = np.arange(n)[:, None] + 0.25
    angle = 2 * np.pi * m * np.arange(tokens)[None, :] / length
    tw = np.stack([np.cos(angle), np.sin(angle)])[:, :, None, :]
    tw = np.broadcast_to(tw, (2, n, ROWS, tokens)).astype(np.float32)
    k = np.arange(tokens)
    inner = 2 * np.pi * ((k[:, None] * k[None, :]) % tokens) / tokens
    c, s = np.cos(inner), np.sin(inner)

    def pair(table):
        hi = table.astype(ml_dtypes.bfloat16)
        lo = (table - hi.astype(np.float64)).astype(ml_dtypes.bfloat16)
        return jnp.asarray(np.concatenate([hi, hi, lo]))

    fwd = pair(np.block([[c, -s], [s, c]]))
    inv = pair(np.block([[c, s], [-s, c]]) / length)
    return jnp.asarray(tw), fwd, inv


def on_device(query_input, key_input, value_input, filters, cotangent):
    n = lax.axis_size("context")
    pair_size = lax.axis_size("dp")
    _, width, tokens = query_input.shape
    channels, length = filters.shape
    scale = 1.0 / math.sqrt(pair_size * length)
    sizes = (n, channels, tokens)
    tw, fwd, inv = tables(n, tokens)
    planes = math.gcd(n, PLANES)
    width = n // planes
    blocks, spectrum = (n, channels, tokens), (n, channels, 2 * tokens)
    one, paired, lags = (width, channels, tokens), (width, planes, channels, tokens), (channels, length)
    flops = 4 * 2 * 2 * tokens * n * channels * tokens
    f32 = jnp.float32
    y = pltpu.VMEM(spectrum, f32)

    def semaphores(*shape):
        return pltpu.SemaphoreType.DMA(shape)

    def part(body, *args):
        return lambda *refs: body(*args, *refs)

    def along_z(xs):
        return [
            lax.ppermute(x, "context", [(i, i ^ (d * width)) for i in range(n)])
            for d, x in enumerate(xs, 1)
        ]

    def within_plane(x):
        members = [[z * width + q for q in range(width)] for z in range(planes)]
        return lax.all_to_all(x, "context", 0, 0, axis_index_groups=members, tiled=True)

    query, key, value, cot = (
        x.reshape(blocks) for x in (query_input, key_input, value_input, cotangent)
    )
    rows, paired_buf = pltpu.VMEM(blocks, f32), pltpu.VMEM(paired, f32)
    by_plane = pltpu.VMEM((planes, *one), f32)
    send = kernel_call(
        part(send_kernel, planes, width), "v", [("h", one)] * planes, [semaphores(planes)]
    )
    merge = kernel_call(
        part(merge_kernel, planes, width), "v" * planes + "a", [("h", paired)], [semaphores(planes)]
    )
    half_sizes = (n, channels // 2, tokens)
    half_spectrum = (n, channels // 2, 2 * tokens)
    def transform_filters(first):
        return kernel_call(
            part(filter_kernel, first, *half_sizes), "avv", [("h", half_spectrum)],
            [
                pltpu.VMEM((channels // 2, length), f32),
                *[pltpu.VMEM(half_spectrum, f32)] * 2,
                semaphores(2, PARTS),
            ],
            flops // 2,
        )(filters, tw, fwd)[0]

    table = pltpu.VMEM(fwd.shape, fwd.dtype)
    transform_scratch = [rows, y, y, y, table, table, semaphores(4, PARTS, max(PARTS, planes))]
    always = lax.axis_index("context") < n

    def grouped(body, *args):
        shapes = jax.eval_shape(body, *args)

        def never(*args):
            return jax.tree.map(lambda x: jnp.zeros(x.shape, x.dtype), shapes)

        return lax.cond(always, body, never, *args)

    keep_p, *send_p = kernel_call(
        part(product_split_kernel, planes, n), "hh", [("h", one)] + [("v", one)] * (planes - 1),
        [by_plane, by_plane, pltpu.VMEM(one, f32), semaphores(planes, 2), pltpu.SemaphoreType.DMA],
    )(key, value)
    got_p = along_z(send_p)

    def first(cot, query, keep_p):
        (conv_grad,) = kernel_call(
            part(product_kernel, planes, n), "hha", [("h", paired)],
            [rows, rows, by_plane, semaphores(planes + 1, planes)],
        )(cot, query, keep_p)
        return send(within_plane(conv_grad)), transform_filters(0)

    (near_g, *send_g), filt_a = grouped(first, cot, query, keep_p)
    far_g = along_z(send_g)

    def second(keep_p, got_p, send_g, filt_a):
        product_ch = within_plane(*merge(keep_p, *got_p, send_g))
        filt = (filt_a, transform_filters(channels // 2))
        *outs, prod_spec = kernel_call(
            part(conv_kernel, planes, *sizes), "vvaahh",
            [("h", one)] * planes + [("h", spectrum)], transform_scratch, 2 * flops,
        )(product_ch, tw, fwd, inv, *filt)
        return outs, prod_spec, filt

    (keep_c, *send_c), prod_spec, filt = grouped(second, keep_p, got_p, send_g[0], filt_a)
    got_c = along_z(send_c)

    def third(near_g, far_g, filt, keep_c, prod_spec):
        back_ch, grad_spec = kernel_call(
            part(back_kernel, planes, *sizes), "a" * planes + "vaahha",
            [("h", paired), ("h", spectrum)], transform_scratch, 2 * flops,
        )(near_g, *far_g, tw, fwd, inv, *filt, keep_c)
        sends = send(within_plane(back_ch))
        (own,) = kernel_call(
            part(filter_grad_kernel, scale, *sizes), "vvhh", [("h", lags)],
            [y, y, y, pltpu.VMEM(lags, f32), semaphores(PARTS + 1, PARTS)], flops,
        )(tw, inv, prod_spec, grad_spec)
        return sends, own

    (near_b, *send_b), own = grouped(third, near_g, far_g, filt, keep_c, prod_spec)
    far_b = along_z(send_b)

    def fourth(keep_c, got_c, query, cot, near_b, value, key, own):
        if pair_size == 2:
            grad_filter = own + lax.ppermute(own, "dp", [(0, 1), (1, 0)])
        else:
            grad_filter = lax.psum(own, "dp")
        conv_tok = within_plane(*merge(keep_c, *got_c, near_b))
        begun = kernel_call(
            part(gate_near_kernel, planes, width), "ahh", [("h", one)] * 2,
            [pltpu.VMEM(one, f32)] * 3 + [semaphores(2, 3)],
        )(near_b, value, key)
        gated, grad_query = kernel_call(
            part(gate_kernel, planes, width), "vaaa", [("h", blocks)] * 2,
            [by_plane, by_plane, semaphores(planes, 2), semaphores(planes, 2)],
        )(conv_tok, query, cot, grad_filter)
        return gated, grad_query, begun, grad_filter

    gated, grad_query, begun, grad_filter = grouped(
        fourth, keep_c, got_c, query, cot, near_b, value, key, own
    )
    grad_key, grad_value = kernel_call(
        part(gate_far_kernel, planes, width), "v" * (planes - 1) + "aavv", [("h", blocks)] * 2,
        [by_plane, by_plane, semaphores(planes, 2), semaphores(planes, 2)],
    )(*far_b, value, key, *begun)
    shape = query_input.shape
    return (
        gated.reshape(shape),
        grad_query.reshape(shape),
        grad_key.reshape(shape),
        grad_value.reshape(shape),
        grad_filter,
    )


def solution(mesh):
    in_specs = (
        P("dp", None, "context"),
        P("dp", None, "context"),
        P("dp", None, "context"),
        P("context", None),
        P("dp", None, "context"),
    )
    out_specs = (
        P("dp", None, "context"),
        P("dp", None, "context"),
        P("dp", None, "context"),
        P("dp", None, "context"),
        P("context", None),
    )
    return jax.shard_map(
        on_device, mesh=mesh, in_specs=in_specs, out_specs=out_specs, check_vma=False
    )
```
